256 devices in a mesh: seq: 64 (over z, x_hi, y), head: 4 (over x_lo, core).
Axes of the slice: x: 4 (x_hi: 2, x_lo: 2; x = x_hi * 2 + x_lo), y: 4, z: 8, core: 2. Of those that a mesh axis runs over, the one named last changes fastest.
Arguments:
- queries: bfloat16 [1, 32768, 1024], P(None, 'seq', 'head'), may hold values from -40 to 40
- key_vectors: bfloat16 [1, 32768, 1024], P(None, 'seq', 'head'), may hold values from -40 to 40
- value_vectors: bfloat16 [1, 32768, 1024], P(None, 'seq', 'head'), may hold values from -6 to 6
- out_weight: bfloat16 [1024, 1024], replicated, may hold values from -0.1875 to 0.1875
Outputs:
- layer_output: bfloat16 [1, 32768, 1024], P(None, ('seq', 'head'))
The draws below stay inside these ranges and needn't reach their ends.
All inputs are finite; a program needn't handle non-finite values.
Results may differ from the reference program's by a relative error of at most 0.038.
Values may be sent and summed in bfloat16 or wider, within the bound.
A program may use at most 192 MiB of HBM per device.

```python
import jax
import jax.numpy as jnp
from jax import lax

HEADS = 16
HD = 64
WIDTH = 1024
BLOCK = 128
LEVELS = 4
BATCH = 1
LENGTH = 32768


def draw_queries(key, part):
    key = jax.random.fold_in(key, 11)
    base = 1.4 * jax.random.truncated_normal(key, -6.0, 6.0, (BATCH, LENGTH, WIDTH), jnp.float32)
    return base.astype(jnp.bfloat16)


def draw_key_vectors(key, part):
    key = jax.random.fold_in(key, 12)
    base = 1.4 * jax.random.truncated_normal(key, -6.0, 6.0, (BATCH, LENGTH, WIDTH), jnp.float32)
    return base.astype(jnp.bfloat16)


def block_scale(rng, shape, cuts, low, high):
    def one(axis_at, parts):
        steps = jax.random.uniform(jax.random.fold_in(jax.random.fold_in(rng, 6), axis_at), (parts,), jnp.float32, low / len(cuts), high / len(cuts))
        return jnp.repeat(jnp.exp(steps), shape[axis_at] // parts).reshape((-1,) + (1,) * (len(shape) - axis_at - 1))

    gain = one(*cuts[0])
    for cut in cuts[1:]:
        gain = gain * one(*cut)
    return gain


def scatter_about(own_key, extent, width, most, pieces=(), held_as=jnp.bfloat16):
    gain = block_scale(own_key, extent, pieces, -0.22, 0.18) if pieces else 1.0
    entries = jax.random.normal(own_key, extent, jnp.float32) * width * gain
    return jnp.minimum(jnp.maximum(entries, -most), most).astype(held_as)


def setup_inputs(seed: int = 0) -> dict:
    key_of = jax.random.split(jax.random.key(seed), 5)
    queries = draw_queries(jax.random.fold_in(key_of[4], 71), 0)
    key_vectors = draw_key_vectors(jax.random.fold_in(key_of[4], 71), 0)
    value_vectors = scatter_about(key_of[2], (BATCH, LENGTH, WIDTH), 1.0, 6.0, ((1, 64), (2, 4)))
    out_weight = scatter_about(key_of[3], (WIDTH, WIDTH), WIDTH ** -0.5, 0.1875)
    return dict(queries=queries, key_vectors=key_vectors, value_vectors=value_vectors, out_weight=out_weight)


neg_fill = -1.0e30
root_half = 0.7071067811865476


def pooled(field):
    return ((field[0::2].astype(jnp.float32) + field[1::2].astype(jnp.float32)) * root_half).astype(jnp.bfloat16)


def attend(query_blocks, key_blocks, value_blocks, allowed):
    scaling = HD ** -0.5
    scores = jnp.einsum("nqd,nkd->nqk", query_blocks.astype(jnp.float32), key_blocks.astype(jnp.float32)) * scaling
    scores = jnp.where(allowed, scores, neg_fill)
    row_max = jnp.max(scores, axis=-1)
    chances = jnp.exp(scores - row_max[..., None]).astype(jnp.bfloat16)
    row_sum = jnp.sum(chances.astype(jnp.float32), axis=-1)
    numerator = jnp.einsum("nqk,nkd->nqd", chances.astype(jnp.float32), value_blocks.astype(jnp.float32))
    return row_max.reshape(-1), numerator.reshape(-1, HD), row_sum.reshape(-1)


def merged(terms, length):
    expanded = [jnp.repeat(record[1], 2 ** record[0], axis=0) for record in terms]
    top_max = expanded[0]
    for other_max in expanded[1:]:
        top_max = jnp.maximum(top_max, other_max)
    numerator = jnp.zeros((length, HD), jnp.float32)
    denominator = jnp.zeros((length,), jnp.float32)
    for record, fine_max in zip(terms, expanded):
        factor = jnp.exp(fine_max - top_max)
        numerator = numerator + jnp.repeat(record[2], 2 ** record[0], axis=0) * factor[:, None]
        denominator = denominator + jnp.repeat(record[3], 2 ** record[0], axis=0) * factor
    return (numerator / denominator[:, None]).astype(jnp.bfloat16)


def one_head(triple):
    query_rows, key_rows, value_rows = triple
    length = query_rows.shape[0]
    blocks = length // BLOCK

    def windowed(field):
        padded = jnp.pad(field, ((BLOCK, BLOCK), (0, 0)))
        return jnp.concatenate([padded[:length].reshape(blocks, BLOCK, HD), padded[BLOCK:length + BLOCK].reshape(blocks, BLOCK, HD), padded[2 * BLOCK:].reshape(blocks, BLOCK, HD)], axis=1)

    block_ids = jnp.arange(blocks)
    left_ok = jnp.broadcast_to((block_ids > 0)[:, None], (blocks, BLOCK))
    right_ok = jnp.broadcast_to((block_ids < blocks - 1)[:, None], (blocks, BLOCK))
    allowed = jnp.concatenate([left_ok, jnp.ones((blocks, BLOCK), jnp.bool_), right_ok], axis=1)[:, None, :]
    terms = [(0,) + attend(query_rows.reshape(blocks, BLOCK, HD), windowed(key_rows), windowed(value_rows), allowed)]
    level_q, level_k, level_v = query_rows, key_rows, value_rows
    for ladder in range(1, LEVELS + 1):
        level_q, level_k, level_v = pooled(level_q), pooled(level_k), pooled(level_v)
        count_now = level_q.shape[0] // BLOCK
        partner_k = level_k.reshape(count_now // 2, 2, BLOCK, HD)[:, ::-1].reshape(count_now, BLOCK, HD)
        partner_v = level_v.reshape(count_now // 2, 2, BLOCK, HD)[:, ::-1].reshape(count_now, BLOCK, HD)
        terms.append((ladder,) + attend(level_q.reshape(count_now, BLOCK, HD), partner_k, partner_v, True))
    terms.append((LEVELS,) + attend(level_q[None], level_k[None], level_v[None], True))
    return merged(terms, length)


def reference(queries, key_vectors, value_vectors, out_weight):
    samples, length, features = queries.shape

    def split_heads(field):
        return jnp.transpose(field.reshape(samples, length, HEADS, HD), (0, 2, 1, 3)).reshape(samples * HEADS, length, HD)

    attended = lax.map(one_head, (split_heads(queries), split_heads(key_vectors), split_heads(value_vectors)))
    attended = jnp.transpose(attended.reshape(samples, HEADS, length, HD), (0, 2, 1, 3)).reshape(samples * length, features)
    projected = jnp.dot(attended, out_weight, preferred_element_type=jnp.float32).astype(jnp.bfloat16)
    return projected.reshape(samples, length, features)
```

```python
import math

import jax
import jax.numpy as jnp
from jax import lax
from jax.experimental import pallas as pl
from jax.experimental.pallas import tpu as pltpu
from jax.sharding import PartitionSpec as P

HD = 64
BLOCK = 128
HEADS_HERE = 4
ROWS = 512
FEATURES = HEADS_HERE * HD
SLAB = HD + 16
SCALE = HD**-0.5 * math.log2(math.e)
MASKED = -1e30
BF16, F32 = jnp.bfloat16, jnp.float32
MESH = pl.DeviceIdType.MESH


def iota(shape, axis):
    return lax.broadcasted_iota(jnp.int32, shape, axis)


def dot(a, b):
    return jnp.dot(a, b, preferred_element_type=F32)


def dot_nt(a, b):
    return lax.dot_general(a, b, (((1,), (1,)), ((), ())), preferred_element_type=F32)


def rounded(value):
    return value.astype(BF16).astype(F32)


def split_top(top):
    high = rounded(top)
    return high, rounded(top - high)


def selector(rows, columns, shift, offset=0):
    hit = iota((rows, columns), 0) == offset + (iota((rows, columns), 1) >> shift)
    return jnp.where(hit, 1.0, 0.0).astype(BF16)


def pooler(level):
    rows = ROWS >> level
    hit = iota((rows, ROWS), 0) == (iota((rows, ROWS), 1) >> level)
    return jnp.where(hit, 1.0, 0.0).astype(BF16)


def kernel(
    q_hbm, k_hbm, v_hbm, w_hbm, o_ref,
    q_s, kx, vx, w_s,
    qn, q1m, q2m, q3m,
    k1, v1, kv2_s, kv2_r, kv3_s, kv3_r,
    vtn, vt1, vt2, vt3,
    s1, r1, kv_all, q_far, st, p_s, lhs_s, ret_s, ret_r,
    x1, x2, x3, x4, e1, e2, e3, e4,
    near, near_top, att_s, att_r,
    in_sem, halo_send, halo_recv, s1_send, s1_recv, l2_send, l2_recv, l3_send, l3_recv,
    kv_send, kv_recv, q_send, q_recv, own_send, own_recv, far_send, far_recv, a2a_send, a2a_recv,
):
    s, g = lax.axis_index("seq"), lax.axis_index("head")
    last = lax.axis_size("seq") - 1
    z, x, y = lax.div(s, 8), lax.rem(lax.div(s, 4), 2), lax.rem(s, 4)
    ring = s - y
    half = lax.div(z, 4) * 32
    place = lax.rem(z, 4) * 2 + x
    mirror = (7 - z) * 8 + x * 4

    def ring_peer(d):
        return ring + lax.rem(y + d, 4)

    def half_peer(d):
        n = lax.rem(place + d, 8)
        return half + n * 4 + y

    barrier = pltpu.get_barrier_semaphore()

    def greet(seq, head):
        pl.semaphore_signal(barrier, inc=1, device_id=(seq, head), device_id_type=MESH)

    for d in range(1, 4):
        greet(ring_peer(d), g)
    for d in range(1, 8):
        greet(half_peer(d), g)
    for j in range(4):
        greet(mirror + j, g)
    for d in range(1, 4):
        greet(s, lax.rem(g + d, 4))

    @pl.when(s > 0)
    def _():
        greet(s - 1, g)

    @pl.when(s < last)
    def _():
        greet(s + 1, g)

    loads = [
        pltpu.make_async_copy(k_hbm.at[0], kx.at[pl.ds(BLOCK, ROWS)], in_sem.at[0]),
        pltpu.make_async_copy(v_hbm.at[0], vx.at[pl.ds(BLOCK, ROWS)], in_sem.at[1]),
        pltpu.make_async_copy(q_hbm.at[0], q_s, in_sem.at[2]),
        pltpu.make_async_copy(w_hbm, w_s, in_sem.at[3]),
    ]
    for load in loads:
        load.start()

    lane = iota((32, 128), 1)
    low = lane < HD

    for load in loads[:3]:
        load.wait()
    own_k, own_v = kx.at[pl.ds(BLOCK, ROWS)], vx.at[pl.ds(BLOCK, ROWS)]
    pool4 = pooler(4)
    k4 = rounded(dot(pool4, own_k[...]) * 0.25)
    v4 = rounded(dot(pool4, own_v[...]) * 0.25)
    q4 = rounded(dot(pool4, q_s[...]) * 0.25)
    for h in range(HEADS_HERE):
        pair = slice(h // 2 * 128, h // 2 * 128 + 128)
        kp, vp, qp = k4[:, pair], v4[:, pair], q4[:, pair]
        if h % 2 == 0:
            packed = jnp.where(low, kp, pltpu.roll(vp, HD, 1))
        else:
            packed = jnp.where(low, pltpu.roll(kp, HD, 1), vp)
            qp = pltpu.roll(qp, HD, 1)
        s1[h, 0] = packed.astype(BF16)
        s1[h, 1] = jnp.where(low, qp, 0.0).astype(BF16)

    pl.semaphore_wait(
        barrier, 17 + jnp.where(s > 0, 1, 0) + jnp.where(s < last, 1, 0)
    )

    def remote(src, dst, send, recv, seq, head=None):
        return pltpu.make_async_remote_copy(
            src_ref=src, dst_ref=dst, send_sem=send, recv_sem=recv,
            device_id=(seq, g if head is None else head), device_id_type=MESH,
        )

    my_rows = pl.ds(pl.multiple_of(y * 32, 32), 32)
    ring_copies = [
        remote(
            s1.at[lax.rem(y + d, 4)], r1.at[:, my_rows, :],
            s1_send.at[d - 1], s1_recv.at[d - 1], ring_peer(d),
        )
        for d in range(1, 4)
    ]
    for copy in ring_copies:
        copy.start()
    r1[:, my_rows, :] = s1[y]

    def pool_pair(level, scale):
        pool = pooler(level)
        return dot(pool, own_k[...]) * scale, dot(pool, own_v[...]) * scale

    kp, vp = pool_pair(3, 0.5**1.5)
    kv3_s[0], kv3_s[1] = kp.astype(BF16), vp.astype(BF16)
    slot3 = pl.ds(pl.multiple_of(lax.rem(y, 2) * 64, 64), 64)
    pair3 = ring + (1 - lax.div(y, 2)) * 2
    l3_copies = [
        remote(kv3_s, kv3_r.at[:, slot3, :], l3_send.at[j], l3_recv.at[lax.rem(y, 2)], pair3 + j)
        for j in range(2)
    ]
    for copy in l3_copies:
        copy.start()
    kp, vp = pool_pair(2, 0.5)
    kv2_s[0], kv2_s[1] = kp.astype(BF16), vp.astype(BF16)
    l2_copy = remote(
        kv2_s, kv2_r, l2_send, l2_recv, s + 1 - 2 * lax.rem(y, 2)
    )
    l2_copy.start()

    head_rows, tail_rows = pl.ds(0, BLOCK), pl.ds(ROWS - BLOCK, BLOCK)
    to_left = [
        remote(k_hbm.at[0, head_rows], kx.at[pl.ds(BLOCK + ROWS, BLOCK)], halo_send.at[0], halo_recv.at[0], s - 1),
        remote(v_hbm.at[0, head_rows], vx.at[pl.ds(BLOCK + ROWS, BLOCK)], halo_send.at[1], halo_recv.at[1], s - 1),
    ]
    to_right = [
        remote(k_hbm.at[0, tail_rows], kx.at[pl.ds(0, BLOCK)], halo_send.at[2], halo_recv.at[2], s + 1),
        remote(v_hbm.at[0, tail_rows], vx.at[pl.ds(0, BLOCK)], halo_send.at[3], halo_recv.at[3], s + 1),
    ]

    @pl.when(s > 0)
    def _():
        for copy in to_left:
            copy.start()

    @pl.when(s < last)
    def _():
        for copy in to_right:
            copy.start()

    zeros = jnp.zeros((BLOCK, FEATURES), BF16)

    @pl.when(s == 0)
    def _():
        kx[0:BLOCK] = zeros
        vx[0:BLOCK] = zeros

    @pl.when(s == last)
    def _():
        kx[BLOCK + ROWS :] = zeros
        vx[BLOCK + ROWS :] = zeros

    for copy in ring_copies:
        copy.wait_recv()
    kv_all[place] = r1[0]
    half_copies = [
        remote(r1.at[0], kv_all.at[place], kv_send.at[d - 1], kv_recv.at[d - 1], half_peer(d))
        for d in range(1, 8)
    ]
    far_q = remote(r1.at[1], q_far, q_send, q_recv, mirror + y)
    far_q.start()
    for copy in half_copies:
        copy.start()

    lane_half = iota((1, 128), 1) < HD
    halves = [jnp.where(lane_half, 1.0, 0.0), jnp.where(lane_half, 0.0, 1.0)]

    def masked_queries(dst, field, count):
        for p in range(2):
            part = field[:, p * 128 : p * 128 + 128]
            for odd in range(2):
                dst[p, odd * count : (odd + 1) * count, :] = (part * halves[odd]).astype(BF16)

    for b in range(4):
        masked_queries(qn.at[b], q_s[b * BLOCK : (b + 1) * BLOCK, :].astype(F32), BLOCK)
    pooled_q = dot(pooler(1), q_s[...]) * 0.5**0.5
    for b in range(2):
        masked_queries(q1m.at[b], pooled_q[b * BLOCK : (b + 1) * BLOCK, :], BLOCK)
    masked_queries(q2m, dot(pooler(2), q_s[...]) * 0.5, BLOCK)
    masked_queries(q3m, dot(pooler(3), q_s[...]) * 0.5**1.5, 64)
    kp, vp = pool_pair(1, 0.5**0.5)
    k1[...] = kp.astype(BF16)
    v1[...] = vp.astype(BF16)

    ones16 = jnp.ones((16, BLOCK), BF16)

    def turn(dst, block, column):
        turned = block.T
        for h in range(HEADS_HERE):
            dst[h, 0:HD, column : column + BLOCK] = turned[h * HD : (h + 1) * HD, :]
            dst[h, HD:SLAB, column : column + BLOCK] = ones16

    for b in range(1, 5):
        turn(vtn, vx[b * BLOCK : (b + 1) * BLOCK, :], b * BLOCK)
    for b in range(2):
        turn(vt1, v1[b * BLOCK : (b + 1) * BLOCK, :], b * BLOCK)

    def attend(keys, queries, values, count, exact, biases=None):
        scores = [dot_nt(key, queries) for key in keys]
        if biases:
            scores = [a if bias is None else a + bias for a, bias in zip(scores, biases)]
        top = jnp.max(scores[0], axis=0, keepdims=True)
        for part in scores[1:]:
            top = jnp.maximum(top, jnp.max(part, axis=0, keepdims=True))
        top = top * SCALE
        high = below = None
        if not exact:
            high, below = split_top(top)
            top = high + below
        weights = [jnp.exp2(part * SCALE - top).astype(BF16) for part in scores]
        weights = weights[0] if len(weights) == 1 else jnp.concatenate(weights, axis=0)
        results = [
            dot(values[odd], weights[:, odd * count : (odd + 1) * count]) for odd in range(2)
        ]
        return top, high, below, results

    def near_block(b):
        for p in range(2):
            lanes = slice(p * 128, p * 128 + 128)
            keys = [kx[(b + i) * BLOCK : (b + i + 1) * BLOCK, lanes] for i in range(3)]
            values = [vtn[2 * p + odd, :, b * BLOCK : (b + 3) * BLOCK] for odd in range(2)]
            biases = [None, None, None]
            if b == 0:
                biases[0] = jnp.where(s == 0, MASKED, 0.0)
            if b == 3:
                biases[2] = jnp.where(s == last, MASKED, 0.0)
            top, _, _, results = attend(keys, qn[b, p], values, BLOCK, True, biases)
            columns = slice(b * BLOCK, (b + 1) * BLOCK)
            for odd in range(2):
                h = 2 * p + odd
                near[h, :, columns] = results[odd]
                near_top[h : h + 1, columns] = top[:, odd * BLOCK : (odd + 1) * BLOCK]

    def small_rows(count, high, below, total):
        row = iota((16, count), 0)
        total_high = rounded(total)
        rows = jnp.where(row == 2, total_high, total - total_high)
        rows = jnp.where(row == 1, below, rows)
        return jnp.where(row == 0, high, rows)

    def sibling(dst, keys, queries, values, count, column):
        for p in range(2):
            lanes = slice(p * 128, p * 128 + 128)
            _, high, below, results = attend(
                [keys[:, lanes]], queries[p], [values(2 * p), values(2 * p + 1)], count, False
            )
            for odd in range(2):
                h = 2 * p + odd
                own = slice(odd * count, (odd + 1) * count)
                columns = slice(column, column + count)
                dst[h * SLAB : h * SLAB + HD, columns] = results[odd][0:HD].astype(BF16)
                dst[h * SLAB + HD : (h + 1) * SLAB, columns] = small_rows(
                    count, high[:, own], below[:, own], results[odd][HD : HD + 1]
                ).astype(BF16)

    near_block(1)
    near_block(2)

    far_q.wait_recv()
    for copy in half_copies:
        copy.wait_recv()
    queries = jnp.concatenate([r1[1], q_far[...]], axis=0)
    full_low = iota((128, 128), 1) < HD
    top = None
    for j in range(8):
        block = kv_all[j]
        part = dot_nt(block, queries)
        st[j] = part
        part_top = jnp.max(part, axis=0, keepdims=True)
        top = part_top if top is None else jnp.maximum(top, part_top)
        turned = jnp.where(full_low, 1.0, block.astype(F32)).T
        lhs_s[:, j * 128 : (j + 1) * 128] = turned.astype(BF16)
    high, below = split_top(top * SCALE)
    top = high + below
    partner = place + 1 - 2 * x
    for j in range(8):
        weights = jnp.exp2(st[j] * SCALE - top)
        times = jnp.where(partner == j, 2.0, 1.0)
        p_s[j * 128 : (j + 1) * 128, 0:128] = (weights[:, 0:128] * times).astype(BF16)
        p_s[j * 128 : (j + 1) * 128, 128:256] = weights[:, 128:256].astype(BF16)
    result = dot(lhs_s[...], p_s[...])
    row = iota((128, 128), 0)
    for group in range(2):
        own = slice(group * 128, group * 128 + 128)
        part = result[:, own]
        total = part[4:5, :]
        total_high = rounded(total)
        part = jnp.where(row == 3, total - total_high, part)
        part = jnp.where(row == 2, total_high, part)
        part = jnp.where(row == 1, below[:, own], part)
        part = jnp.where(row == 0, high[:, own], part)
        ret_s[group] = part.T.astype(BF16)
    ret_copies = []
    for d in range(1, 4):
        there = pl.ds(pl.multiple_of(lax.rem(y + d, 4) * 32, 32), 32)
        ret_copies.append(
            remote(
                ret_s.at[0, there, :], ret_r.at[0, my_rows, :],
                own_send.at[d - 1], own_recv.at[d - 1], ring_peer(d),
            )
        )
    for j in range(4):
        ret_copies.append(
            remote(
                ret_s.at[1, pl.ds(j * 32, 32), :], ret_r.at[1, my_rows, :],
                far_send.at[j], far_recv.at[y], mirror + j,
            )
        )
    for copy in ret_copies:
        copy.start()
    ret_r[0, my_rows, :] = ret_s[0, my_rows, :]

    for b in range(2):
        other = 1 - b
        sibling(
            x1, k1[other * BLOCK : (other + 1) * BLOCK, :], q1m.at[b],
            lambda h, other=other: vt1[h, :, other * BLOCK : (other + 1) * BLOCK], BLOCK, b * BLOCK,
        )

    e1[...] = selector(256, ROWS, 1)
    e2[...] = selector(128, ROWS, 2)
    e3[...] = selector(64, ROWS, 3)
    for h in range(HEADS_HERE):
        e4[h] = selector(128, ROWS, 4, h * 32)

    for j in range(2):
        remote(kv3_s, kv3_r.at[:, pl.ds(j * 64, 64), :], l3_send.at[j], l3_recv.at[j], pair3 + j).wait_recv()
    turn(vt3, kv3_r[1], 0)
    sibling(x3, kv3_r[0], q3m, lambda h: vt3[h], 64, 0)
    l2_copy.wait_recv()
    turn(vt2, kv2_r[1], 0)
    sibling(x2, kv2_r[0], q2m, lambda h: vt2[h], BLOCK, 0)

    @pl.when(s > 0)
    def _():
        for copy in to_right:
            copy.wait_recv()

    turn(vtn, vx[0:BLOCK, :], 0)
    near_block(0)

    @pl.when(s < last)
    def _():
        for copy in to_left:
            copy.wait_recv()

    turn(vtn, vx[BLOCK + ROWS :, :], BLOCK + ROWS)
    near_block(3)

    for copy in ret_copies[:3]:
        copy.wait_recv()
    for j in range(4):
        remote(
            ret_s.at[1, pl.ds(j * 32, 32), :], ret_r.at[1, pl.ds(j * 32, 32), :],
            far_send.at[j], far_recv.at[j], mirror + j,
        ).wait_recv()
    parts = [ret_r[i].astype(F32).T for i in range(2)]
    tops = [part[0:1] + part[1:2] for part in parts]
    sums = [part[2:3] + part[3:4] for part in parts]
    top = jnp.maximum(tops[0], tops[1])
    factors = [jnp.exp2(t - top) for t in tops]
    high, below = split_top(top)
    x4[0:HD] = (parts[0][HD:] * factors[0] + parts[1][HD:] * factors[1]).astype(BF16)
    x4[HD:SLAB] = small_rows(
        128, high, below, sums[0] * factors[0] + sums[1] * factors[1]
    ).astype(BF16)

    a2a = []
    for d in (1, 2, 3, 0):
        target = lax.rem(g + d, 4)
        columns = pl.ds(pl.multiple_of(target * BLOCK, BLOCK), BLOCK)
        wide = [
            dot(field[...], select[:, columns])
            for field, select in ((x1, e1), (x2, e2), (x3, e3))
        ]
        for h in range(HEADS_HERE):
            terms = [part[h * SLAB : (h + 1) * SLAB] for part in wide]
            terms.append(dot(x4[...], e4[h, :, columns]))
            tops = [t[HD : HD + 1] + t[HD + 1 : HD + 2] for t in terms]
            sums = [t[HD + 2 : HD + 3] + t[HD + 3 : HD + 4] for t in terms]
            near_here = near[h, :, columns]
            tops.append(near_top[h : h + 1, columns])
            sums.append(near_here[HD : HD + 1])
            terms.append(near_here)
            top = tops[0]
            for other in tops[1:]:
                top = jnp.maximum(top, other)
            total = jnp.zeros((1, BLOCK), F32)
            factors = [jnp.exp2(t - top) for t in tops]
            for factor, part in zip(factors, sums):
                total = total + factor * part
            inverse = 1.0 / total
            mixed = jnp.zeros((HD, BLOCK), F32)
            for factor, part in zip(factors, terms):
                mixed = mixed + part[0:HD] * (factor * inverse)
            att_s[d, :, h * HD : (h + 1) * HD] = mixed.T.astype(BF16)
        if d:
            copy = remote(
                att_s.at[d], att_r.at[d], a2a_send.at[d - 1], a2a_recv.at[d - 1], s, target
            )
            copy.start()
            a2a.append(copy)

    loads[3].wait()

    def project(block, owner):
        return dot(block, w_s[pl.ds(pl.multiple_of(owner * FEATURES, FEATURES), FEATURES), :])

    total = project(att_s[0], g)
    for d in (1, 2, 3):
        a2a[d - 1].wait_recv()
        total = total + project(att_r[d], lax.rem(g + 4 - d, 4))
    o_ref[0] = total.astype(BF16)

    for copy in [*ring_copies, *l3_copies, l2_copy, far_q, *half_copies, *ret_copies, *a2a]:
        copy.wait_send()

    @pl.when(s > 0)
    def _():
        for copy in to_left:
            copy.wait_send()

    @pl.when(s < last)
    def _():
        for copy in to_right:
            copy.wait_send()


def per_device(queries, key_vectors, value_vectors, out_weight):
    def buf(*shape, dtype=BF16):
        return pltpu.VMEM(shape, dtype)

    dma = pltpu.SemaphoreType.DMA
    scratch = [
        buf(ROWS, 256), buf(768, 256), buf(768, 256), buf(1024, 1024),
        buf(4, 2, 256, 128), buf(2, 2, 256, 128), buf(2, 256, 128), buf(2, 128, 128),
        buf(256, 256), buf(256, 256), buf(2, 128, 256), buf(2, 128, 256), buf(2, 64, 256), buf(2, 128, 256),
        buf(4, SLAB, 768), buf(4, SLAB, 256), buf(4, SLAB, 128), buf(4, SLAB, 128),
        buf(4, 2, 32, 128), buf(2, 128, 128), buf(8, 128, 128), buf(128, 128),
        buf(8, 128, 256, dtype=F32), buf(1024, 256), buf(128, 1024), buf(2, 128, 128), buf(2, 128, 128),
        buf(4 * SLAB, 256), buf(4 * SLAB, 128), buf(4 * SLAB, 64), buf(SLAB, 128),
        buf(256, ROWS), buf(128, ROWS), buf(64, ROWS), buf(4, 128, ROWS),
        buf(4, SLAB, ROWS, dtype=F32), buf(8, ROWS, dtype=F32), buf(4, 128, 256), buf(4, 128, 256),
        dma((4,)), dma((4,)), dma((4,)), dma((3,)), dma((3,)), dma, dma, dma((2,)), dma((2,)),
        dma((7,)), dma((7,)), dma, dma, dma((3,)), dma((3,)), dma((4,)), dma((4,)), dma((3,)), dma((3,)),
    ]
    return pl.pallas_call(
        kernel,
        out_shape=jax.ShapeDtypeStruct((1, BLOCK, 1024), BF16),
        in_specs=[pl.BlockSpec(memory_space=pl.ANY)] * 4,
        out_specs=pl.BlockSpec(memory_space=pltpu.VMEM),
        scratch_shapes=scratch,
        compiler_params=pltpu.CompilerParams(
            collective_id=0, has_side_effects=True, vmem_limit_bytes=40 * 2**20
        ),
    )(queries, key_vectors, value_vectors, out_weight)


def solution(mesh):
    return jax.shard_map(
        per_device,
        mesh=mesh,
        in_specs=(P(None, "seq", "head"), P(None, "seq", "head"), P(None, "seq", "head"), P()),
        out_specs=P(None, ("seq", "head"), None),
        check_vma=False,
    )
```

```python
import math

import jax
import jax.numpy as jnp
from jax import lax
from jax.experimental import pallas as pl
from jax.experimental.pallas import tpu as pltpu
from jax.sharding import PartitionSpec as P

HD = 64
BLOCK = 128
HEADS_HERE = 4
ROWS = 512
FEATURES = HEADS_HERE * HD
SLAB = HD + 16
SCALE = HD**-0.5 * math.log2(math.e)
MASKED = -1e30
BF16, F32 = jnp.bfloat16, jnp.float32
MESH = pl.DeviceIdType.MESH


def iota(shape, axis):
    return lax.broadcasted_iota(jnp.int32, shape, axis)


def dot(a, b):
    return jnp.dot(a, b, preferred_element_type=F32)


def dot_nt(a, b):
    return lax.dot_general(a, b, (((1,), (1,)), ((), ())), preferred_element_type=F32)


def rounded(value):
    return value.astype(BF16).astype(F32)


def split_top(top):
    high = rounded(top)
    return high, rounded(top - high)


def selector(rows, columns, shift, offset=0):
    hit = iota((rows, columns), 0) == offset + (iota((rows, columns), 1) >> shift)
    return jnp.where(hit, 1.0, 0.0).astype(BF16)


def pooler(level):
    rows = ROWS >> level
    hit = iota((rows, ROWS), 0) == (iota((rows, ROWS), 1) >> level)
    return jnp.where(hit, 1.0, 0.0).astype(BF16)


def kernel(
    q_hbm, k_hbm, v_hbm, w_hbm, o_ref,
    q_s, kx, vx, w_s,
    qn, q1m, q2m, q3m,
    k1, v1, kv2_s, kv2_r, kv3_s, kv3_r,
    vtn, vt1, vt2, vt3,
    s1, r1, kv_all, q_far, ret_s, top_r,
    x1, x2, x3, e1, e2, e3,
    near, near_top, att_s, att_r, om_s, om_r, om_x, att_f,
    in_sem, halo_send, halo_recv, s1_send, s1_recv, l2_send, l2_recv, l3_send, l3_recv,
    kv_send, kv_recv, q_send, q_recv, ret_send, ret_recv, a2a_send, a2a_recv, om_send, om_recv,
    half_ready, mirror_ready,
):
    s, g = lax.axis_index("seq"), lax.axis_index("head")
    last = lax.axis_size("seq") - 1
    z, x, y = lax.div(s, 8), lax.rem(lax.div(s, 4), 2), lax.rem(s, 4)
    ring = s - y
    zl = lax.rem(z, 4)
    bit1, bit0 = lax.div(zl, 2), lax.rem(zl, 2)
    half = lax.div(z, 4) * 32
    place = zl * 2 + x
    mirror = (7 - z) * 8 + x * 4
    early, late = z < 4, z >= 4

    def flipped(f):
        high = 1 - bit1 if f & 4 else bit1
        low = 1 - bit0 if f & 2 else bit0
        return (high * 2 + low) * 2 + (1 - x if f & 1 else x)

    def half_peer(f):
        return half + flipped(f) * 4 + y

    loads = [
        pltpu.make_async_copy(k_hbm.at[0], kx.at[pl.ds(BLOCK, ROWS)], in_sem.at[0]),
        pltpu.make_async_copy(v_hbm.at[0], vx.at[pl.ds(BLOCK, ROWS)], in_sem.at[1]),
        pltpu.make_async_copy(q_hbm.at[0], q_s, in_sem.at[2]),
        pltpu.make_async_copy(w_hbm, w_s, in_sem.at[3]),
    ]
    for load in loads:
        load.start()

    barrier = pltpu.get_barrier_semaphore()

    def signal(semaphore, seq, head):
        pl.semaphore_signal(semaphore, inc=1, device_id=(seq, head), device_id_type=MESH)

    for dy in range(4):
        for dg in range(4):
            if dy or dg:
                signal(barrier, ring + lax.rem(y + dy, 4), lax.rem(g + dg, 4))
    left_out = (y == 0) & (s > 0)
    right_out = (y == 3) & (s < last)

    @pl.when(left_out)
    def _():
        signal(barrier, s - 1, g)

    @pl.when(right_out)
    def _():
        signal(barrier, s + 1, g)

    @pl.when(early)
    def _():
        signal(barrier, mirror + y, g)

    for f in range(1, 8):

        @pl.when(late | (flipped(f) > place))
        def _(f=f):
            signal(barrier, half_peer(f), g)

    low32 = iota((32, 128), 1) < HD

    pool4 = pooler(4)
    own_k, own_v = kx.at[pl.ds(BLOCK, ROWS)], vx.at[pl.ds(BLOCK, ROWS)]
    loads[0].wait()
    k4 = rounded(dot(pool4, own_k[...]) * 0.25)
    loads[1].wait()
    v4 = rounded(dot(pool4, own_v[...]) * 0.25)
    loads[2].wait()
    q4 = rounded(dot(pool4, q_s[...]) * 0.25)
    for h in range(HEADS_HERE):
        pair = slice(h // 2 * 128, h // 2 * 128 + 128)
        kp, vp, qp = k4[:, pair], v4[:, pair], q4[:, pair]
        if h % 2 == 0:
            packed = jnp.where(low32, kp, pltpu.roll(vp, HD, 1))
        else:
            packed = jnp.where(low32, pltpu.roll(kp, HD, 1), vp)
            qp = pltpu.roll(qp, HD, 1)
        s1[h, 0] = packed.astype(BF16)
        s1[h, 1] = jnp.where(low32, qp, 0.0).astype(BF16)
    my_rows = pl.ds(pl.multiple_of(y * 32, 32), 32)
    r1[:, my_rows, :] = s1[y]

    pl.semaphore_wait(
        barrier,
        15 + jnp.where(left_out, 1, 0) + jnp.where(right_out, 1, 0) + jnp.where(late, 8, place),
    )

    def remote(src, dst, send, recv, seq, head=None):
        return pltpu.make_async_remote_copy(
            src_ref=src, dst_ref=dst, send_sem=send, recv_sem=recv,
            device_id=(seq, g if head is None else head), device_id_type=MESH,
        )

    ring_copies = [
        remote(
            s1.at[lax.rem(y + d, 4)], r1.at[:, my_rows, :],
            s1_send.at[d - 1], s1_recv.at[d - 1], ring + lax.rem(y + d, 4),
        )
        for d in range(1, 4)
    ]
    for copy in ring_copies:
        copy.start()

    def forward(rows):
        for f in range(1, 8):
            remote(
                r1.at[0, rows, :], kv_all.at[place, rows, :],
                kv_send.at[f - 1], kv_recv.at[f - 1], half_peer(f),
            ).start()

    @pl.when(late)
    def _():
        forward(my_rows)
        signal(mirror_ready, mirror + y, g)

    for f in range(1, 8):

        @pl.when(early & (flipped(f) < place))
        def _(f=f):
            signal(half_ready, half_peer(f), g)

    def pool_pair(level, scale):
        pool = pooler(level)
        return dot(pool, own_k[...]) * scale, dot(pool, own_v[...]) * scale

    kp, vp = pool_pair(3, 0.5**1.5)
    kv3_s[0], kv3_s[1] = kp.astype(BF16), vp.astype(BF16)
    slot3 = pl.ds(pl.multiple_of(lax.rem(y, 2) * 64, 64), 64)
    pair3 = ring + (1 - lax.div(y, 2)) * 2
    l3_copies = [
        remote(kv3_s, kv3_r.at[:, slot3, :], l3_send.at[j], l3_recv.at[lax.rem(y, 2)], pair3 + j)
        for j in range(2)
    ]
    for copy in l3_copies:
        copy.start()
    kp, vp = pool_pair(2, 0.5)
    kv2_s[0], kv2_s[1] = kp.astype(BF16), vp.astype(BF16)
    l2_copy = remote(kv2_s, kv2_r, l2_send, l2_recv, s + 1 - 2 * lax.rem(y, 2))
    l2_copy.start()

    head_rows, tail_rows = pl.ds(0, BLOCK), pl.ds(ROWS - BLOCK, BLOCK)
    to_left = [
        remote(k_hbm.at[0, head_rows], kx.at[pl.ds(BLOCK + ROWS, BLOCK)], halo_send.at[0], halo_recv.at[0], s - 1),
        remote(v_hbm.at[0, head_rows], vx.at[pl.ds(BLOCK + ROWS, BLOCK)], halo_send.at[1], halo_recv.at[1], s - 1),
    ]
    to_right = [
        remote(k_hbm.at[0, tail_rows], kx.at[pl.ds(0, BLOCK)], halo_send.at[2], halo_recv.at[2], s + 1),
        remote(v_hbm.at[0, tail_rows], vx.at[pl.ds(0, BLOCK)], halo_send.at[3], halo_recv.at[3], s + 1),
    ]

    @pl.when(s > 0)
    def _():
        for copy in to_left:
            copy.start()

    @pl.when(s < last)
    def _():
        for copy in to_right:
            copy.start()

    zeros = jnp.zeros((BLOCK, FEATURES), BF16)

    @pl.when(s == 0)
    def _():
        kx[0:BLOCK] = zeros
        vx[0:BLOCK] = zeros

    @pl.when(s == last)
    def _():
        kx[BLOCK + ROWS :] = zeros
        vx[BLOCK + ROWS :] = zeros

    lane_half = iota((1, 128), 1) < HD
    halves = [jnp.where(lane_half, 1.0, 0.0), jnp.where(lane_half, 0.0, 1.0)]

    def masked_queries(dst, field, count):
        for p in range(2):
            part = field[:, p * 128 : p * 128 + 128]
            for odd in range(2):
                dst[p, odd * count : (odd + 1) * count, :] = (part * halves[odd]).astype(BF16)

    for b in range(4):
        masked_queries(qn.at[b], q_s[b * BLOCK : (b + 1) * BLOCK, :].astype(F32), BLOCK)

    ones16 = jnp.ones((16, BLOCK), BF16)

    def turn(dst, block, column):
        turned = block.T
        for h in range(HEADS_HERE):
            dst[h, 0:HD, column : column + BLOCK] = turned[h * HD : (h + 1) * HD, :]
            dst[h, HD:SLAB, column : column + BLOCK] = ones16

    for b in range(1, 5):
        turn(vtn, vx[b * BLOCK : (b + 1) * BLOCK, :], b * BLOCK)

    def attend(keys, queries, values, count, exact, biases=None):
        scores = [dot_nt(key, queries) for key in keys]
        if biases:
            scores = [a if bias is None else a + bias for a, bias in zip(scores, biases)]
        top = jnp.max(scores[0], axis=0, keepdims=True)
        for part in scores[1:]:
            top = jnp.maximum(top, jnp.max(part, axis=0, keepdims=True))
        top = top * SCALE
        high = below = None
        if not exact:
            high, below = split_top(top)
            top = high + below
        weights = [jnp.exp2(part * SCALE - top).astype(BF16) for part in scores]
        weights = weights[0] if len(weights) == 1 else jnp.concatenate(weights, axis=0)
        results = [
            dot(values[odd], weights[:, odd * count : (odd + 1) * count]) for odd in range(2)
        ]
        return top, high, below, results

    def near_block(b):
        for p in range(2):
            lanes = slice(p * 128, p * 128 + 128)
            keys = [kx[(b + i) * BLOCK : (b + i + 1) * BLOCK, lanes] for i in range(3)]
            values = [vtn[2 * p + odd, :, b * BLOCK : (b + 3) * BLOCK] for odd in range(2)]
            biases = [None, None, None]
            if b == 0:
                biases[0] = jnp.where(s == 0, MASKED, 0.0)
            if b == 3:
                biases[2] = jnp.where(s == last, MASKED, 0.0)
            top, _, _, results = attend(keys, qn[b, p], values, BLOCK, True, biases)
            columns = slice(b * BLOCK, (b + 1) * BLOCK)
            for odd in range(2):
                h = 2 * p + odd
                near[h, :, columns] = results[odd]
                near_top[h : h + 1, columns] = top[:, odd * BLOCK : (odd + 1) * BLOCK]

    def small_rows(count, high, below, total):
        row = iota((16, count), 0)
        total_high = rounded(total)
        rows = jnp.where(row == 2, total_high, total - total_high)
        rows = jnp.where(row == 1, below, rows)
        return jnp.where(row == 0, high, rows)

    def sibling(dst, keys, queries, values, count, column):
        for p in range(2):
            lanes = slice(p * 128, p * 128 + 128)
            _, high, below, results = attend(
                [keys[:, lanes]], queries[p], [values(2 * p), values(2 * p + 1)], count, False
            )
            for odd in range(2):
                h = 2 * p + odd
                own = slice(odd * count, (odd + 1) * count)
                columns = slice(column, column + count)
                dst[h * SLAB : h * SLAB + HD, columns] = results[odd][0:HD].astype(BF16)
                dst[h * SLAB + HD : (h + 1) * SLAB, columns] = small_rows(
                    count, high[:, own], below[:, own], results[odd][HD : HD + 1]
                ).astype(BF16)

    near_block(1)

    far_q = remote(r1.at[1], q_far, q_send, q_recv, mirror + y)

    @pl.when(late)
    def _():
        for d in (1, 3, 2):
            ring_copies[d - 1].wait_recv()
            rows = pl.ds(pl.multiple_of(lax.rem(y + 4 - d, 4) * 32, 32), 32)
            forward(rows)
        far_q.start()

    near_block(2)
    pooled_q = dot(pooler(1), q_s[...]) * 0.5**0.5
    for b in range(2):
        masked_queries(q1m.at[b], pooled_q[b * BLOCK : (b + 1) * BLOCK, :], BLOCK)
    masked_queries(q2m, dot(pooler(2), q_s[...]) * 0.5, BLOCK)
    masked_queries(q3m, dot(pooler(3), q_s[...]) * 0.5**1.5, 64)
    kp, vp = pool_pair(1, 0.5**0.5)
    k1[...] = kp.astype(BF16)
    v1[...] = vp.astype(BF16)
    for b in range(2):
        turn(vt1, v1[b * BLOCK : (b + 1) * BLOCK, :], b * BLOCK)
    for b in range(2):
        other = 1 - b
        sibling(
            x1, k1[other * BLOCK : (other + 1) * BLOCK, :], q1m.at[b],
            lambda h, other=other: vt1[h, :, other * BLOCK : (other + 1) * BLOCK], BLOCK, b * BLOCK,
        )
    e1[...] = selector(256, ROWS, 1)
    e2[...] = selector(128, ROWS, 2)
    e3[...] = selector(64, ROWS, 3)

    @pl.when(early)
    def _():
        for copy in ring_copies:
            copy.wait_recv()

        @pl.when(place < 7)
        def _():
            pl.semaphore_wait(half_ready, 7 - place)

        forward(pl.ds(0, BLOCK))

    for j in range(2):
        remote(kv3_s, kv3_r.at[:, pl.ds(j * 64, 64), :], l3_send.at[j], l3_recv.at[j], pair3 + j).wait_recv()
    turn(vt3, kv3_r[1], 0)
    sibling(x3, kv3_r[0], q3m, lambda h: vt3[h], 64, 0)
    l2_copy.wait_recv()
    turn(vt2, kv2_r[1], 0)
    sibling(x2, kv2_r[0], q2m, lambda h: vt2[h], BLOCK, 0)

    @pl.when(s > 0)
    def _():
        for copy in to_right:
            copy.wait_recv()

    turn(vtn, vx[0:BLOCK, :], 0)
    near_block(0)

    @pl.when(s < last)
    def _():
        for copy in to_left:
            copy.wait_recv()

    turn(vtn, vx[BLOCK + ROWS :, :], BLOCK + ROWS)
    near_block(3)

    @pl.when(early)
    def _():
        pl.semaphore_wait(mirror_ready, 1)
        far_q.start()

    a2a = []
    for d in (1, 2, 3, 0):
        target = lax.rem(g + d, 4)
        columns = pl.ds(pl.multiple_of(target * BLOCK, BLOCK), BLOCK)
        wide = [
            dot(field[...], select[:, columns])
            for field, select in ((x1, e1), (x2, e2), (x3, e3))
        ]
        mixes, logs = [], []
        for h in range(HEADS_HERE):
            terms = [part[h * SLAB : (h + 1) * SLAB] for part in wide]
            tops = [t[HD : HD + 1] + t[HD + 1 : HD + 2] for t in terms]
            sums = [t[HD + 2 : HD + 3] + t[HD + 3 : HD + 4] for t in terms]
            near_here = near[h, :, columns]
            tops.append(near_top[h : h + 1, columns])
            sums.append(near_here[HD : HD + 1])
            terms.append(near_here)
            top = tops[0]
            for other in tops[1:]:
                top = jnp.maximum(top, other)
            total = jnp.zeros((1, BLOCK), F32)
            factors = [jnp.exp2(t - top) for t in tops]
            for factor, part in zip(factors, sums):
                total = total + factor * part
            inverse = 1.0 / total
            mixed = jnp.zeros((HD, BLOCK), F32)
            for factor, part in zip(factors, terms):
                mixed = mixed + part[0:HD] * (factor * inverse)
            mixes.append(mixed)
            logs.append(top + jnp.log2(total))
        mixed = jnp.concatenate(mixes, axis=0).T.astype(BF16)
        row = iota((8, BLOCK), 0)
        rows = jnp.zeros((8, BLOCK), F32)
        for h in range(HEADS_HERE):
            rows = jnp.where(row == h, logs[h], rows)
        if d:
            att_s[d - 1] = mixed
            om_s[d - 1] = rows
            pair = [
                remote(att_s.at[d - 1], att_r.at[g], a2a_send.at[d - 1], a2a_recv.at[d - 1], s, target),
                remote(om_s.at[d - 1], om_r.at[g], om_send.at[d - 1], om_recv.at[d - 1], s, target),
            ]
            for copy in pair:
                copy.start()
            a2a += pair
        else:
            att_r[g] = mixed
            om_r[g] = rows

    far_q.wait_recv()
    queries = jnp.concatenate([r1[1], q_far[...]], axis=0)
    low128 = iota((128, 128), 1) < HD
    top = acc = None
    for f in range(8):
        if f:
            remote(
                r1.at[0], kv_all.at[flipped(f)], kv_send.at[f - 1], kv_recv.at[f - 1], half_peer(f)
            ).wait_recv()
        block = kv_all[flipped(f)] if f else r1[0]
        scores = dot_nt(block, queries)
        turned = jnp.where(low128, 1.0, block.astype(F32)).T.astype(BF16)
        here = jnp.max(scores, axis=0, keepdims=True) * SCALE
        high = here if f == 0 else jnp.maximum(top, here)
        weights = jnp.exp2(scores * SCALE - high)
        if f == 1:
            weights = jnp.concatenate([weights[:, 0:128] * 2.0, weights[:, 128:256]], axis=1)
        part = dot(turned, weights.astype(BF16))
        acc = part if f == 0 else acc * jnp.exp2(top - high) + part
        top = high
    sums = acc[0:HD]
    logs = top + jnp.log2(sums)
    means = acc[HD:] / sums
    odd_head = lax.rem(y, 2) == 1
    result = jnp.concatenate(
        [jnp.where(odd_head, logs, means), jnp.where(odd_head, means, logs)], axis=0
    )
    ret_s[...] = result.T
    head_here = g * 4 + y

    def give(slot, row, seq, head):
        remote(
            ret_s.at[pl.ds(pl.multiple_of(row, 8), 8), :], top_r.at[slot, head_here],
            ret_send.at[slot], ret_recv.at[slot], seq, head,
        ).start()

    for j in range(4):
        for t in range(4):
            give(1, 128 + j * 32 + t * 8, mirror + j, t)
    for dy in range(4):
        for dg in range(4):
            if dy or dg:
                there, t = lax.rem(y + dy, 4), lax.rem(g + dg, 4)
                give(0, there * 32 + t * 8, ring + there, t)
    top_r[0, head_here] = ret_s[pl.ds(pl.multiple_of(y * 32 + g * 8, 8), 8), :]

    for copy in a2a:
        copy.wait_recv()
    logs = om_r[...].reshape(32, BLOCK)
    high = rounded(logs)
    middle = rounded(logs - high)
    lowest = rounded(logs - high - middle)
    logs = jnp.concatenate([high, middle, lowest, jnp.zeros((32, BLOCK), F32)], axis=0)
    k, c = iota((128, 1024), 0), iota((128, 1024), 1)
    hit = ((k & 31) == ((c >> 8) * 8 + ((c >> 6) & 3))) & (k < 96)
    spread = jnp.where(hit, 1.0, 0.0).astype(BF16)
    om_x[...] = dot(logs.T.astype(BF16), spread)
    loads[3].wait()

    def arrived(slot, heads):
        remote(
            top_r.at[slot, pl.ds(0, heads)], top_r.at[slot, pl.ds(0, heads)],
            ret_send.at[slot], ret_recv.at[slot], mirror + y,
        ).wait_recv()

    arrived(0, 15)
    arrived(1, 16)
    low8 = iota((8, 128), 1) < HD
    for p in range(8):
        means, logs = [], []
        for slot in range(2):
            even, odd = top_r[slot, 2 * p], top_r[slot, 2 * p + 1]
            means.append(jnp.where(low8, even, odd))
            logs.append(pltpu.roll(jnp.where(low8, odd, even), HD, 1))
        top = jnp.maximum(logs[0], logs[1])
        factors = [jnp.exp2(t - top) for t in logs]
        total = factors[0] + factors[1]
        mean = (means[0] * factors[0] + means[1] * factors[1]) / total
        log = top + jnp.log2(total)
        lanes = slice(p * 128, p * 128 + 128)
        here = slice(p % 2 * 128, p % 2 * 128 + 128)
        for q in range(8):
            rows = slice(q * 16, q * 16 + 16)
            other = att_r[p // 2, rows, here].astype(F32)
            share = 1.0 / (1.0 + jnp.exp2(om_x[rows, lanes] - log[q : q + 1]))
            att_f[rows, lanes] = (other + (mean[q : q + 1] - other) * share).astype(BF16)
    o_ref[0] = dot(att_f[...], w_s[...]).astype(BF16)

    for copy in [*ring_copies, *l3_copies, l2_copy, far_q, *a2a]:
        copy.wait_send()
    for f in range(1, 8):
        remote(r1.at[0], kv_all.at[place], kv_send.at[f - 1], kv_recv.at[f - 1], half_peer(f)).wait_send()
    for slot, rows in ((0, 120), (1, 128)):
        remote(
            ret_s.at[pl.ds(0, rows)], ret_s.at[pl.ds(0, rows)],
            ret_send.at[slot], ret_recv.at[slot], mirror + y,
        ).wait_send()

    @pl.when(s > 0)
    def _():
        for copy in to_left:
            copy.wait_send()

    @pl.when(s < last)
    def _():
        for copy in to_right:
            copy.wait_send()


def per_device(queries, key_vectors, value_vectors, out_weight):
    def buf(*shape, dtype=BF16):
        return pltpu.VMEM(shape, dtype)

    dma = pltpu.SemaphoreType.DMA
    regular = pltpu.SemaphoreType.REGULAR
    scratch = [
        buf(ROWS, 256), buf(768, 256), buf(768, 256), buf(1024, 1024),
        buf(4, 2, 256, 128), buf(2, 2, 256, 128), buf(2, 256, 128), buf(2, 128, 128),
        buf(256, 256), buf(256, 256), buf(2, 128, 256), buf(2, 128, 256), buf(2, 64, 256), buf(2, 128, 256),
        buf(4, SLAB, 768), buf(4, SLAB, 256), buf(4, SLAB, 128), buf(4, SLAB, 128),
        buf(4, 2, 32, 128), buf(2, 128, 128), buf(8, 128, 128), buf(128, 128),
        buf(256, 128, dtype=F32), buf(2, 16, 8, 128, dtype=F32),
        buf(4 * SLAB, 256), buf(4 * SLAB, 128), buf(4 * SLAB, 64),
        buf(256, ROWS), buf(128, ROWS), buf(64, ROWS),
        buf(4, SLAB, ROWS, dtype=F32), buf(8, ROWS, dtype=F32), buf(3, 128, 256), buf(4, 128, 256),
        buf(3, 8, 128, dtype=F32), buf(4, 8, 128, dtype=F32), buf(128, 1024, dtype=F32), buf(128, 1024),
        dma((4,)), dma((4,)), dma((4,)), dma((3,)), dma((3,)), dma, dma, dma((2,)), dma((2,)),
        dma((7,)), dma((7,)), dma, dma, dma((2,)), dma((2,)), dma((3,)), dma((3,)), dma((3,)), dma((3,)),
        regular, regular,
    ]
    return pl.pallas_call(
        kernel,
        out_shape=pltpu.VMEM((1, BLOCK, 1024), BF16),
        in_specs=[pl.BlockSpec(memory_space=pl.ANY)] * 4,
        out_specs=pl.BlockSpec(memory_space=pltpu.VMEM),
        scratch_shapes=scratch,
        compiler_params=pltpu.CompilerParams(
            collective_id=0, has_side_effects=True, vmem_limit_bytes=58 * 2**20
        ),
    )(queries, key_vectors, value_vectors, out_weight)


def solution(mesh):
    return jax.shard_map(
        per_device,
        mesh=mesh,
        in_specs=(P(None, "seq", "head"), P(None, "seq", "head"), P(None, "seq", "head"), P()),
        out_specs=P(None, ("seq", "head"), None),
        check_vma=False,
    )
```

```python
import math

import jax
import jax.numpy as jnp
from jax import lax
from jax.experimental import pallas as pl
from jax.experimental.pallas import tpu as pltpu
from jax.sharding import PartitionSpec as P

HD = 64
BLOCK = 128
HEADS_HERE = 4
ROWS = 512
FEATURES = HEADS_HERE * HD
SLAB = HD + 16
SCALE = HD**-0.5 * math.log2(math.e)
MASKED = -1e30
BF16, F32 = jnp.bfloat16, jnp.float32
MESH = pl.DeviceIdType.MESH


def iota(shape, axis):
    return lax.broadcasted_iota(jnp.int32, shape, axis)


def dot(a, b):
    return jnp.dot(a, b, preferred_element_type=F32)


def dot_nt(a, b):
    return lax.dot_general(a, b, (((1,), (1,)), ((), ())), preferred_element_type=F32)


def rounded(value):
    return value.astype(BF16).astype(F32)


def split_top(top):
    high = rounded(top)
    return high, rounded(top - high)


def selector(rows, columns, shift, offset=0):
    hit = iota((rows, columns), 0) == offset + (iota((rows, columns), 1) >> shift)
    return jnp.where(hit, 1.0, 0.0).astype(BF16)


def pooler(level):
    rows = ROWS >> level
    hit = iota((rows, ROWS), 0) == (iota((rows, ROWS), 1) >> level)
    return jnp.where(hit, 1.0, 0.0).astype(BF16)


def kernel(
    q_hbm, k_hbm, v_hbm, w_hbm, o_ref,
    q_s, kx, vx, w_s,
    qn, q1m, q2m, q3m,
    k1, v1, kv2_s, kv2_r, kv3_s, kv3_r,
    vtn, vt1, vt2, vt3,
    s1, r1, kv_all, q_far, ret_s, top_r,
    x1, x2, x3, e1, e2, e3,
    near, near_top, att_s, att_r, om_s, om_r, om_x, att_f,
    in_sem, halo_send, halo_recv, s1_send, s1_recv, l2_send, l2_recv, l3_send, l3_recv,
    kv_send, direct_send, kv_recv, q_send, q_recv, ret_send, ret_recv, a2a_send, a2a_recv, om_send, om_recv,
    chain_up, chain_down, late_in,
):
    s, g = lax.axis_index("seq"), lax.axis_index("head")
    last = lax.axis_size("seq") - 1
    z, x, y = lax.div(s, 8), lax.rem(lax.div(s, 4), 2), lax.rem(s, 4)
    ring = s - y
    zl = lax.rem(z, 4)
    bits = [lax.rem(z, 2), lax.rem(lax.div(z, 2), 2), lax.div(z, 4)]
    mirror = z * 8 + (1 - x) * 4
    early, late = z < 4, z >= 4

    def flipped(f):
        low, middle, high = [1 - bit if f >> i & 1 else bit for i, bit in enumerate(bits)]
        return high * 4 + middle * 2 + low

    def column(other):
        return other * 8 + x * 4

    loads = [
        pltpu.make_async_copy(k_hbm.at[0], kx.at[pl.ds(BLOCK, ROWS)], in_sem.at[0]),
        pltpu.make_async_copy(v_hbm.at[0], vx.at[pl.ds(BLOCK, ROWS)], in_sem.at[1]),
        pltpu.make_async_copy(q_hbm.at[0], q_s, in_sem.at[2]),
        pltpu.make_async_copy(w_hbm, w_s, in_sem.at[3]),
    ]
    for load in loads:
        load.start()

    barrier = pltpu.get_barrier_semaphore()

    def signal(semaphore, seq, head):
        pl.semaphore_signal(semaphore, inc=1, device_id=(seq, head), device_id_type=MESH)

    ring_start, ring_end = (y == 0) & (s > 0), (y == 3) & (s < last)

    @pl.when(early)
    def _():
        for other in range(4, 8):
            for j in range(4):
                signal(barrier, column(other) + j, g)

    @pl.when(ring_start)
    def _():
        signal(barrier, s - 1, g)

    @pl.when(ring_end)
    def _():
        signal(barrier, s + 1, g)

    for d in range(1, 4):
        signal(barrier, ring + lax.rem(y + d, 4), g)
        signal(barrier, s, lax.rem(g + d, 4))
    signal(barrier, mirror + y, g)

    @pl.when(zl < 3)
    def _():
        signal(barrier, s + 8, g)

    @pl.when(zl > 0)
    def _():
        signal(barrier, s - 8, g)

    low32 = iota((32, 128), 1) < HD

    pool4 = pooler(4)
    own_k, own_v = kx.at[pl.ds(BLOCK, ROWS)], vx.at[pl.ds(BLOCK, ROWS)]
    loads[0].wait()
    k4 = rounded(dot(pool4, own_k[...]) * 0.25)
    loads[1].wait()
    v4 = rounded(dot(pool4, own_v[...]) * 0.25)
    loads[2].wait()
    q4 = rounded(dot(pool4, q_s[...]) * 0.25)
    for h in range(HEADS_HERE):
        pair = slice(h // 2 * 128, h // 2 * 128 + 128)
        kp, vp, qp = k4[:, pair], v4[:, pair], q4[:, pair]
        if h % 2 == 0:
            packed = jnp.where(low32, kp, pltpu.roll(vp, HD, 1))
        else:
            packed = jnp.where(low32, pltpu.roll(kp, HD, 1), vp)
            qp = pltpu.roll(qp, HD, 1)
        s1[h, 0] = packed.astype(BF16)
        s1[h, 1] = jnp.where(low32, qp, 0.0).astype(BF16)
    my_rows = pl.ds(pl.multiple_of(y * 32, 32), 32)
    r1[:, my_rows, :] = s1[y]

    pl.semaphore_wait(
        barrier,
        7
        + jnp.where(late, 16, 0)
        + jnp.where(zl > 0, 1, 0)
        + jnp.where(zl < 3, 1, 0)
        + jnp.where(ring_start, 1, 0)
        + jnp.where(ring_end, 1, 0),
    )

    def remote(src, dst, send, recv, seq, head=None):
        return pltpu.make_async_remote_copy(
            src_ref=src, dst_ref=dst, send_sem=send, recv_sem=recv,
            device_id=(seq, g if head is None else head), device_id_type=MESH,
        )

    ring_copies = [
        remote(
            s1.at[lax.rem(y + d, 4)], r1.at[:, my_rows, :],
            s1_send.at[d - 1], s1_recv.at[d - 1], ring + lax.rem(y + d, 4),
        )
        for d in range(1, 4)
    ]
    head_rows, tail_rows = pl.ds(0, BLOCK), pl.ds(ROWS - BLOCK, BLOCK)
    to_left = [
        remote(k_hbm.at[0, head_rows], kx.at[pl.ds(BLOCK + ROWS, BLOCK)], halo_send.at[0], halo_recv.at[0], s - 1),
        remote(v_hbm.at[0, head_rows], vx.at[pl.ds(BLOCK + ROWS, BLOCK)], halo_send.at[1], halo_recv.at[1], s - 1),
    ]
    to_right = [
        remote(k_hbm.at[0, tail_rows], kx.at[pl.ds(0, BLOCK)], halo_send.at[2], halo_recv.at[2], s + 1),
        remote(v_hbm.at[0, tail_rows], vx.at[pl.ds(0, BLOCK)], halo_send.at[3], halo_recv.at[3], s + 1),
    ]
    for copy in ring_copies:
        copy.start()

    @pl.when(s > 0)
    def _():
        for copy in to_left:
            copy.start()

    @pl.when(s < last)
    def _():
        for copy in to_right:
            copy.start()

    @pl.when(zl == 1)
    def _():
        signal(chain_up, s + 8, g)

    @pl.when(zl == 2)
    def _():
        signal(chain_down, s - 8, g)

    @pl.when(late)
    def _():
        for i in range(4):
            h = lax.rem(y + i, 4)
            for other in range(4):
                remote(
                    s1.at[h, 0], kv_all.at[z, my_rows, :], direct_send, kv_recv.at[z],
                    column(other) + h,
                ).start()
        for other in range(4):
            signal(late_in, column(other) + y, g)

    def pool_pair(level, scale):
        pool = pooler(level)
        return dot(pool, own_k[...]) * scale, dot(pool, own_v[...]) * scale

    kp, vp = pool_pair(3, 0.5**1.5)
    kv3_s[0], kv3_s[1] = kp.astype(BF16), vp.astype(BF16)
    kp, vp = pool_pair(2, 0.5)
    kv2_s[0], kv2_s[1] = kp.astype(BF16), vp.astype(BF16)

    slot3 = pl.ds(pl.multiple_of(lax.rem(y, 2) * 64, 64), 64)
    pair3 = ring + (1 - lax.div(y, 2)) * 2
    l3_copies = [
        remote(kv3_s, kv3_r.at[:, slot3, :], l3_send.at[j], l3_recv.at[lax.rem(y, 2)], pair3 + j)
        for j in range(2)
    ]
    l2_copy = remote(kv2_s, kv2_r, l2_send, l2_recv, s + 1 - 2 * lax.rem(y, 2))
    for copy in [*l3_copies, l2_copy]:
        copy.start()

    zeros = jnp.zeros((BLOCK, FEATURES), BF16)

    @pl.when(s == 0)
    def _():
        kx[0:BLOCK] = zeros
        vx[0:BLOCK] = zeros

    @pl.when(s == last)
    def _():
        kx[BLOCK + ROWS :] = zeros
        vx[BLOCK + ROWS :] = zeros

    lane_half = iota((1, 128), 1) < HD
    halves = [jnp.where(lane_half, 1.0, 0.0), jnp.where(lane_half, 0.0, 1.0)]

    def masked_queries(dst, field, count):
        for p in range(2):
            part = field[:, p * 128 : p * 128 + 128]
            for odd in range(2):
                dst[p, odd * count : (odd + 1) * count, :] = (part * halves[odd]).astype(BF16)

    for b in range(4):
        masked_queries(qn.at[b], q_s[b * BLOCK : (b + 1) * BLOCK, :].astype(F32), BLOCK)

    ones16 = jnp.ones((16, BLOCK), BF16)

    def turn(dst, block, column):
        turned = block.T
        for h in range(HEADS_HERE):
            dst[h, 0:HD, column : column + BLOCK] = turned[h * HD : (h + 1) * HD, :]
            dst[h, HD:SLAB, column : column + BLOCK] = ones16

    for b in range(1, 5):
        turn(vtn, vx[b * BLOCK : (b + 1) * BLOCK, :], b * BLOCK)

    def attend(keys, queries, values, count, exact, biases=None):
        scores = [dot_nt(key, queries) for key in keys]
        if biases:
            scores = [a if bias is None else a + bias for a, bias in zip(scores, biases)]
        top = jnp.max(scores[0], axis=0, keepdims=True)
        for part in scores[1:]:
            top = jnp.maximum(top, jnp.max(part, axis=0, keepdims=True))
        top = top * SCALE
        high = below = None
        if not exact:
            high, below = split_top(top)
            top = high + below
        weights = [jnp.exp2(part * SCALE - top).astype(BF16) for part in scores]
        weights = weights[0] if len(weights) == 1 else jnp.concatenate(weights, axis=0)
        results = [
            dot(values[odd], weights[:, odd * count : (odd + 1) * count]) for odd in range(2)
        ]
        return top, high, below, results

    def near_block(b):
        for p in range(2):
            lanes = slice(p * 128, p * 128 + 128)
            keys = [kx[(b + i) * BLOCK : (b + i + 1) * BLOCK, lanes] for i in range(3)]
            values = [vtn[2 * p + odd, :, b * BLOCK : (b + 3) * BLOCK] for odd in range(2)]
            biases = [None, None, None]
            if b == 0:
                biases[0] = jnp.where(s == 0, MASKED, 0.0)
            if b == 3:
                biases[2] = jnp.where(s == last, MASKED, 0.0)
            top, _, _, results = attend(keys, qn[b, p], values, BLOCK, True, biases)
            columns = slice(b * BLOCK, (b + 1) * BLOCK)
            for odd in range(2):
                h = 2 * p + odd
                near[h, :, columns] = results[odd]
                near_top[h : h + 1, columns] = top[:, odd * BLOCK : (odd + 1) * BLOCK]

    def small_rows(count, high, below, total):
        row = iota((16, count), 0)
        total_high = rounded(total)
        rows = jnp.where(row == 2, total_high, total - total_high)
        rows = jnp.where(row == 1, below, rows)
        return jnp.where(row == 0, high, rows)

    def sibling(dst, keys, queries, values, count, column):
        for p in range(2):
            lanes = slice(p * 128, p * 128 + 128)
            _, high, below, results = attend(
                [keys[:, lanes]], queries[p], [values(2 * p), values(2 * p + 1)], count, False
            )
            for odd in range(2):
                h = 2 * p + odd
                own = slice(odd * count, (odd + 1) * count)
                columns = slice(column, column + count)
                dst[h * SLAB : h * SLAB + HD, columns] = results[odd][0:HD].astype(BF16)
                dst[h * SLAB + HD : (h + 1) * SLAB, columns] = small_rows(
                    count, high[:, own], below[:, own], results[odd][HD : HD + 1]
                ).astype(BF16)

    near_block(1)
    @pl.when(zl <= 1)
    def _():
        pl.semaphore_wait(chain_down, 1)

    @pl.when(zl >= 2)
    def _():
        pl.semaphore_wait(chain_up, 1)

    @pl.when(zl == 1)
    def _():
        signal(chain_down, s - 8, g)

    @pl.when(zl == 2)
    def _():
        signal(chain_up, s + 8, g)

    near_block(2)
    pooled_q = dot(pooler(1), q_s[...]) * 0.5**0.5
    for b in range(2):
        masked_queries(q1m.at[b], pooled_q[b * BLOCK : (b + 1) * BLOCK, :], BLOCK)
    masked_queries(q2m, dot(pooler(2), q_s[...]) * 0.5, BLOCK)
    masked_queries(q3m, dot(pooler(3), q_s[...]) * 0.5**1.5, 64)
    kp, vp = pool_pair(1, 0.5**0.5)
    k1[...] = kp.astype(BF16)
    v1[...] = vp.astype(BF16)
    for b in range(2):
        turn(vt1, v1[b * BLOCK : (b + 1) * BLOCK, :], b * BLOCK)
    for b in range(2):
        other = 1 - b
        sibling(
            x1, k1[other * BLOCK : (other + 1) * BLOCK, :], q1m.at[b],
            lambda h, other=other: vt1[h, :, other * BLOCK : (other + 1) * BLOCK], BLOCK, b * BLOCK,
        )
    e1[...] = selector(256, ROWS, 1)
    e2[...] = selector(128, ROWS, 2)
    e3[...] = selector(64, ROWS, 3)

    far_q = remote(r1.at[1], q_far, q_send, q_recv, mirror + y)
    for copy in ring_copies:
        copy.wait_recv()
    far_q.start()

    def forward(f):
        return remote(
            r1.at[0], kv_all.at[z], kv_send.at[f - 1], kv_recv.at[z], column(flipped(f)) + y
        )

    for f in range(1, 4):
        forward(f).start()

    @pl.when(s > 0)
    def _():
        for copy in to_right:
            copy.wait_recv()

    turn(vtn, vx[0:BLOCK, :], 0)
    near_block(0)

    @pl.when(s < last)
    def _():
        for copy in to_left:
            copy.wait_recv()

    turn(vtn, vx[BLOCK + ROWS :, :], BLOCK + ROWS)
    near_block(3)

    @pl.when(early)
    def _():
        pl.semaphore_wait(late_in, 4)
        for f in range(4, 8):
            forward(f).start()

    l2_copy.wait_recv()
    turn(vt2, kv2_r[1], 0)
    sibling(x2, kv2_r[0], q2m, lambda h: vt2[h], BLOCK, 0)

    for j in range(2):
        remote(kv3_s, kv3_r.at[:, pl.ds(j * 64, 64), :], l3_send.at[j], l3_recv.at[j], pair3 + j).wait_recv()
    turn(vt3, kv3_r[1], 0)
    sibling(x3, kv3_r[0], q3m, lambda h: vt3[h], 64, 0)
    a2a = []
    for d in (1, 2, 3, 0):
        target = lax.rem(g + d, 4)
        columns = pl.ds(pl.multiple_of(target * BLOCK, BLOCK), BLOCK)
        wide = [
            dot(field[...], select[:, columns])
            for field, select in ((x1, e1), (x2, e2), (x3, e3))
        ]
        mixes, logs = [], []
        for h in range(HEADS_HERE):
            terms = [part[h * SLAB : (h + 1) * SLAB] for part in wide]
            tops = [t[HD : HD + 1] + t[HD + 1 : HD + 2] for t in terms]
            sums = [t[HD + 2 : HD + 3] + t[HD + 3 : HD + 4] for t in terms]
            near_here = near[h, :, columns]
            tops.append(near_top[h : h + 1, columns])
            sums.append(near_here[HD : HD + 1])
            terms.append(near_here)
            top = tops[0]
            for other in tops[1:]:
                top = jnp.maximum(top, other)
            total = jnp.zeros((1, BLOCK), F32)
            factors = [jnp.exp2(t - top) for t in tops]
            for factor, part in zip(factors, sums):
                total = total + factor * part
            inverse = 1.0 / total
            mixed = jnp.zeros((HD, BLOCK), F32)
            for factor, part in zip(factors, terms):
                mixed = mixed + part[0:HD] * (factor * inverse)
            mixes.append(mixed)
            logs.append(top + jnp.log2(total))
        mixed = jnp.concatenate(mixes, axis=0).T.astype(BF16)
        row = iota((8, BLOCK), 0)
        rows = jnp.zeros((8, BLOCK), F32)
        for h in range(HEADS_HERE):
            rows = jnp.where(row == h, logs[h], rows)
        if d:
            att_s[d - 1] = mixed
            om_s[d - 1] = rows
            pair = [
                remote(att_s.at[d - 1], att_r.at[g], a2a_send.at[d - 1], a2a_recv.at[d - 1], s, target),
                remote(om_s.at[d - 1], om_r.at[g], om_send.at[d - 1], om_recv.at[d - 1], s, target),
            ]
            for copy in pair:
                copy.start()
            a2a += pair
        else:
            att_r[g] = mixed
            om_r[g] = rows

    far_q.wait_recv()
    queries = jnp.concatenate([r1[1], q_far[...]], axis=0)
    low128 = iota((128, 128), 1) < HD
    top = acc = None
    for f in (0, 1, 2, 3, 7, 6, 5, 4):
        if f:
            other = flipped(f)
            remote(
                kv_all.at[other], kv_all.at[other], kv_send.at[f - 1], kv_recv.at[other], column(other) + y
            ).wait_recv()
        block = kv_all[flipped(f)] if f else r1[0]
        scores = dot_nt(block, queries)
        turned = jnp.where(low128, 1.0, block.astype(F32)).T.astype(BF16)
        here = jnp.max(scores, axis=0, keepdims=True) * SCALE
        high = here if f == 0 else jnp.maximum(top, here)
        weights = jnp.exp2(scores * SCALE - high)
        if f == 0:
            weights = jnp.concatenate([weights[:, 0:128], weights[:, 128:256] * 2.0], axis=1)
        part = dot(turned, weights.astype(BF16))
        acc = part if f == 0 else acc * jnp.exp2(top - high) + part
        top = high
    sums = acc[0:HD]
    logs = top + jnp.log2(sums)
    means = acc[HD:] / sums
    odd_head = lax.rem(y, 2) == 1
    result = jnp.concatenate(
        [jnp.where(odd_head, logs, means), jnp.where(odd_head, means, logs)], axis=0
    )
    ret_s[...] = result.T
    head_here = g * 4 + y

    def give(slot, row, seq, head):
        remote(
            ret_s.at[pl.ds(pl.multiple_of(row, 8), 8), :], top_r.at[slot, head_here],
            ret_send.at[slot], ret_recv.at[slot], seq, head,
        ).start()

    for j in range(4):
        for t in range(4):
            give(1, 128 + j * 32 + t * 8, mirror + j, t)
    for dy in range(4):
        for dg in range(4):
            if dy or dg:
                there, t = lax.rem(y + dy, 4), lax.rem(g + dg, 4)
                give(0, there * 32 + t * 8, ring + there, t)
    top_r[0, head_here] = ret_s[pl.ds(pl.multiple_of(y * 32 + g * 8, 8), 8), :]

    for copy in a2a:
        copy.wait_recv()
    logs = om_r[...].reshape(32, BLOCK)
    high = rounded(logs)
    middle = rounded(logs - high)
    lowest = rounded(logs - high - middle)
    logs = jnp.concatenate([high, middle, lowest, jnp.zeros((32, BLOCK), F32)], axis=0)
    k, c = iota((128, 1024), 0), iota((128, 1024), 1)
    hit = ((k & 31) == ((c >> 8) * 8 + ((c >> 6) & 3))) & (k < 96)
    spread = jnp.where(hit, 1.0, 0.0).astype(BF16)
    om_x[...] = dot(logs.T.astype(BF16), spread)
    loads[3].wait()

    def arrived(slot, heads):
        remote(
            top_r.at[slot, pl.ds(0, heads)], top_r.at[slot, pl.ds(0, heads)],
            ret_send.at[slot], ret_recv.at[slot], mirror + y,
        ).wait_recv()

    arrived(0, 15)
    arrived(1, 16)
    low8 = iota((8, 128), 1) < HD
    for p in range(8):
        means, logs = [], []
        for slot in range(2):
            even, odd = top_r[slot, 2 * p], top_r[slot, 2 * p + 1]
            means.append(jnp.where(low8, even, odd))
            logs.append(pltpu.roll(jnp.where(low8, odd, even), HD, 1))
        top = jnp.maximum(logs[0], logs[1])
        factors = [jnp.exp2(t - top) for t in logs]
        total = factors[0] + factors[1]
        mean = (means[0] * factors[0] + means[1] * factors[1]) / total
        log = top + jnp.log2(total)
        lanes = slice(p * 128, p * 128 + 128)
        here = slice(p % 2 * 128, p % 2 * 128 + 128)
        for q in range(8):
            rows = slice(q * 16, q * 16 + 16)
            other = att_r[p // 2, rows, here].astype(F32)
            share = 1.0 / (1.0 + jnp.exp2(om_x[rows, lanes] - log[q : q + 1]))
            att_f[rows, lanes] = (other + (mean[q : q + 1] - other) * share).astype(BF16)
    o_ref[0] = dot(att_f[...], w_s[...]).astype(BF16)

    for copy in [*ring_copies, *l3_copies, l2_copy, far_q, *a2a]:
        copy.wait_send()
    for f in range(1, 4):
        forward(f).wait_send()

    @pl.when(early)
    def _():
        for f in range(4, 8):
            forward(f).wait_send()

    @pl.when(late)
    def _():
        remote(kv_all.at[0:4], kv_all.at[0:4], direct_send, kv_recv.at[z], mirror + y).wait_send()

    for slot, rows in ((0, 120), (1, 128)):
        remote(
            ret_s.at[pl.ds(0, rows)], ret_s.at[pl.ds(0, rows)],
            ret_send.at[slot], ret_recv.at[slot], mirror + y,
        ).wait_send()

    @pl.when(s > 0)
    def _():
        for copy in to_left:
            copy.wait_send()

    @pl.when(s < last)
    def _():
        for copy in to_right:
            copy.wait_send()


def per_device(queries, key_vectors, value_vectors, out_weight):
    def buf(*shape, dtype=BF16):
        return pltpu.VMEM(shape, dtype)

    dma = pltpu.SemaphoreType.DMA
    regular = pltpu.SemaphoreType.REGULAR
    scratch = [
        buf(ROWS, 256), buf(768, 256), buf(768, 256), buf(1024, 1024),
        buf(4, 2, 256, 128), buf(2, 2, 256, 128), buf(2, 256, 128), buf(2, 128, 128),
        buf(256, 256), buf(256, 256), buf(2, 128, 256), buf(2, 128, 256), buf(2, 64, 256), buf(2, 128, 256),
        buf(4, SLAB, 768), buf(4, SLAB, 256), buf(4, SLAB, 128), buf(4, SLAB, 128),
        buf(4, 2, 32, 128), buf(2, 128, 128), buf(8, 128, 128), buf(128, 128),
        buf(256, 128, dtype=F32), buf(2, 16, 8, 128, dtype=F32),
        buf(4 * SLAB, 256), buf(4 * SLAB, 128), buf(4 * SLAB, 64),
        buf(256, ROWS), buf(128, ROWS), buf(64, ROWS),
        buf(4, SLAB, ROWS, dtype=F32), buf(8, ROWS, dtype=F32), buf(3, 128, 256), buf(4, 128, 256),
        buf(3, 8, 128, dtype=F32), buf(4, 8, 128, dtype=F32), buf(128, 1024, dtype=F32), buf(128, 1024),
        dma((4,)), dma((4,)), dma((4,)), dma((3,)), dma((3,)), dma, dma, dma((2,)), dma((2,)),
        dma((7,)), dma, dma((8,)), dma, dma, dma((2,)), dma((2,)), dma((3,)), dma((3,)), dma((3,)), dma((3,)),
        regular, regular, regular,
    ]
    return pl.pallas_call(
        kernel,
        out_shape=pltpu.VMEM((1, BLOCK, 1024), BF16),
        in_specs=[pl.BlockSpec(memory_space=pl.ANY)] * 4,
        out_specs=pl.BlockSpec(memory_space=pltpu.VMEM),
        scratch_shapes=scratch,
        compiler_params=pltpu.CompilerParams(
            collective_id=0, has_side_effects=True, vmem_limit_bytes=58 * 2**20
        ),
    )(queries, key_vectors, value_vectors, out_weight)


def solution(mesh):
    return jax.shard_map(
        per_device,
        mesh=mesh,
        in_specs=(P(None, "seq", "head"), P(None, "seq", "head"), P(None, "seq", "head"), P()),
        out_specs=P(None, ("seq", "head"), None),
        check_vma=False,
    )
```

```python
import math

import jax
import jax.numpy as jnp
from jax import lax
from jax.experimental import pallas as pl
from jax.experimental.pallas import tpu as pltpu
from jax.sharding import PartitionSpec as P

HD = 64
BLOCK = 128
HEADS_HERE = 4
ROWS = 512
FEATURES = HEADS_HERE * HD
SLAB = HD + 16
SCALE = HD**-0.5 * math.log2(math.e)
MASKED = -1e30
BF16, F32 = jnp.bfloat16, jnp.float32
MESH = pl.DeviceIdType.MESH


def iota(shape, axis):
    return lax.broadcasted_iota(jnp.int32, shape, axis)


def dot(a, b):
    return jnp.dot(a, b, preferred_element_type=F32)


def dot_nt(a, b):
    return lax.dot_general(a, b, (((1,), (1,)), ((), ())), preferred_element_type=F32)


def rounded(value):
    return value.astype(BF16).astype(F32)


def split_top(top):
    high = rounded(top)
    return high, rounded(top - high)


def selector(rows, columns, shift, offset=0):
    hit = iota((rows, columns), 0) == offset + (iota((rows, columns), 1) >> shift)
    return jnp.where(hit, 1.0, 0.0).astype(BF16)


def pooler(level):
    rows = ROWS >> level
    hit = iota((rows, ROWS), 0) == (iota((rows, ROWS), 1) >> level)
    return jnp.where(hit, 1.0, 0.0).astype(BF16)


def kernel(
    q_hbm, k_hbm, v_hbm, w_hbm, o_ref,
    q_s, kx, vx, w_s,
    qn, q1m, q2m, q3m,
    k1, v1, kv2_s, kv2_r, kv3_s, kv3_r,
    vtn, vt1, vt2, vt3,
    s1, r1, kv_all, q_far, ret_s, top_r,
    x1, x2, x3, e1, e2, e3,
    near, near_top, att_s, att_r, om_s, om_r, om_x, att_f,
    in_sem, halo_send, halo_recv, s1_send, s1_recv, l2_send, l2_recv, l3_send, l3_recv,
    kv_send, direct_send, kv_recv, q_send, q_recv, ret_send, ret_recv, a2a_send, a2a_recv, om_send, om_recv,
    chain_up, chain_down, late_in,
):
    s, g = lax.axis_index("seq"), lax.axis_index("head")
    last = lax.axis_size("seq") - 1
    z, x, y = lax.div(s, 8), lax.rem(lax.div(s, 4), 2), lax.rem(s, 4)
    ring = s - y
    zl = lax.rem(z, 4)
    bits = [lax.rem(z, 2), lax.rem(lax.div(z, 2), 2), lax.div(z, 4)]
    mirror = z * 8 + (1 - x) * 4
    early, late = z < 4, z >= 4

    def flipped(f):
        low, middle, high = [1 - bit if f >> i & 1 else bit for i, bit in enumerate(bits)]
        return high * 4 + middle * 2 + low

    def column(other):
        return other * 8 + x * 4

    loads = [
        pltpu.make_async_copy(k_hbm.at[0], kx.at[pl.ds(BLOCK, ROWS)], in_sem.at[0]),
        pltpu.make_async_copy(v_hbm.at[0], vx.at[pl.ds(BLOCK, ROWS)], in_sem.at[1]),
        pltpu.make_async_copy(q_hbm.at[0], q_s, in_sem.at[2]),
        pltpu.make_async_copy(w_hbm, w_s, in_sem.at[3]),
    ]
    for load in loads:
        load.start()

    barrier = pltpu.get_barrier_semaphore()

    def signal(semaphore, seq, head):
        pl.semaphore_signal(semaphore, inc=1, device_id=(seq, head), device_id_type=MESH)

    ring_start, ring_end = (y == 0) & (s > 0), (y == 3) & (s < last)

    @pl.when(early)
    def _():
        for other in range(4, 8):
            for j in range(4):
                signal(barrier, column(other) + j, g)

    @pl.when(ring_start)
    def _():
        signal(barrier, s - 1, g)

    @pl.when(ring_end)
    def _():
        signal(barrier, s + 1, g)

    for d in range(1, 4):
        signal(barrier, ring + lax.rem(y + d, 4), g)
        signal(barrier, s, lax.rem(g + d, 4))
    signal(barrier, mirror + y, g)

    @pl.when(zl < 3)
    def _():
        signal(barrier, s + 8, g)

    @pl.when(zl > 0)
    def _():
        signal(barrier, s - 8, g)

    low32 = iota((32, 128), 1) < HD

    pool4 = pooler(4)
    own_k, own_v = kx.at[pl.ds(BLOCK, ROWS)], vx.at[pl.ds(BLOCK, ROWS)]
    loads[0].wait()
    k4 = rounded(dot(pool4, own_k[...]) * 0.25)
    loads[1].wait()
    v4 = rounded(dot(pool4, own_v[...]) * 0.25)
    loads[2].wait()
    q4 = rounded(dot(pool4, q_s[...]) * 0.25)
    for h in range(HEADS_HERE):
        pair = slice(h // 2 * 128, h // 2 * 128 + 128)
        kp, vp, qp = k4[:, pair], v4[:, pair], q4[:, pair]
        if h % 2 == 0:
            packed = jnp.where(low32, kp, pltpu.roll(vp, HD, 1))
        else:
            packed = jnp.where(low32, pltpu.roll(kp, HD, 1), vp)
            qp = pltpu.roll(qp, HD, 1)
        s1[h, 0] = packed.astype(BF16)
        s1[h, 1] = jnp.where(low32, qp, 0.0).astype(BF16)
    my_rows = pl.ds(pl.multiple_of(y * 32, 32), 32)
    r1[:, my_rows, :] = s1[y]

    pl.semaphore_wait(
        barrier,
        7
        + jnp.where(late, 16, 0)
        + jnp.where(zl > 0, 1, 0)
        + jnp.where(zl < 3, 1, 0)
        + jnp.where(ring_start, 1, 0)
        + jnp.where(ring_end, 1, 0),
    )

    def remote(src, dst, send, recv, seq, head=None):
        return pltpu.make_async_remote_copy(
            src_ref=src, dst_ref=dst, send_sem=send, recv_sem=recv,
            device_id=(seq, g if head is None else head), device_id_type=MESH,
        )

    ring_copies = [
        remote(
            s1.at[lax.rem(y + d, 4)], r1.at[:, my_rows, :],
            s1_send.at[d - 1], s1_recv.at[d - 1], ring + lax.rem(y + d, 4),
        )
        for d in range(1, 4)
    ]
    head_rows, tail_rows = pl.ds(0, BLOCK), pl.ds(ROWS - BLOCK, BLOCK)
    to_left = [
        remote(k_hbm.at[0, head_rows], kx.at[pl.ds(BLOCK + ROWS, BLOCK)], halo_send.at[0], halo_recv.at[0], s - 1),
        remote(v_hbm.at[0, head_rows], vx.at[pl.ds(BLOCK + ROWS, BLOCK)], halo_send.at[1], halo_recv.at[1], s - 1),
    ]
    to_right = [
        remote(k_hbm.at[0, tail_rows], kx.at[pl.ds(0, BLOCK)], halo_send.at[2], halo_recv.at[2], s + 1),
        remote(v_hbm.at[0, tail_rows], vx.at[pl.ds(0, BLOCK)], halo_send.at[3], halo_recv.at[3], s + 1),
    ]
    for copy in ring_copies:
        copy.start()

    @pl.when(zl == 1)
    def _():
        signal(chain_up, s + 8, g)

    @pl.when(zl == 2)
    def _():
        signal(chain_down, s - 8, g)

    @pl.when(late)
    def _():
        for i in range(4):
            h = lax.rem(y + i, 4)
            for other in range(4):
                remote(
                    s1.at[h, 0], kv_all.at[z, my_rows, :], direct_send, kv_recv.at[z],
                    column(other) + h,
                ).start()
        for other in range(4):
            signal(late_in, column(other) + y, g)

    def pool_pair(level, scale):
        pool = pooler(level)
        return dot(pool, own_k[...]) * scale, dot(pool, own_v[...]) * scale

    kp, vp = pool_pair(3, 0.5**1.5)
    kv3_s[0], kv3_s[1] = kp.astype(BF16), vp.astype(BF16)
    kp, vp = pool_pair(2, 0.5)
    kv2_s[0], kv2_s[1] = kp.astype(BF16), vp.astype(BF16)

    slot3 = pl.ds(pl.multiple_of(lax.rem(y, 2) * 64, 64), 64)
    pair3 = ring + (1 - lax.div(y, 2)) * 2
    l3_copies = [
        remote(kv3_s, kv3_r.at[:, slot3, :], l3_send.at[j], l3_recv.at[lax.rem(y, 2)], pair3 + j)
        for j in range(2)
    ]
    l2_copy = remote(kv2_s, kv2_r, l2_send, l2_recv, s + 1 - 2 * lax.rem(y, 2))
    for copy in [*l3_copies, l2_copy]:
        copy.start()

    zeros = jnp.zeros((BLOCK, FEATURES), BF16)

    @pl.when(s == 0)
    def _():
        kx[0:BLOCK] = zeros
        vx[0:BLOCK] = zeros

    @pl.when(s == last)
    def _():
        kx[BLOCK + ROWS :] = zeros
        vx[BLOCK + ROWS :] = zeros

    lane_half = iota((1, 128), 1) < HD
    halves = [jnp.where(lane_half, 1.0, 0.0), jnp.where(lane_half, 0.0, 1.0)]

    def masked_queries(dst, field, count):
        for p in range(2):
            part = field[:, p * 128 : p * 128 + 128]
            for odd in range(2):
                dst[p, odd * count : (odd + 1) * count, :] = (part * halves[odd]).astype(BF16)

    for b in range(4):
        masked_queries(qn.at[b], q_s[b * BLOCK : (b + 1) * BLOCK, :].astype(F32), BLOCK)

    ones16 = jnp.ones((16, BLOCK), BF16)

    def turn(dst, block, column):
        turned = block.T
        for h in range(HEADS_HERE):
            dst[h, 0:HD, column : column + BLOCK] = turned[h * HD : (h + 1) * HD, :]
            dst[h, HD:SLAB, column : column + BLOCK] = ones16

    for b in range(1, 5):
        turn(vtn, vx[b * BLOCK : (b + 1) * BLOCK, :], b * BLOCK)

    def attend(keys, queries, values, count, exact, biases=None):
        scores = [dot_nt(key, queries) for key in keys]
        if biases:
            scores = [a if bias is None else a + bias for a, bias in zip(scores, biases)]
        top = jnp.max(scores[0], axis=0, keepdims=True)
        for part in scores[1:]:
            top = jnp.maximum(top, jnp.max(part, axis=0, keepdims=True))
        top = top * SCALE
        high = below = None
        if not exact:
            high, below = split_top(top)
            top = high + below
        weights = [jnp.exp2(part * SCALE - top).astype(BF16) for part in scores]
        weights = weights[0] if len(weights) == 1 else jnp.concatenate(weights, axis=0)
        results = [
            dot(values[odd], weights[:, odd * count : (odd + 1) * count]) for odd in range(2)
        ]
        return top, high, below, results

    def near_block(b):
        for p in range(2):
            lanes = slice(p * 128, p * 128 + 128)
            keys = [kx[(b + i) * BLOCK : (b + i + 1) * BLOCK, lanes] for i in range(3)]
            values = [vtn[2 * p + odd, :, b * BLOCK : (b + 3) * BLOCK] for odd in range(2)]
            biases = [None, None, None]
            if b == 0:
                biases[0] = jnp.where(s == 0, MASKED, 0.0)
            if b == 3:
                biases[2] = jnp.where(s == last, MASKED, 0.0)
            top, _, _, results = attend(keys, qn[b, p], values, BLOCK, True, biases)
            columns = slice(b * BLOCK, (b + 1) * BLOCK)
            for odd in range(2):
                h = 2 * p + odd
                near[h, :, columns] = results[odd]
                near_top[h : h + 1, columns] = top[:, odd * BLOCK : (odd + 1) * BLOCK]

    def small_rows(count, high, below, total):
        row = iota((16, count), 0)
        total_high = rounded(total)
        rows = jnp.where(row == 2, total_high, total - total_high)
        rows = jnp.where(row == 1, below, rows)
        return jnp.where(row == 0, high, rows)

    def sibling(dst, keys, queries, values, count, column):
        for p in range(2):
            lanes = slice(p * 128, p * 128 + 128)
            _, high, below, results = attend(
                [keys[:, lanes]], queries[p], [values(2 * p), values(2 * p + 1)], count, False
            )
            for odd in range(2):
                h = 2 * p + odd
                own = slice(odd * count, (odd + 1) * count)
                columns = slice(column, column + count)
                dst[h * SLAB : h * SLAB + HD, columns] = results[odd][0:HD].astype(BF16)
                dst[h * SLAB + HD : (h + 1) * SLAB, columns] = small_rows(
                    count, high[:, own], below[:, own], results[odd][HD : HD + 1]
                ).astype(BF16)

    @pl.when(s > 0)
    def _():
        for copy in to_left:
            copy.start()

    @pl.when(s < last)
    def _():
        for copy in to_right:
            copy.start()

    near_block(1)
    near_block(2)
    pooled_q = dot(pooler(1), q_s[...]) * 0.5**0.5
    for b in range(2):
        masked_queries(q1m.at[b], pooled_q[b * BLOCK : (b + 1) * BLOCK, :], BLOCK)
    masked_queries(q2m, dot(pooler(2), q_s[...]) * 0.5, BLOCK)
    masked_queries(q3m, dot(pooler(3), q_s[...]) * 0.5**1.5, 64)
    kp, vp = pool_pair(1, 0.5**0.5)
    k1[...] = kp.astype(BF16)
    v1[...] = vp.astype(BF16)
    for b in range(2):
        turn(vt1, v1[b * BLOCK : (b + 1) * BLOCK, :], b * BLOCK)
    for b in range(2):
        other = 1 - b
        sibling(
            x1, k1[other * BLOCK : (other + 1) * BLOCK, :], q1m.at[b],
            lambda h, other=other: vt1[h, :, other * BLOCK : (other + 1) * BLOCK], BLOCK, b * BLOCK,
        )
    e1[...] = selector(256, ROWS, 1)
    e2[...] = selector(128, ROWS, 2)
    e3[...] = selector(64, ROWS, 3)

    @pl.when(zl <= 1)
    def _():
        pl.semaphore_wait(chain_down, 1)

    @pl.when(zl >= 2)
    def _():
        pl.semaphore_wait(chain_up, 1)

    @pl.when(zl == 1)
    def _():
        signal(chain_down, s - 8, g)

    @pl.when(zl == 2)
    def _():
        signal(chain_up, s + 8, g)

    far_q = remote(r1.at[1], q_far, q_send, q_recv, mirror + y)
    for copy in ring_copies:
        copy.wait_recv()
    far_q.start()

    def forward(f):
        return remote(
            r1.at[0], kv_all.at[z], kv_send.at[f - 1], kv_recv.at[z], column(flipped(f)) + y
        )

    for f in range(1, 4):
        forward(f).start()

    a2a = []
    for d in range(1, 4):
        a2a += [
            remote(att_s.at[d - 1], att_r.at[g], a2a_send.at[d - 1], a2a_recv.at[d - 1], s, lax.rem(g + d, 4)),
            remote(om_s.at[d - 1], om_r.at[g], om_send.at[d - 1], om_recv.at[d - 1], s, lax.rem(g + d, 4)),
        ]

    def rest():
        @pl.when(s > 0)
        def _():
            for copy in to_right:
                copy.wait_recv()

        @pl.when(s < last)
        def _():
            for copy in to_left:
                copy.wait_recv()

        turn(vtn, vx[0:BLOCK, :], 0)
        near_block(0)

        turn(vtn, vx[BLOCK + ROWS :, :], BLOCK + ROWS)
        near_block(3)

        for d in (1, 2, 3, 0):
            target = lax.rem(g + d, 4)
            columns = pl.ds(pl.multiple_of(target * BLOCK, BLOCK), BLOCK)
            wide = [
                dot(field[...], select[:, columns])
                for field, select in ((x1, e1), (x2, e2), (x3, e3))
            ]
            mixes, logs = [], []
            for h in range(HEADS_HERE):
                terms = [part[h * SLAB : (h + 1) * SLAB] for part in wide]
                tops = [t[HD : HD + 1] + t[HD + 1 : HD + 2] for t in terms]
                sums = [t[HD + 2 : HD + 3] + t[HD + 3 : HD + 4] for t in terms]
                near_here = near[h, :, columns]
                tops.append(near_top[h : h + 1, columns])
                sums.append(near_here[HD : HD + 1])
                terms.append(near_here)
                top = tops[0]
                for other in tops[1:]:
                    top = jnp.maximum(top, other)
                total = jnp.zeros((1, BLOCK), F32)
                factors = [jnp.exp2(t - top) for t in tops]
                for factor, part in zip(factors, sums):
                    total = total + factor * part
                inverse = 1.0 / total
                mixed = jnp.zeros((HD, BLOCK), F32)
                for factor, part in zip(factors, terms):
                    mixed = mixed + part[0:HD] * (factor * inverse)
                mixes.append(mixed)
                logs.append(top + jnp.log2(total))
            mixed = jnp.concatenate(mixes, axis=0).T.astype(BF16)
            row = iota((8, BLOCK), 0)
            rows = jnp.zeros((8, BLOCK), F32)
            for h in range(HEADS_HERE):
                rows = jnp.where(row == h, logs[h], rows)
            if d:
                att_s[d - 1] = mixed
                om_s[d - 1] = rows
                for copy in a2a[2 * d - 2 : 2 * d]:
                    copy.start()
            else:
                att_r[g] = mixed
                om_r[g] = rows

    @pl.when(early)
    def _():
        pl.semaphore_wait(late_in, 4)
        for f in range(4, 8):
            forward(f).start()

    l2_copy.wait_recv()
    for j in range(2):
        remote(kv3_s, kv3_r.at[:, pl.ds(j * 64, 64), :], l3_send.at[j], l3_recv.at[j], pair3 + j).wait_recv()
    turn(vt2, kv2_r[1], 0)
    sibling(x2, kv2_r[0], q2m, lambda h: vt2[h], BLOCK, 0)

    turn(vt3, kv3_r[1], 0)
    sibling(x3, kv3_r[0], q3m, lambda h: vt3[h], 64, 0)
    @pl.when(z < 3)
    def _():
        rest()

    far_q.wait_recv()
    for f in range(1, 8):
        other = flipped(f)
        remote(
            kv_all.at[other], kv_all.at[other], kv_send.at[f - 1], kv_recv.at[other], column(other) + y
        ).wait_recv()
    queries = jnp.concatenate([r1[1], q_far[...]], axis=0)
    low128 = iota((128, 128), 1) < HD
    top = acc = None
    for f in (0, 1, 2, 3, 7, 6, 5, 4):
        block = kv_all[flipped(f)] if f else r1[0]
        scores = dot_nt(block, queries)
        turned = jnp.where(low128, 1.0, block.astype(F32)).T.astype(BF16)
        here = jnp.max(scores, axis=0, keepdims=True) * SCALE
        high = here if f == 0 else jnp.maximum(top, here)
        weights = jnp.exp2(scores * SCALE - high)
        if f == 0:
            weights = jnp.concatenate([weights[:, 0:128], weights[:, 128:256] * 2.0], axis=1)
        part = dot(turned, weights.astype(BF16))
        acc = part if f == 0 else acc * jnp.exp2(top - high) + part
        top = high
    sums = acc[0:HD]
    logs = top + jnp.log2(sums)
    means = acc[HD:] / sums
    odd_head = lax.rem(y, 2) == 1
    result = jnp.concatenate(
        [jnp.where(odd_head, logs, means), jnp.where(odd_head, means, logs)], axis=0
    )
    ret_s[...] = result.T
    head_here = g * 4 + y

    def give(slot, row, seq, head):
        remote(
            ret_s.at[pl.ds(pl.multiple_of(row, 8), 8), :], top_r.at[slot, head_here],
            ret_send.at[slot], ret_recv.at[slot], seq, head,
        ).start()

    for j in range(4):
        for t in range(4):
            give(1, 128 + j * 32 + t * 8, mirror + j, t)
    for dy in range(4):
        for dg in range(4):
            if dy or dg:
                there, t = lax.rem(y + dy, 4), lax.rem(g + dg, 4)
                give(0, there * 32 + t * 8, ring + there, t)
    top_r[0, head_here] = ret_s[pl.ds(pl.multiple_of(y * 32 + g * 8, 8), 8), :]

    @pl.when(z >= 3)
    def _():
        rest()

    for copy in a2a:
        copy.wait_recv()
    logs = om_r[...].reshape(32, BLOCK)
    high = rounded(logs)
    middle = rounded(logs - high)
    lowest = rounded(logs - high - middle)
    logs = jnp.concatenate([high, middle, lowest, jnp.zeros((32, BLOCK), F32)], axis=0)
    k, c = iota((128, 1024), 0), iota((128, 1024), 1)
    hit = ((k & 31) == ((c >> 8) * 8 + ((c >> 6) & 3))) & (k < 96)
    spread = jnp.where(hit, 1.0, 0.0).astype(BF16)
    om_x[...] = dot(logs.T.astype(BF16), spread)
    loads[3].wait()

    def arrived(slot, heads):
        remote(
            top_r.at[slot, pl.ds(0, heads)], top_r.at[slot, pl.ds(0, heads)],
            ret_send.at[slot], ret_recv.at[slot], mirror + y,
        ).wait_recv()

    arrived(0, 15)
    arrived(1, 16)
    low8 = iota((8, 128), 1) < HD
    for p in range(8):
        means, logs = [], []
        for slot in range(2):
            even, odd = top_r[slot, 2 * p], top_r[slot, 2 * p + 1]
            means.append(jnp.where(low8, even, odd))
            logs.append(pltpu.roll(jnp.where(low8, odd, even), HD, 1))
        top = jnp.maximum(logs[0], logs[1])
        factors = [jnp.exp2(t - top) for t in logs]
        total = factors[0] + factors[1]
        mean = (means[0] * factors[0] + means[1] * factors[1]) / total
        log = top + jnp.log2(total)
        lanes = slice(p * 128, p * 128 + 128)
        here = slice(p % 2 * 128, p % 2 * 128 + 128)
        for q in range(8):
            rows = slice(q * 16, q * 16 + 16)
            other = att_r[p // 2, rows, here].astype(F32)
            share = 1.0 / (1.0 + jnp.exp2(om_x[rows, lanes] - log[q : q + 1]))
            att_f[rows, lanes] = (other + (mean[q : q + 1] - other) * share).astype(BF16)
    o_ref[0] = dot(att_f[...], w_s[...]).astype(BF16)

    for copy in [*ring_copies, *l3_copies, l2_copy, far_q, *a2a]:
        copy.wait_send()
    for f in range(1, 4):
        forward(f).wait_send()

    @pl.when(early)
    def _():
        for f in range(4, 8):
            forward(f).wait_send()

    @pl.when(late)
    def _():
        remote(kv_all.at[0:4], kv_all.at[0:4], direct_send, kv_recv.at[z], mirror + y).wait_send()

    for slot, rows in ((0, 120), (1, 128)):
        remote(
            ret_s.at[pl.ds(0, rows)], ret_s.at[pl.ds(0, rows)],
            ret_send.at[slot], ret_recv.at[slot], mirror + y,
        ).wait_send()

    @pl.when(s > 0)
    def _():
        for copy in to_left:
            copy.wait_send()

    @pl.when(s < last)
    def _():
        for copy in to_right:
            copy.wait_send()


def per_device(queries, key_vectors, value_vectors, out_weight):
    def buf(*shape, dtype=BF16):
        return pltpu.VMEM(shape, dtype)

    dma = pltpu.SemaphoreType.DMA
    regular = pltpu.SemaphoreType.REGULAR
    scratch = [
        buf(ROWS, 256), buf(768, 256), buf(768, 256), buf(1024, 1024),
        buf(4, 2, 256, 128), buf(2, 2, 256, 128), buf(2, 256, 128), buf(2, 128, 128),
        buf(256, 256), buf(256, 256), buf(2, 128, 256), buf(2, 128, 256), buf(2, 64, 256), buf(2, 128, 256),
        buf(4, SLAB, 768), buf(4, SLAB, 256), buf(4, SLAB, 128), buf(4, SLAB, 128),
        buf(4, 2, 32, 128), buf(2, 128, 128), buf(8, 128, 128), buf(128, 128),
        buf(256, 128, dtype=F32), buf(2, 16, 8, 128, dtype=F32),
        buf(4 * SLAB, 256), buf(4 * SLAB, 128), buf(4 * SLAB, 64),
        buf(256, ROWS), buf(128, ROWS), buf(64, ROWS),
        buf(4, SLAB, ROWS, dtype=F32), buf(8, ROWS, dtype=F32), buf(3, 128, 256), buf(4, 128, 256),
        buf(3, 8, 128, dtype=F32), buf(4, 8, 128, dtype=F32), buf(128, 1024, dtype=F32), buf(128, 1024),
        dma((4,)), dma((4,)), dma((4,)), dma((3,)), dma((3,)), dma, dma, dma((2,)), dma((2,)),
        dma((7,)), dma, dma((8,)), dma, dma, dma((2,)), dma((2,)), dma((3,)), dma((3,)), dma((3,)), dma((3,)),
        regular, regular, regular,
    ]
    return pl.pallas_call(
        kernel,
        out_shape=pltpu.VMEM((1, BLOCK, 1024), BF16),
        in_specs=[pl.BlockSpec(memory_space=pl.ANY)] * 4,
        out_specs=pl.BlockSpec(memory_space=pltpu.VMEM),
        scratch_shapes=scratch,
        compiler_params=pltpu.CompilerParams(
            collective_id=0, has_side_effects=True, vmem_limit_bytes=58 * 2**20
        ),
    )(queries, key_vectors, value_vectors, out_weight)


def solution(mesh):
    return jax.shard_map(
        per_device,
        mesh=mesh,
        in_specs=(P(None, "seq", "head"), P(None, "seq", "head"), P(None, "seq", "head"), P()),
        out_specs=P(None, ("seq", "head"), None),
        check_vma=False,
    )
```

```python
import math

import jax
import jax.numpy as jnp
from jax import lax
from jax.experimental import pallas as pl
from jax.experimental.pallas import tpu as pltpu
from jax.sharding import PartitionSpec as P

HD = 64
BLOCK = 128
HEADS_HERE = 4
ROWS = 512
FEATURES = HEADS_HERE * HD
SLAB = HD + 16
SCALE = HD**-0.5 * math.log2(math.e)
MASKED = -1e30
BF16, F32 = jnp.bfloat16, jnp.float32
MESH = pl.DeviceIdType.MESH


def iota(shape, axis):
    return lax.broadcasted_iota(jnp.int32, shape, axis)


def dot(a, b):
    return jnp.dot(a, b, preferred_element_type=F32)


def dot_nt(a, b):
    return lax.dot_general(a, b, (((1,), (1,)), ((), ())), preferred_element_type=F32)


def rounded(value):
    return value.astype(BF16).astype(F32)


def split_top(top):
    high = rounded(top)
    return high, rounded(top - high)


def selector(rows, columns, shift, offset=0):
    hit = iota((rows, columns), 0) == offset + (iota((rows, columns), 1) >> shift)
    return jnp.where(hit, 1.0, 0.0).astype(BF16)


def pooler(level):
    rows = ROWS >> level
    hit = iota((rows, ROWS), 0) == (iota((rows, ROWS), 1) >> level)
    return jnp.where(hit, 1.0, 0.0).astype(BF16)


def kernel(
    q_hbm, k_hbm, v_hbm, w_hbm, o_ref,
    q_s, kx, vx, w_s,
    qn, q1m, q2m, q3m,
    k1, v1, kv2_s, kv2_r, kv3_s, kv3_r,
    vtn, vt1, vt2, vt3,
    s1, r1, kv_all, q_far, ret_s, top_r,
    x1, x2, x3, e1, e2, e3,
    near, near_top, att_s, att_r, om_s, om_r, om_x, att_f,
    in_sem, halo_send, halo_recv, s1_send, s1_recv, l2_send, l2_recv, l3_send, l3_recv,
    kv_send, direct_send, kv_recv, q_send, q_recv, ret_send, ret_recv, a2a_send, a2a_recv, om_send, om_recv,
    chain_up, chain_down, late_in,
):
    s, g = lax.axis_index("seq"), lax.axis_index("head")
    last = lax.axis_size("seq") - 1
    z, x, y = lax.div(s, 8), lax.rem(lax.div(s, 4), 2), lax.rem(s, 4)
    ring = s - y
    zl = lax.rem(z, 4)
    bits = [lax.rem(z, 2), lax.rem(lax.div(z, 2), 2), lax.div(z, 4)]
    mirror = z * 8 + (1 - x) * 4
    early, late = z < 4, z >= 4

    def flipped(f):
        low, middle, high = [1 - bit if f >> i & 1 else bit for i, bit in enumerate(bits)]
        return high * 4 + middle * 2 + low

    def column(other):
        return other * 8 + x * 4

    loads = [
        pltpu.make_async_copy(k_hbm.at[0], kx.at[pl.ds(BLOCK, ROWS)], in_sem.at[0]),
        pltpu.make_async_copy(v_hbm.at[0], vx.at[pl.ds(BLOCK, ROWS)], in_sem.at[1]),
        pltpu.make_async_copy(q_hbm.at[0], q_s, in_sem.at[2]),
        pltpu.make_async_copy(w_hbm, w_s, in_sem.at[3]),
    ]
    for load in loads:
        load.start()

    barrier = pltpu.get_barrier_semaphore()

    def signal(semaphore, seq, head):
        pl.semaphore_signal(semaphore, inc=1, device_id=(seq, head), device_id_type=MESH)

    ring_start, ring_end = (y == 0) & (s > 0), (y == 3) & (s < last)

    @pl.when(early)
    def _():
        for other in range(4, 8):
            for j in range(4):
                signal(barrier, column(other) + j, g)

    @pl.when(ring_start)
    def _():
        signal(barrier, s - 1, g)

    @pl.when(ring_end)
    def _():
        signal(barrier, s + 1, g)

    for d in range(1, 4):
        signal(barrier, ring + lax.rem(y + d, 4), g)
        signal(barrier, s, lax.rem(g + d, 4))
    signal(barrier, mirror + y, g)

    @pl.when(zl < 3)
    def _():
        signal(barrier, s + 8, g)

    @pl.when(zl > 0)
    def _():
        signal(barrier, s - 8, g)

    low32 = iota((32, 128), 1) < HD

    pool4 = pooler(4)
    own_k, own_v = kx.at[pl.ds(BLOCK, ROWS)], vx.at[pl.ds(BLOCK, ROWS)]
    loads[0].wait()
    k4 = rounded(dot(pool4, own_k[...]) * 0.25)
    loads[1].wait()
    v4 = rounded(dot(pool4, own_v[...]) * 0.25)
    loads[2].wait()
    q4 = rounded(dot(pool4, q_s[...]) * 0.25)
    for h in range(HEADS_HERE):
        pair = slice(h // 2 * 128, h // 2 * 128 + 128)
        kp, vp, qp = k4[:, pair], v4[:, pair], q4[:, pair]
        if h % 2 == 0:
            packed = jnp.where(low32, kp, pltpu.roll(vp, HD, 1))
        else:
            packed = jnp.where(low32, pltpu.roll(kp, HD, 1), vp)
            qp = pltpu.roll(qp, HD, 1)
        s1[h, 0] = packed.astype(BF16)
        s1[h, 1] = jnp.where(low32, qp, 0.0).astype(BF16)
    my_rows = pl.ds(pl.multiple_of(y * 32, 32), 32)
    r1[:, my_rows, :] = s1[y]

    pl.semaphore_wait(
        barrier,
        7
        + jnp.where(late, 16, 0)
        + jnp.where(zl > 0, 1, 0)
        + jnp.where(zl < 3, 1, 0)
        + jnp.where(ring_start, 1, 0)
        + jnp.where(ring_end, 1, 0),
    )

    def remote(src, dst, send, recv, seq, head=None):
        return pltpu.make_async_remote_copy(
            src_ref=src, dst_ref=dst, send_sem=send, recv_sem=recv,
            device_id=(seq, g if head is None else head), device_id_type=MESH,
        )

    ring_copies = [
        remote(
            s1.at[lax.rem(y + d, 4)], r1.at[:, my_rows, :],
            s1_send.at[d - 1], s1_recv.at[d - 1], ring + lax.rem(y + d, 4),
        )
        for d in range(1, 4)
    ]
    head_rows, tail_rows = pl.ds(0, BLOCK), pl.ds(ROWS - BLOCK, BLOCK)
    to_left = [
        remote(k_hbm.at[0, head_rows], kx.at[pl.ds(BLOCK + ROWS, BLOCK)], halo_send.at[0], halo_recv.at[0], s - 1),
        remote(v_hbm.at[0, head_rows], vx.at[pl.ds(BLOCK + ROWS, BLOCK)], halo_send.at[1], halo_recv.at[1], s - 1),
    ]
    to_right = [
        remote(k_hbm.at[0, tail_rows], kx.at[pl.ds(0, BLOCK)], halo_send.at[2], halo_recv.at[2], s + 1),
        remote(v_hbm.at[0, tail_rows], vx.at[pl.ds(0, BLOCK)], halo_send.at[3], halo_recv.at[3], s + 1),
    ]
    for copy in ring_copies:
        copy.start()

    @pl.when(zl == 1)
    def _():
        signal(chain_up, s + 8, g)

    @pl.when(zl == 2)
    def _():
        signal(chain_down, s - 8, g)

    @pl.when(late)
    def _():
        for i in range(4):
            h = lax.rem(y + i, 4)
            for other in range(4):
                remote(
                    s1.at[h, 0], kv_all.at[z, my_rows, :], direct_send, kv_recv.at[z],
                    column(other) + h,
                ).start()
        for other in range(4):
            signal(late_in, column(other) + y, g)

    def pool_pair(level, scale):
        pool = pooler(level)
        return dot(pool, own_k[...]) * scale, dot(pool, own_v[...]) * scale

    kp, vp = pool_pair(3, 0.5**1.5)
    kv3_s[0], kv3_s[1] = kp.astype(BF16), vp.astype(BF16)
    kp, vp = pool_pair(2, 0.5)
    kv2_s[0], kv2_s[1] = kp.astype(BF16), vp.astype(BF16)

    slot3 = pl.ds(pl.multiple_of(lax.rem(y, 2) * 64, 64), 64)
    pair3 = ring + (1 - lax.div(y, 2)) * 2
    l3_copies = [
        remote(kv3_s, kv3_r.at[:, slot3, :], l3_send.at[j], l3_recv.at[lax.rem(y, 2)], pair3 + j)
        for j in range(2)
    ]
    l2_copy = remote(kv2_s, kv2_r, l2_send, l2_recv, s + 1 - 2 * lax.rem(y, 2))
    for copy in [*l3_copies, l2_copy]:
        copy.start()

    zeros = jnp.zeros((BLOCK, FEATURES), BF16)

    @pl.when(s == 0)
    def _():
        kx[0:BLOCK] = zeros
        vx[0:BLOCK] = zeros

    @pl.when(s == last)
    def _():
        kx[BLOCK + ROWS :] = zeros
        vx[BLOCK + ROWS :] = zeros

    lane_half = iota((1, 128), 1) < HD
    halves = [jnp.where(lane_half, 1.0, 0.0), jnp.where(lane_half, 0.0, 1.0)]

    def masked_queries(dst, field, count):
        for p in range(2):
            part = field[:, p * 128 : p * 128 + 128]
            for odd in range(2):
                dst[p, odd * count : (odd + 1) * count, :] = (part * halves[odd]).astype(BF16)

    for b in range(4):
        masked_queries(qn.at[b], q_s[b * BLOCK : (b + 1) * BLOCK, :].astype(F32), BLOCK)

    ones16 = jnp.ones((16, BLOCK), BF16)

    def turn(dst, block, column):
        turned = block.T
        for h in range(HEADS_HERE):
            dst[h, 0:HD, column : column + BLOCK] = turned[h * HD : (h + 1) * HD, :]
            dst[h, HD:SLAB, column : column + BLOCK] = ones16

    for b in range(1, 5):
        turn(vtn, vx[b * BLOCK : (b + 1) * BLOCK, :], b * BLOCK)

    def attend(keys, queries, values, count, exact, biases=None):
        scores = [dot_nt(key, queries) for key in keys]
        if biases:
            scores = [a if bias is None else a + bias for a, bias in zip(scores, biases)]
        top = jnp.max(scores[0], axis=0, keepdims=True)
        for part in scores[1:]:
            top = jnp.maximum(top, jnp.max(part, axis=0, keepdims=True))
        top = top * SCALE
        high = below = None
        if not exact:
            high, below = split_top(top)
            top = high + below
        weights = [jnp.exp2(part * SCALE - top).astype(BF16) for part in scores]
        weights = weights[0] if len(weights) == 1 else jnp.concatenate(weights, axis=0)
        results = [
            dot(values[odd], weights[:, odd * count : (odd + 1) * count]) for odd in range(2)
        ]
        return top, high, below, results

    def near_block(b):
        for p in range(2):
            lanes = slice(p * 128, p * 128 + 128)
            keys = [kx[(b + i) * BLOCK : (b + i + 1) * BLOCK, lanes] for i in range(3)]
            values = [vtn[2 * p + odd, :, b * BLOCK : (b + 3) * BLOCK] for odd in range(2)]
            biases = [None, None, None]
            if b == 0:
                biases[0] = jnp.where(s == 0, MASKED, 0.0)
            if b == 3:
                biases[2] = jnp.where(s == last, MASKED, 0.0)
            top, _, _, results = attend(keys, qn[b, p], values, BLOCK, True, biases)
            columns = slice(b * BLOCK, (b + 1) * BLOCK)
            for odd in range(2):
                h = 2 * p + odd
                near[h, :, columns] = results[odd]
                near_top[h : h + 1, columns] = top[:, odd * BLOCK : (odd + 1) * BLOCK]

    def small_rows(count, high, below, total):
        row = iota((16, count), 0)
        total_high = rounded(total)
        rows = jnp.where(row == 2, total_high, total - total_high)
        rows = jnp.where(row == 1, below, rows)
        return jnp.where(row == 0, high, rows)

    def sibling(dst, keys, queries, values, count, column):
        for p in range(2):
            lanes = slice(p * 128, p * 128 + 128)
            _, high, below, results = attend(
                [keys[:, lanes]], queries[p], [values(2 * p), values(2 * p + 1)], count, False
            )
            for odd in range(2):
                h = 2 * p + odd
                own = slice(odd * count, (odd + 1) * count)
                columns = slice(column, column + count)
                dst[h * SLAB : h * SLAB + HD, columns] = results[odd][0:HD].astype(BF16)
                dst[h * SLAB + HD : (h + 1) * SLAB, columns] = small_rows(
                    count, high[:, own], below[:, own], results[odd][HD : HD + 1]
                ).astype(BF16)

    calm = (z < 3) | (z > 3)

    @pl.when((s > 0) & (calm | (y > 0)))
    def _():
        for copy in to_left:
            copy.start()

    @pl.when((s < last) & (calm | (y < 3)))
    def _():
        for copy in to_right:
            copy.start()

    near_block(1)
    near_block(2)
    pooled_q = dot(pooler(1), q_s[...]) * 0.5**0.5
    for b in range(2):
        masked_queries(q1m.at[b], pooled_q[b * BLOCK : (b + 1) * BLOCK, :], BLOCK)
    masked_queries(q2m, dot(pooler(2), q_s[...]) * 0.5, BLOCK)
    masked_queries(q3m, dot(pooler(3), q_s[...]) * 0.5**1.5, 64)
    kp, vp = pool_pair(1, 0.5**0.5)
    k1[...] = kp.astype(BF16)
    v1[...] = vp.astype(BF16)
    for b in range(2):
        turn(vt1, v1[b * BLOCK : (b + 1) * BLOCK, :], b * BLOCK)
    for b in range(2):
        other = 1 - b
        sibling(
            x1, k1[other * BLOCK : (other + 1) * BLOCK, :], q1m.at[b],
            lambda h, other=other: vt1[h, :, other * BLOCK : (other + 1) * BLOCK], BLOCK, b * BLOCK,
        )
    e1[...] = selector(256, ROWS, 1)
    e2[...] = selector(128, ROWS, 2)
    e3[...] = selector(64, ROWS, 3)

    @pl.when(zl <= 1)
    def _():
        pl.semaphore_wait(chain_down, 1)

    @pl.when(zl >= 2)
    def _():
        pl.semaphore_wait(chain_up, 1)

    @pl.when(zl == 1)
    def _():
        signal(chain_down, s - 8, g)

    @pl.when(zl == 2)
    def _():
        signal(chain_up, s + 8, g)

    far_q = remote(r1.at[1], q_far, q_send, q_recv, mirror + y)
    for copy in ring_copies:
        copy.wait_recv()
    far_q.start()

    def forward(f):
        return remote(
            r1.at[0], kv_all.at[z], kv_send.at[f - 1], kv_recv.at[z], column(flipped(f)) + y
        )

    for f in range(1, 4):
        forward(f).start()

    @pl.when(ring_start & (z == 3))
    def _():
        for copy in to_left:
            copy.start()

    @pl.when(ring_end & (z == 3))
    def _():
        for copy in to_right:
            copy.start()

    @pl.when(early)
    def _():
        pl.semaphore_wait(late_in, 4)
        for f in range(4, 8):
            forward(f).start()

    l2_copy.wait_recv()
    for j in range(2):
        remote(kv3_s, kv3_r.at[:, pl.ds(j * 64, 64), :], l3_send.at[j], l3_recv.at[j], pair3 + j).wait_recv()
    turn(vt2, kv2_r[1], 0)
    sibling(x2, kv2_r[0], q2m, lambda h: vt2[h], BLOCK, 0)

    turn(vt3, kv3_r[1], 0)
    sibling(x3, kv3_r[0], q3m, lambda h: vt3[h], 64, 0)
    def a2a(block, owner):
        return [
            remote(att_s.at[block], att_r.at[owner], a2a_send.at[block], a2a_recv.at[owner], s, block),
            remote(om_s.at[block], om_r.at[owner], om_send.at[block], om_recv.at[owner], s, block),
        ]

    def combine(blocks):
        for block in blocks:
            columns = slice(block * BLOCK, (block + 1) * BLOCK)
            wide = [
                dot(field[...], select[:, columns])
                for field, select in ((x1, e1), (x2, e2), (x3, e3))
            ]
            mixes, logs = [], []
            for h in range(HEADS_HERE):
                terms = [part[h * SLAB : (h + 1) * SLAB] for part in wide]
                tops = [t[HD : HD + 1] + t[HD + 1 : HD + 2] for t in terms]
                sums = [t[HD + 2 : HD + 3] + t[HD + 3 : HD + 4] for t in terms]
                near_here = near[h, :, columns]
                tops.append(near_top[h : h + 1, columns])
                sums.append(near_here[HD : HD + 1])
                terms.append(near_here)
                top = tops[0]
                for other in tops[1:]:
                    top = jnp.maximum(top, other)
                total = jnp.zeros((1, BLOCK), F32)
                factors = [jnp.exp2(t - top) for t in tops]
                for factor, part in zip(factors, sums):
                    total = total + factor * part
                inverse = 1.0 / total
                mixed = jnp.zeros((HD, BLOCK), F32)
                for factor, part in zip(factors, terms):
                    mixed = mixed + part[0:HD] * (factor * inverse)
                mixes.append(mixed)
                logs.append(top + jnp.log2(total))
            mixed = jnp.concatenate(mixes, axis=0).T.astype(BF16)
            row = iota((8, BLOCK), 0)
            rows = jnp.zeros((8, BLOCK), F32)
            for h in range(HEADS_HERE):
                rows = jnp.where(row == h, logs[h], rows)
            att_s[block] = mixed
            om_s[block] = rows
        for block in blocks:

            @pl.when(g == block)
            def _(block=block):
                att_r[g] = att_s[block]
                om_r[g] = om_s[block]

            @pl.when(g != block)
            def _(block=block):
                for copy in a2a(block, g):
                    copy.start()

    combine((1, 2))

    def rest():
        @pl.when(s > 0)
        def _():
            for copy in to_right:
                copy.wait_recv()

        @pl.when(s < last)
        def _():
            for copy in to_left:
                copy.wait_recv()

        turn(vtn, vx[0:BLOCK, :], 0)
        near_block(0)

        turn(vtn, vx[BLOCK + ROWS :, :], BLOCK + ROWS)
        near_block(3)
        combine((0, 3))

    @pl.when(z < 2)
    def _():
        rest()

    far_q.wait_recv()
    for f in range(1, 8):
        other = flipped(f)
        remote(
            kv_all.at[other], kv_all.at[other], kv_send.at[f - 1], kv_recv.at[other], column(other) + y
        ).wait_recv()
    queries = jnp.concatenate([r1[1], q_far[...]], axis=0)
    low128 = iota((128, 128), 1) < HD
    top = acc = None
    for f in (0, 1, 2, 3, 7, 6, 5, 4):
        block = kv_all[flipped(f)] if f else r1[0]
        scores = dot_nt(block, queries)
        turned = jnp.where(low128, 1.0, block.astype(F32)).T.astype(BF16)
        here = jnp.max(scores, axis=0, keepdims=True) * SCALE
        high = here if f == 0 else jnp.maximum(top, here)
        weights = jnp.exp2(scores * SCALE - high)
        if f == 0:
            weights = jnp.concatenate([weights[:, 0:128], weights[:, 128:256] * 2.0], axis=1)
        part = dot(turned, weights.astype(BF16))
        acc = part if f == 0 else acc * jnp.exp2(top - high) + part
        top = high
    sums = acc[0:HD]
    logs = top + jnp.log2(sums)
    means = acc[HD:] / sums
    odd_head = lax.rem(y, 2) == 1
    result = jnp.concatenate(
        [jnp.where(odd_head, logs, means), jnp.where(odd_head, means, logs)], axis=0
    )
    ret_s[...] = result.T
    head_here = g * 4 + y

    def give(slot, row, seq, head):
        remote(
            ret_s.at[pl.ds(pl.multiple_of(row, 8), 8), :], top_r.at[slot, head_here],
            ret_send.at[slot], ret_recv.at[slot], seq, head,
        ).start()

    for j in range(4):
        for t in range(4):
            give(1, 128 + j * 32 + t * 8, mirror + j, t)
    for dy in range(4):
        for dg in range(4):
            if dy or dg:
                there, t = lax.rem(y + dy, 4), lax.rem(g + dg, 4)
                give(0, there * 32 + t * 8, ring + there, t)
    top_r[0, head_here] = ret_s[pl.ds(pl.multiple_of(y * 32 + g * 8, 8), 8), :]

    @pl.when(z >= 2)
    def _():
        rest()

    for d in range(1, 4):
        for copy in a2a(0, lax.rem(g + d, 4)):
            copy.wait_recv()
    logs = om_r[...].reshape(32, BLOCK)
    high = rounded(logs)
    middle = rounded(logs - high)
    lowest = rounded(logs - high - middle)
    logs = jnp.concatenate([high, middle, lowest, jnp.zeros((32, BLOCK), F32)], axis=0)
    k, c = iota((128, 1024), 0), iota((128, 1024), 1)
    hit = ((k & 31) == ((c >> 8) * 8 + ((c >> 6) & 3))) & (k < 96)
    spread = jnp.where(hit, 1.0, 0.0).astype(BF16)
    om_x[...] = dot(logs.T.astype(BF16), spread)
    loads[3].wait()

    def arrived(slot, heads):
        remote(
            top_r.at[slot, pl.ds(0, heads)], top_r.at[slot, pl.ds(0, heads)],
            ret_send.at[slot], ret_recv.at[slot], mirror + y,
        ).wait_recv()

    arrived(0, 15)
    arrived(1, 16)
    low8 = iota((8, 128), 1) < HD
    for p in range(8):
        means, logs = [], []
        for slot in range(2):
            even, odd = top_r[slot, 2 * p], top_r[slot, 2 * p + 1]
            means.append(jnp.where(low8, even, odd))
            logs.append(pltpu.roll(jnp.where(low8, odd, even), HD, 1))
        top = jnp.maximum(logs[0], logs[1])
        factors = [jnp.exp2(t - top) for t in logs]
        total = factors[0] + factors[1]
        mean = (means[0] * factors[0] + means[1] * factors[1]) / total
        log = top + jnp.log2(total)
        lanes = slice(p * 128, p * 128 + 128)
        here = slice(p % 2 * 128, p % 2 * 128 + 128)
        for q in range(8):
            rows = slice(q * 16, q * 16 + 16)
            other = att_r[p // 2, rows, here].astype(F32)
            share = 1.0 / (1.0 + jnp.exp2(om_x[rows, lanes] - log[q : q + 1]))
            att_f[rows, lanes] = (other + (mean[q : q + 1] - other) * share).astype(BF16)
    o_ref[0] = dot(att_f[...], w_s[...]).astype(BF16)

    for copy in [*ring_copies, *l3_copies, l2_copy, far_q]:
        copy.wait_send()
    for block in range(4):

        @pl.when(g != block)
        def _(block=block):
            for copy in a2a(block, g):
                copy.wait_send()

    for f in range(1, 4):
        forward(f).wait_send()

    @pl.when(early)
    def _():
        for f in range(4, 8):
            forward(f).wait_send()

    @pl.when(late)
    def _():
        remote(kv_all.at[0:4], kv_all.at[0:4], direct_send, kv_recv.at[z], mirror + y).wait_send()

    for slot, rows in ((0, 120), (1, 128)):
        remote(
            ret_s.at[pl.ds(0, rows)], ret_s.at[pl.ds(0, rows)],
            ret_send.at[slot], ret_recv.at[slot], mirror + y,
        ).wait_send()

    @pl.when(s > 0)
    def _():
        for copy in to_left:
            copy.wait_send()

    @pl.when(s < last)
    def _():
        for copy in to_right:
            copy.wait_send()


def per_device(queries, key_vectors, value_vectors, out_weight):
    def buf(*shape, dtype=BF16):
        return pltpu.VMEM(shape, dtype)

    dma = pltpu.SemaphoreType.DMA
    regular = pltpu.SemaphoreType.REGULAR
    scratch = [
        buf(ROWS, 256), buf(768, 256), buf(768, 256), buf(1024, 1024),
        buf(4, 2, 256, 128), buf(2, 2, 256, 128), buf(2, 256, 128), buf(2, 128, 128),
        buf(256, 256), buf(256, 256), buf(2, 128, 256), buf(2, 128, 256), buf(2, 64, 256), buf(2, 128, 256),
        buf(4, SLAB, 768), buf(4, SLAB, 256), buf(4, SLAB, 128), buf(4, SLAB, 128),
        buf(4, 2, 32, 128), buf(2, 128, 128), buf(8, 128, 128), buf(128, 128),
        buf(256, 128, dtype=F32), buf(2, 16, 8, 128, dtype=F32),
        buf(4 * SLAB, 256), buf(4 * SLAB, 128), buf(4 * SLAB, 64),
        buf(256, ROWS), buf(128, ROWS), buf(64, ROWS),
        buf(4, SLAB, ROWS, dtype=F32), buf(8, ROWS, dtype=F32), buf(4, 128, 256), buf(4, 128, 256),
        buf(4, 8, 128, dtype=F32), buf(4, 8, 128, dtype=F32), buf(128, 1024, dtype=F32), buf(128, 1024),
        dma((4,)), dma((4,)), dma((4,)), dma((3,)), dma((3,)), dma, dma, dma((2,)), dma((2,)),
        dma((7,)), dma, dma((8,)), dma, dma, dma((2,)), dma((2,)), dma((4,)), dma((4,)), dma((4,)), dma((4,)),
        regular, regular, regular,
    ]
    return pl.pallas_call(
        kernel,
        out_shape=pltpu.VMEM((1, BLOCK, 1024), BF16),
        in_specs=[pl.BlockSpec(memory_space=pl.ANY)] * 4,
        out_specs=pl.BlockSpec(memory_space=pltpu.VMEM),
        scratch_shapes=scratch,
        compiler_params=pltpu.CompilerParams(
            collective_id=0, has_side_effects=True, vmem_limit_bytes=58 * 2**20
        ),
    )(queries, key_vectors, value_vectors, out_weight)


def solution(mesh):
    return jax.shard_map(
        per_device,
        mesh=mesh,
        in_specs=(P(None, "seq", "head"), P(None, "seq", "head"), P(None, "seq", "head"), P()),
        out_specs=P(None, ("seq", "head"), None),
        check_vma=False,
    )
```

```python
import math

import jax
import jax.numpy as jnp
from jax import lax
from jax.experimental import pallas as pl
from jax.experimental.pallas import tpu as pltpu
from jax.sharding import PartitionSpec as P

HD = 64
BLOCK = 128
HEADS_HERE = 4
ROWS = 512
FEATURES = HEADS_HERE * HD
SLAB = HD + 16
SCALE = HD**-0.5 * math.log2(math.e)
MASKED = -1e30
BF16, F32 = jnp.bfloat16, jnp.float32
MESH = pl.DeviceIdType.MESH


def iota(shape, axis):
    return lax.broadcasted_iota(jnp.int32, shape, axis)


def dot(a, b):
    return jnp.dot(a, b, preferred_element_type=F32)


def dot_nt(a, b):
    return lax.dot_general(a, b, (((1,), (1,)), ((), ())), preferred_element_type=F32)


def rounded(value):
    return value.astype(BF16).astype(F32)


def split_top(top):
    high = rounded(top)
    return high, rounded(top - high)


def selector(rows, columns, shift, offset=0):
    hit = iota((rows, columns), 0) == offset + (iota((rows, columns), 1) >> shift)
    return jnp.where(hit, 1.0, 0.0).astype(BF16)


def pooler(level):
    rows = ROWS >> level
    hit = iota((rows, ROWS), 0) == (iota((rows, ROWS), 1) >> level)
    return jnp.where(hit, 1.0, 0.0).astype(BF16)


def kernel(
    q_hbm, k_hbm, v_hbm, w_hbm, o_ref,
    q_s, kx, vx, w_s,
    qn, q1m, q2m, q3m,
    k1, v1, kv2_s, kv2_r, kv3_s, kv3_r,
    vtn, vt1, vt2, vt3,
    s1, r1, kv_all, q_far, ret_s, top_r,
    x1, x2, x3, e1, e2, e3,
    near, near_top, att_s, att_r, om_s, om_r, om_x, att_f,
    in_sem, halo_send, halo_recv, s1_send, s1_recv, l2_send, l2_recv, l3_send, l3_recv,
    kv_send, direct_send, kv_recv, q_send, q_recv, ret_send, ret_recv, a2a_send, a2a_recv, om_send, om_recv,
    chain_up, chain_down, late_in,
):
    s, g = lax.axis_index("seq"), lax.axis_index("head")
    last = lax.axis_size("seq") - 1
    z, x, y = lax.div(s, 8), lax.rem(lax.div(s, 4), 2), lax.rem(s, 4)
    ring = s - y
    zl = lax.rem(z, 4)
    bits = [lax.rem(z, 2), lax.rem(lax.div(z, 2), 2), lax.div(z, 4)]
    mirror = z * 8 + (1 - x) * 4
    early, late = z < 4, z >= 4

    def flipped(f):
        low, middle, high = [1 - bit if f >> i & 1 else bit for i, bit in enumerate(bits)]
        return high * 4 + middle * 2 + low

    def column(other):
        return other * 8 + x * 4

    loads = [
        pltpu.make_async_copy(k_hbm.at[0], kx.at[pl.ds(BLOCK, ROWS)], in_sem.at[0]),
        pltpu.make_async_copy(v_hbm.at[0], vx.at[pl.ds(BLOCK, ROWS)], in_sem.at[1]),
        pltpu.make_async_copy(q_hbm.at[0], q_s, in_sem.at[2]),
        pltpu.make_async_copy(w_hbm, w_s, in_sem.at[3]),
    ]
    for load in loads:
        load.start()

    barrier = pltpu.get_barrier_semaphore()

    def signal(semaphore, seq, head):
        pl.semaphore_signal(semaphore, inc=1, device_id=(seq, head), device_id_type=MESH)

    ring_start, ring_end = (y == 0) & (s > 0), (y == 3) & (s < last)

    @pl.when(early)
    def _():
        for other in range(4, 8):
            for j in range(4):
                signal(barrier, column(other) + j, g)

    @pl.when(ring_start)
    def _():
        signal(barrier, s - 1, g)

    @pl.when(ring_end)
    def _():
        signal(barrier, s + 1, g)

    for d in range(1, 4):
        signal(barrier, ring + lax.rem(y + d, 4), g)
        signal(barrier, s, lax.rem(g + d, 4))
    signal(barrier, mirror + y, g)

    @pl.when(zl < 3)
    def _():
        signal(barrier, s + 8, g)

    @pl.when(zl > 0)
    def _():
        signal(barrier, s - 8, g)

    low32 = iota((32, 128), 1) < HD

    pool4 = pooler(4)
    own_k, own_v = kx.at[pl.ds(BLOCK, ROWS)], vx.at[pl.ds(BLOCK, ROWS)]
    loads[0].wait()
    k4 = rounded(dot(pool4, own_k[...]) * 0.25)
    loads[1].wait()
    v4 = rounded(dot(pool4, own_v[...]) * 0.25)
    loads[2].wait()
    q4 = rounded(dot(pool4, q_s[...]) * 0.25)
    for h in range(HEADS_HERE):
        pair = slice(h // 2 * 128, h // 2 * 128 + 128)
        kp, vp, qp = k4[:, pair], v4[:, pair], q4[:, pair]
        if h % 2 == 0:
            packed = jnp.where(low32, kp, pltpu.roll(vp, HD, 1))
        else:
            packed = jnp.where(low32, pltpu.roll(kp, HD, 1), vp)
            qp = pltpu.roll(qp, HD, 1)
        s1[h, 0] = packed.astype(BF16)
        s1[h, 1] = jnp.where(low32, qp, 0.0).astype(BF16)
    my_rows = pl.ds(pl.multiple_of(y * 32, 32), 32)
    r1[:, my_rows, :] = s1[y]

    pl.semaphore_wait(
        barrier,
        7
        + jnp.where(late, 16, 0)
        + jnp.where(zl > 0, 1, 0)
        + jnp.where(zl < 3, 1, 0)
        + jnp.where(ring_start, 1, 0)
        + jnp.where(ring_end, 1, 0),
    )

    def remote(src, dst, send, recv, seq, head=None):
        return pltpu.make_async_remote_copy(
            src_ref=src, dst_ref=dst, send_sem=send, recv_sem=recv,
            device_id=(seq, g if head is None else head), device_id_type=MESH,
        )

    ring_copies = [
        remote(
            s1.at[lax.rem(y + d, 4)], r1.at[:, my_rows, :],
            s1_send.at[d - 1], s1_recv.at[d - 1], ring + lax.rem(y + d, 4),
        )
        for d in range(1, 4)
    ]
    head_rows, tail_rows = pl.ds(0, BLOCK), pl.ds(ROWS - BLOCK, BLOCK)
    to_left = [
        remote(k_hbm.at[0, head_rows], kx.at[pl.ds(BLOCK + ROWS, BLOCK)], halo_send.at[0], halo_recv.at[0], s - 1),
        remote(v_hbm.at[0, head_rows], vx.at[pl.ds(BLOCK + ROWS, BLOCK)], halo_send.at[1], halo_recv.at[1], s - 1),
    ]
    to_right = [
        remote(k_hbm.at[0, tail_rows], kx.at[pl.ds(0, BLOCK)], halo_send.at[2], halo_recv.at[2], s + 1),
        remote(v_hbm.at[0, tail_rows], vx.at[pl.ds(0, BLOCK)], halo_send.at[3], halo_recv.at[3], s + 1),
    ]
    for copy in ring_copies:
        copy.start()

    @pl.when(zl == 1)
    def _():
        signal(chain_up, s + 8, g)

    @pl.when(zl == 2)
    def _():
        signal(chain_down, s - 8, g)

    @pl.when(late)
    def _():
        for i in range(4):
            h = lax.rem(y + i, 4)
            for other in range(4):
                remote(
                    s1.at[h, 0], kv_all.at[z, my_rows, :], direct_send, kv_recv.at[z],
                    column(other) + h,
                ).start()
        for other in range(4):
            signal(late_in, column(other) + y, g)

    def pool_pair(level, scale):
        pool = pooler(level)
        return dot(pool, own_k[...]) * scale, dot(pool, own_v[...]) * scale

    kp, vp = pool_pair(3, 0.5**1.5)
    kv3_s[0], kv3_s[1] = kp.astype(BF16), vp.astype(BF16)
    kp, vp = pool_pair(2, 0.5)
    kv2_s[0], kv2_s[1] = kp.astype(BF16), vp.astype(BF16)

    slot3 = pl.ds(pl.multiple_of(lax.rem(y, 2) * 64, 64), 64)
    pair3 = ring + (1 - lax.div(y, 2)) * 2
    l3_copies = [
        remote(kv3_s, kv3_r.at[:, slot3, :], l3_send.at[j], l3_recv.at[lax.rem(y, 2)], pair3 + j)
        for j in range(2)
    ]
    l2_copy = remote(kv2_s, kv2_r, l2_send, l2_recv, s + 1 - 2 * lax.rem(y, 2))
    for copy in [*l3_copies, l2_copy]:
        copy.start()

    zeros = jnp.zeros((BLOCK, FEATURES), BF16)

    @pl.when(s == 0)
    def _():
        kx[0:BLOCK] = zeros
        vx[0:BLOCK] = zeros

    @pl.when(s == last)
    def _():
        kx[BLOCK + ROWS :] = zeros
        vx[BLOCK + ROWS :] = zeros

    lane_half = iota((1, 128), 1) < HD
    halves = [jnp.where(lane_half, 1.0, 0.0), jnp.where(lane_half, 0.0, 1.0)]

    def masked_queries(dst, field, count):
        for p in range(2):
            part = field[:, p * 128 : p * 128 + 128]
            for odd in range(2):
                dst[p, odd * count : (odd + 1) * count, :] = (part * halves[odd]).astype(BF16)

    for b in range(4):
        masked_queries(qn.at[b], q_s[b * BLOCK : (b + 1) * BLOCK, :].astype(F32), BLOCK)

    ones16 = jnp.ones((16, BLOCK), BF16)

    def turn(dst, block, column):
        turned = block.T
        for h in range(HEADS_HERE):
            dst[h, 0:HD, column : column + BLOCK] = turned[h * HD : (h + 1) * HD, :]
            dst[h, HD:SLAB, column : column + BLOCK] = ones16

    for b in range(1, 5):
        turn(vtn, vx[b * BLOCK : (b + 1) * BLOCK, :], b * BLOCK)

    def attend(keys, queries, values, count, exact, biases=None):
        scores = [dot_nt(key, queries) for key in keys]
        if biases:
            scores = [a if bias is None else a + bias for a, bias in zip(scores, biases)]
        top = jnp.max(scores[0], axis=0, keepdims=True)
        for part in scores[1:]:
            top = jnp.maximum(top, jnp.max(part, axis=0, keepdims=True))
        top = top * SCALE
        high = below = None
        if not exact:
            high, below = split_top(top)
            top = high + below
        weights = [jnp.exp2(part * SCALE - top).astype(BF16) for part in scores]
        weights = weights[0] if len(weights) == 1 else jnp.concatenate(weights, axis=0)
        results = [
            dot(values[odd], weights[:, odd * count : (odd + 1) * count]) for odd in range(2)
        ]
        return top, high, below, results

    def near_block(b):
        for p in range(2):
            lanes = slice(p * 128, p * 128 + 128)
            keys = [kx[(b + i) * BLOCK : (b + i + 1) * BLOCK, lanes] for i in range(3)]
            values = [vtn[2 * p + odd, :, b * BLOCK : (b + 3) * BLOCK] for odd in range(2)]
            biases = [None, None, None]
            if b == 0:
                biases[0] = jnp.where(s == 0, MASKED, 0.0)
            if b == 3:
                biases[2] = jnp.where(s == last, MASKED, 0.0)
            top, _, _, results = attend(keys, qn[b, p], values, BLOCK, True, biases)
            columns = slice(b * BLOCK, (b + 1) * BLOCK)
            for odd in range(2):
                h = 2 * p + odd
                near[h, :, columns] = results[odd]
                near_top[h : h + 1, columns] = top[:, odd * BLOCK : (odd + 1) * BLOCK]

    def small_rows(count, high, below, total):
        row = iota((16, count), 0)
        total_high = rounded(total)
        rows = jnp.where(row == 2, total_high, total - total_high)
        rows = jnp.where(row == 1, below, rows)
        return jnp.where(row == 0, high, rows)

    def sibling(dst, keys, queries, values, count, column):
        for p in range(2):
            lanes = slice(p * 128, p * 128 + 128)
            _, high, below, results = attend(
                [keys[:, lanes]], queries[p], [values(2 * p), values(2 * p + 1)], count, False
            )
            for odd in range(2):
                h = 2 * p + odd
                own = slice(odd * count, (odd + 1) * count)
                columns = slice(column, column + count)
                dst[h * SLAB : h * SLAB + HD, columns] = results[odd][0:HD].astype(BF16)
                dst[h * SLAB + HD : (h + 1) * SLAB, columns] = small_rows(
                    count, high[:, own], below[:, own], results[odd][HD : HD + 1]
                ).astype(BF16)

    calm = (z < 3) | (z > 3)

    @pl.when((s > 0) & (calm | (y > 0)))
    def _():
        for copy in to_left:
            copy.start()

    @pl.when((s < last) & (calm | (y < 3)))
    def _():
        for copy in to_right:
            copy.start()

    near_block(1)
    near_block(2)
    pooled_q = dot(pooler(1), q_s[...]) * 0.5**0.5
    for b in range(2):
        masked_queries(q1m.at[b], pooled_q[b * BLOCK : (b + 1) * BLOCK, :], BLOCK)
    masked_queries(q2m, dot(pooler(2), q_s[...]) * 0.5, BLOCK)
    masked_queries(q3m, dot(pooler(3), q_s[...]) * 0.5**1.5, 64)
    kp, vp = pool_pair(1, 0.5**0.5)
    k1[...] = kp.astype(BF16)
    v1[...] = vp.astype(BF16)
    for b in range(2):
        turn(vt1, v1[b * BLOCK : (b + 1) * BLOCK, :], b * BLOCK)
    for b in range(2):
        other = 1 - b
        sibling(
            x1, k1[other * BLOCK : (other + 1) * BLOCK, :], q1m.at[b],
            lambda h, other=other: vt1[h, :, other * BLOCK : (other + 1) * BLOCK], BLOCK, b * BLOCK,
        )
    e1[...] = selector(256, ROWS, 1)
    e2[...] = selector(128, ROWS, 2)
    e3[...] = selector(64, ROWS, 3)

    @pl.when(zl <= 1)
    def _():
        pl.semaphore_wait(chain_down, 1)

    @pl.when(zl >= 2)
    def _():
        pl.semaphore_wait(chain_up, 1)

    @pl.when(zl == 1)
    def _():
        signal(chain_down, s - 8, g)

    @pl.when(zl == 2)
    def _():
        signal(chain_up, s + 8, g)

    far_q = remote(r1.at[1], q_far, q_send, q_recv, mirror + y)
    for copy in ring_copies:
        copy.wait_recv()
    far_q.start()

    def forward(f):
        return remote(
            r1.at[0], kv_all.at[z], kv_send.at[f - 1], kv_recv.at[z], column(flipped(f)) + y
        )

    for f in (3, 2, 1):
        forward(f).start()

    @pl.when(ring_start & (z == 3))
    def _():
        for copy in to_left:
            copy.start()

    @pl.when(ring_end & (z == 3))
    def _():
        for copy in to_right:
            copy.start()

    @pl.when(early)
    def _():
        pl.semaphore_wait(late_in, 4)
        for f in range(4, 8):
            forward(f).start()

    l2_copy.wait_recv()
    for j in range(2):
        remote(kv3_s, kv3_r.at[:, pl.ds(j * 64, 64), :], l3_send.at[j], l3_recv.at[j], pair3 + j).wait_recv()
    turn(vt2, kv2_r[1], 0)
    sibling(x2, kv2_r[0], q2m, lambda h: vt2[h], BLOCK, 0)

    turn(vt3, kv3_r[1], 0)
    sibling(x3, kv3_r[0], q3m, lambda h: vt3[h], 64, 0)
    def a2a(block, owner):
        return [
            remote(att_s.at[block], att_r.at[owner], a2a_send.at[block], a2a_recv.at[owner], s, block),
            remote(om_s.at[block], om_r.at[owner], om_send.at[block], om_recv.at[owner], s, block),
        ]

    def combine(blocks):
        for block in blocks:
            columns = slice(block * BLOCK, (block + 1) * BLOCK)
            wide = [
                dot(field[...], select[:, columns])
                for field, select in ((x1, e1), (x2, e2), (x3, e3))
            ]
            mixes, logs = [], []
            for h in range(HEADS_HERE):
                terms = [part[h * SLAB : (h + 1) * SLAB] for part in wide]
                tops = [t[HD : HD + 1] + t[HD + 1 : HD + 2] for t in terms]
                sums = [t[HD + 2 : HD + 3] + t[HD + 3 : HD + 4] for t in terms]
                near_here = near[h, :, columns]
                tops.append(near_top[h : h + 1, columns])
                sums.append(near_here[HD : HD + 1])
                terms.append(near_here)
                top = tops[0]
                for other in tops[1:]:
                    top = jnp.maximum(top, other)
                total = jnp.zeros((1, BLOCK), F32)
                factors = [jnp.exp2(t - top) for t in tops]
                for factor, part in zip(factors, sums):
                    total = total + factor * part
                inverse = 1.0 / total
                mixed = jnp.zeros((HD, BLOCK), F32)
                for factor, part in zip(factors, terms):
                    mixed = mixed + part[0:HD] * (factor * inverse)
                mixes.append(mixed)
                logs.append(top + jnp.log2(total))
            mixed = jnp.concatenate(mixes, axis=0).astype(BF16).T
            row = iota((8, BLOCK), 0)
            rows = jnp.zeros((8, BLOCK), F32)
            for h in range(HEADS_HERE):
                rows = jnp.where(row == h, logs[h], rows)
            att_s[block] = mixed
            om_s[block] = rows
        for block in blocks:

            @pl.when(g == block)
            def _(block=block):
                att_r[g] = att_s[block]
                om_r[g] = om_s[block]

            @pl.when(g != block)
            def _(block=block):
                for copy in a2a(block, g):
                    copy.start()

    combine((1, 2))

    def rest():
        @pl.when(s > 0)
        def _():
            for copy in to_right:
                copy.wait_recv()

        @pl.when(s < last)
        def _():
            for copy in to_left:
                copy.wait_recv()

        turn(vtn, vx[0:BLOCK, :], 0)
        near_block(0)

        turn(vtn, vx[BLOCK + ROWS :, :], BLOCK + ROWS)
        near_block(3)
        combine((0, 3))

    @pl.when(z < 2)
    def _():
        rest()

    far_q.wait_recv()
    def arrive(f):
        other = flipped(f)
        remote(
            kv_all.at[other], kv_all.at[other], kv_send.at[f - 1], kv_recv.at[other], column(other) + y
        ).wait_recv()

    for f in (1, 2, 5, 6, 7):
        arrive(f)
    queries = jnp.concatenate([r1[1], q_far[...]], axis=0)
    ones64 = jnp.ones((HD, 128), BF16)
    top = acc = None
    for f in (0, 1, 2, 7, 6, 5, 3, 4):
        if f == 3:
            for late_block in (3, 4,):
                arrive(late_block)
        block = kv_all[flipped(f)] if f else r1[0]
        scores = dot_nt(block, queries)
        turned = jnp.concatenate([ones64, block.T[HD:]], axis=0)
        here = jnp.max(scores, axis=0, keepdims=True) * SCALE
        high = here if f == 0 else jnp.maximum(top, here)
        weights = jnp.exp2(scores * SCALE - high)
        if f == 0:
            weights = jnp.concatenate([weights[:, 0:128], weights[:, 128:256] * 2.0], axis=1)
        part = dot(turned, weights.astype(BF16))
        acc = part if f == 0 else acc * jnp.exp2(top - high) + part
        top = high
    sums = acc[0:HD]
    logs = top + jnp.log2(sums)
    means = acc[HD:] / sums
    odd_head = lax.rem(y, 2) == 1
    result = jnp.concatenate(
        [jnp.where(odd_head, logs, means), jnp.where(odd_head, means, logs)], axis=0
    )
    ret_s[...] = result.T
    head_here = g * 4 + y

    def give(slot, row, seq, head):
        remote(
            ret_s.at[pl.ds(pl.multiple_of(row, 8), 8), :], top_r.at[slot, head_here],
            ret_send.at[slot], ret_recv.at[slot], seq, head,
        ).start()

    for j in range(4):
        for t in range(4):
            give(1, 128 + j * 32 + t * 8, mirror + j, t)
    for dy in range(4):
        for dg in range(4):
            if dy or dg:
                there, t = lax.rem(y + dy, 4), lax.rem(g + dg, 4)
                give(0, there * 32 + t * 8, ring + there, t)
    top_r[0, head_here] = ret_s[pl.ds(pl.multiple_of(y * 32 + g * 8, 8), 8), :]

    @pl.when(z >= 2)
    def _():
        rest()

    for d in range(1, 4):
        for copy in a2a(0, lax.rem(g + d, 4)):
            copy.wait_recv()
    logs = om_r[...].reshape(32, BLOCK)
    high = rounded(logs)
    middle = rounded(logs - high)
    lowest = rounded(logs - high - middle)
    logs = jnp.concatenate([high, middle, lowest, jnp.zeros((32, BLOCK), F32)], axis=0)
    k, c = iota((128, 1024), 0), iota((128, 1024), 1)
    hit = ((k & 31) == ((c >> 8) * 8 + ((c >> 6) & 3))) & (k < 96)
    spread = jnp.where(hit, 1.0, 0.0).astype(BF16)
    om_x[...] = dot(logs.T.astype(BF16), spread)
    loads[3].wait()

    def arrived(slot, heads):
        remote(
            top_r.at[slot, pl.ds(0, heads)], top_r.at[slot, pl.ds(0, heads)],
            ret_send.at[slot], ret_recv.at[slot], mirror + y,
        ).wait_recv()

    arrived(0, 15)
    arrived(1, 16)
    low8 = iota((8, 128), 1) < HD
    for p in range(8):
        means, logs = [], []
        for slot in range(2):
            even, odd = top_r[slot, 2 * p], top_r[slot, 2 * p + 1]
            means.append(jnp.where(low8, even, odd))
            logs.append(pltpu.roll(jnp.where(low8, odd, even), HD, 1))
        top = jnp.maximum(logs[0], logs[1])
        factors = [jnp.exp2(t - top) for t in logs]
        total = factors[0] + factors[1]
        mean = (means[0] * factors[0] + means[1] * factors[1]) / total
        log = top + jnp.log2(total)
        lanes = slice(p * 128, p * 128 + 128)
        here = slice(p % 2 * 128, p % 2 * 128 + 128)
        for q in range(8):
            rows = slice(q * 16, q * 16 + 16)
            other = att_r[p // 2, rows, here].astype(F32)
            share = 1.0 / (1.0 + jnp.exp2(om_x[rows, lanes] - log[q : q + 1]))
            att_f[rows, lanes] = (other + (mean[q : q + 1] - other) * share).astype(BF16)
    o_ref[0] = dot(att_f[...], w_s[...]).astype(BF16)

    for copy in [*ring_copies, *l3_copies, l2_copy, far_q]:
        copy.wait_send()
    for block in range(4):

        @pl.when(g != block)
        def _(block=block):
            for copy in a2a(block, g):
                copy.wait_send()

    for f in range(1, 4):
        forward(f).wait_send()

    @pl.when(early)
    def _():
        for f in range(4, 8):
            forward(f).wait_send()

    @pl.when(late)
    def _():
        remote(kv_all.at[0:4], kv_all.at[0:4], direct_send, kv_recv.at[z], mirror + y).wait_send()

    for slot, rows in ((0, 120), (1, 128)):
        remote(
            ret_s.at[pl.ds(0, rows)], ret_s.at[pl.ds(0, rows)],
            ret_send.at[slot], ret_recv.at[slot], mirror + y,
        ).wait_send()

    @pl.when(s > 0)
    def _():
        for copy in to_left:
            copy.wait_send()

    @pl.when(s < last)
    def _():
        for copy in to_right:
            copy.wait_send()


def per_device(queries, key_vectors, value_vectors, out_weight):
    def buf(*shape, dtype=BF16):
        return pltpu.VMEM(shape, dtype)

    dma = pltpu.SemaphoreType.DMA
    regular = pltpu.SemaphoreType.REGULAR
    scratch = [
        buf(ROWS, 256), buf(768, 256), buf(768, 256), buf(1024, 1024),
        buf(4, 2, 256, 128), buf(2, 2, 256, 128), buf(2, 256, 128), buf(2, 128, 128),
        buf(256, 256), buf(256, 256), buf(2, 128, 256), buf(2, 128, 256), buf(2, 64, 256), buf(2, 128, 256),
        buf(4, SLAB, 768), buf(4, SLAB, 256), buf(4, SLAB, 128), buf(4, SLAB, 128),
        buf(4, 2, 32, 128), buf(2, 128, 128), buf(8, 128, 128), buf(128, 128),
        buf(256, 128, dtype=F32), buf(2, 16, 8, 128, dtype=F32),
        buf(4 * SLAB, 256), buf(4 * SLAB, 128), buf(4 * SLAB, 64),
        buf(256, ROWS), buf(128, ROWS), buf(64, ROWS),
        buf(4, SLAB, ROWS, dtype=F32), buf(8, ROWS, dtype=F32), buf(4, 128, 256), buf(4, 128, 256),
        buf(4, 8, 128, dtype=F32), buf(4, 8, 128, dtype=F32), buf(128, 1024, dtype=F32), buf(128, 1024),
        dma((4,)), dma((4,)), dma((4,)), dma((3,)), dma((3,)), dma, dma, dma((2,)), dma((2,)),
        dma((7,)), dma, dma((8,)), dma, dma, dma((2,)), dma((2,)), dma((4,)), dma((4,)), dma((4,)), dma((4,)),
        regular, regular, regular,
    ]
    return pl.pallas_call(
        kernel,
        out_shape=pltpu.VMEM((1, BLOCK, 1024), BF16),
        in_specs=[pl.BlockSpec(memory_space=pl.ANY)] * 4,
        out_specs=pl.BlockSpec(memory_space=pltpu.VMEM),
        scratch_shapes=scratch,
        compiler_params=pltpu.CompilerParams(
            collective_id=0, has_side_effects=True, vmem_limit_bytes=58 * 2**20
        ),
    )(queries, key_vectors, value_vectors, out_weight)


def solution(mesh):
    return jax.shard_map(
        per_device,
        mesh=mesh,
        in_specs=(P(None, "seq", "head"), P(None, "seq", "head"), P(None, "seq", "head"), P()),
        out_specs=P(None, ("seq", "head"), None),
        check_vma=False,
    )
```

```python
import math

import jax
import jax.numpy as jnp
from jax import lax
from jax.experimental import pallas as pl
from jax.experimental.pallas import tpu as pltpu
from jax.sharding import PartitionSpec as P

HD = 64
BLOCK = 128
HEADS_HERE = 4
ROWS = 512
FEATURES = HEADS_HERE * HD
SLAB = HD + 16
SCALE = HD**-0.5 * math.log2(math.e)
MASKED = -1e30
BF16, F32 = jnp.bfloat16, jnp.float32
MESH = pl.DeviceIdType.MESH


def iota(shape, axis):
    return lax.broadcasted_iota(jnp.int32, shape, axis)


def dot(a, b):
    return jnp.dot(a, b, preferred_element_type=F32)


def dot_nt(a, b):
    return lax.dot_general(a, b, (((1,), (1,)), ((), ())), preferred_element_type=F32)


def rounded(value):
    return value.astype(BF16).astype(F32)


def split_top(top):
    high = rounded(top)
    return high, rounded(top - high)


def selector(rows, columns, shift, offset=0):
    hit = iota((rows, columns), 0) == offset + (iota((rows, columns), 1) >> shift)
    return jnp.where(hit, 1.0, 0.0).astype(BF16)


def pooler(level):
    rows = ROWS >> level
    hit = iota((rows, ROWS), 0) == (iota((rows, ROWS), 1) >> level)
    return jnp.where(hit, 1.0, 0.0).astype(BF16)


def kernel(
    q_hbm, k_hbm, v_hbm, w_hbm, o_ref,
    q_s, kx, vx, w_s,
    qn, q1m, q2m, q3m,
    k1, v1, kv2_s, kv2_r, kv3_s, kv3_r,
    vtn, vt1, vt2, vt3,
    s1, r1, kv_all, q_far, ret_s, top_r,
    x1, x2, x3, e1, e2, e3,
    near, near_top, att_s, att_r, om_s, om_r, om_x, att_f,
    in_sem, halo_send, halo_recv, s1_send, s1_recv, l2_send, l2_recv, l3_send, l3_recv,
    kv_send, direct_send, kv_recv, q_send, q_recv, ret_send, ret_recv, a2a_send, a2a_recv, om_send, om_recv,
    chain_up, chain_down, late_in,
):
    s, g = lax.axis_index("seq"), lax.axis_index("head")
    last = lax.axis_size("seq") - 1
    z, x, y = lax.div(s, 8), lax.rem(lax.div(s, 4), 2), lax.rem(s, 4)
    ring = s - y
    zl = lax.rem(z, 4)
    bits = [lax.rem(z, 2), lax.rem(lax.div(z, 2), 2), lax.div(z, 4)]
    mirror = z * 8 + (1 - x) * 4
    early, late = z < 4, z >= 4

    def flipped(f):
        low, middle, high = [1 - bit if f >> i & 1 else bit for i, bit in enumerate(bits)]
        return high * 4 + middle * 2 + low

    def column(other):
        return other * 8 + x * 4

    loads = [
        pltpu.make_async_copy(k_hbm.at[0], kx.at[pl.ds(BLOCK, ROWS)], in_sem.at[0]),
        pltpu.make_async_copy(v_hbm.at[0], vx.at[pl.ds(BLOCK, ROWS)], in_sem.at[1]),
        pltpu.make_async_copy(q_hbm.at[0], q_s, in_sem.at[2]),
        pltpu.make_async_copy(w_hbm, w_s, in_sem.at[3]),
    ]
    barrier = pltpu.get_barrier_semaphore()

    def signal(semaphore, seq, head):
        pl.semaphore_signal(semaphore, inc=1, device_id=(seq, head), device_id_type=MESH)

    ring_start, ring_end = (y == 0) & (s > 0), (y == 3) & (s < last)

    @pl.when(early)
    def _():
        for other in (7, 6, 5, 4):
            for j in range(4):
                signal(barrier, column(other) + j, g)

    @pl.when(ring_start)
    def _():
        signal(barrier, s - 1, g)

    @pl.when(ring_end)
    def _():
        signal(barrier, s + 1, g)

    for d in range(1, 4):
        signal(barrier, ring + lax.rem(y + d, 4), g)
        signal(barrier, s, lax.rem(g + d, 4))
    signal(barrier, mirror + y, g)

    @pl.when(zl < 3)
    def _():
        signal(barrier, s + 8, g)

    @pl.when(zl > 0)
    def _():
        signal(barrier, s - 8, g)

    for load in loads:
        load.start()

    low32 = iota((32, 128), 1) < HD

    pool4 = pooler(4)
    own_k, own_v = kx.at[pl.ds(BLOCK, ROWS)], vx.at[pl.ds(BLOCK, ROWS)]
    loads[0].wait()
    k4 = rounded(dot(pool4, own_k[...]) * 0.25)
    loads[1].wait()
    v4 = rounded(dot(pool4, own_v[...]) * 0.25)
    loads[2].wait()
    q4 = rounded(dot(pool4, q_s[...]) * 0.25)
    for h in range(HEADS_HERE):
        pair = slice(h // 2 * 128, h // 2 * 128 + 128)
        kp, vp, qp = k4[:, pair], v4[:, pair], q4[:, pair]
        if h % 2 == 0:
            packed = jnp.where(low32, kp, pltpu.roll(vp, HD, 1))
        else:
            packed = jnp.where(low32, pltpu.roll(kp, HD, 1), vp)
            qp = pltpu.roll(qp, HD, 1)
        s1[h, 0] = packed.astype(BF16)
        s1[h, 1] = jnp.where(low32, qp, 0.0).astype(BF16)
    my_rows = pl.ds(pl.multiple_of(y * 32, 32), 32)
    r1[:, my_rows, :] = s1[y]

    pl.semaphore_wait(
        barrier,
        7
        + jnp.where(late, 16, 0)
        + jnp.where(zl > 0, 1, 0)
        + jnp.where(zl < 3, 1, 0)
        + jnp.where(ring_start, 1, 0)
        + jnp.where(ring_end, 1, 0),
    )

    def remote(src, dst, send, recv, seq, head=None):
        return pltpu.make_async_remote_copy(
            src_ref=src, dst_ref=dst, send_sem=send, recv_sem=recv,
            device_id=(seq, g if head is None else head), device_id_type=MESH,
        )

    ring_copies = [
        remote(
            s1.at[lax.rem(y + d, 4)], r1.at[:, my_rows, :],
            s1_send.at[d - 1], s1_recv.at[d - 1], ring + lax.rem(y + d, 4),
        )
        for d in range(1, 4)
    ]
    head_rows, tail_rows = pl.ds(0, BLOCK), pl.ds(ROWS - BLOCK, BLOCK)
    to_left = [
        remote(k_hbm.at[0, head_rows], kx.at[pl.ds(BLOCK + ROWS, BLOCK)], halo_send.at[0], halo_recv.at[0], s - 1),
        remote(v_hbm.at[0, head_rows], vx.at[pl.ds(BLOCK + ROWS, BLOCK)], halo_send.at[1], halo_recv.at[1], s - 1),
    ]
    to_right = [
        remote(k_hbm.at[0, tail_rows], kx.at[pl.ds(0, BLOCK)], halo_send.at[2], halo_recv.at[2], s + 1),
        remote(v_hbm.at[0, tail_rows], vx.at[pl.ds(0, BLOCK)], halo_send.at[3], halo_recv.at[3], s + 1),
    ]
    for copy in ring_copies:
        copy.start()

    @pl.when(zl == 1)
    def _():
        signal(chain_up, s + 8, g)

    @pl.when(zl == 2)
    def _():
        signal(chain_down, s - 8, g)

    @pl.when(late)
    def _():
        for i in range(4):
            h = lax.rem(y + i, 4)
            for other in range(4):
                remote(
                    s1.at[h, 0], kv_all.at[z, my_rows, :], direct_send, kv_recv.at[z],
                    column(other) + h,
                ).start()
        for other in range(4):
            signal(late_in, column(other) + y, g)

    def pool_pair(level, scale):
        pool = pooler(level)
        return dot(pool, own_k[...]) * scale, dot(pool, own_v[...]) * scale

    kp, vp = pool_pair(3, 0.5**1.5)
    kv3_s[0], kv3_s[1] = kp.astype(BF16), vp.astype(BF16)
    kp, vp = pool_pair(2, 0.5)
    kv2_s[0], kv2_s[1] = kp.astype(BF16), vp.astype(BF16)

    slot3 = pl.ds(pl.multiple_of(lax.rem(y, 2) * 64, 64), 64)
    pair3 = ring + (1 - lax.div(y, 2)) * 2
    l3_copies = [
        remote(kv3_s, kv3_r.at[:, slot3, :], l3_send.at[j], l3_recv.at[lax.rem(y, 2)], pair3 + j)
        for j in range(2)
    ]
    l2_copy = remote(kv2_s, kv2_r, l2_send, l2_recv, s + 1 - 2 * lax.rem(y, 2))
    for copy in [*l3_copies, l2_copy]:
        copy.start()

    zeros = jnp.zeros((BLOCK, FEATURES), BF16)

    @pl.when(s == 0)
    def _():
        kx[0:BLOCK] = zeros
        vx[0:BLOCK] = zeros

    @pl.when(s == last)
    def _():
        kx[BLOCK + ROWS :] = zeros
        vx[BLOCK + ROWS :] = zeros

    lane_half = iota((1, 128), 1) < HD
    halves = [jnp.where(lane_half, 1.0, 0.0), jnp.where(lane_half, 0.0, 1.0)]

    def masked_queries(dst, field, count):
        for p in range(2):
            part = field[:, p * 128 : p * 128 + 128]
            for odd in range(2):
                dst[p, odd * count : (odd + 1) * count, :] = (part * halves[odd]).astype(BF16)

    for b in range(4):
        masked_queries(qn.at[b], q_s[b * BLOCK : (b + 1) * BLOCK, :].astype(F32), BLOCK)

    ones16 = jnp.ones((16, BLOCK), BF16)

    def turn(dst, block, column):
        turned = block.T
        for h in range(HEADS_HERE):
            dst[h, 0:HD, column : column + BLOCK] = turned[h * HD : (h + 1) * HD, :]
            dst[h, HD:SLAB, column : column + BLOCK] = ones16

    for b in range(1, 5):
        turn(vtn, vx[b * BLOCK : (b + 1) * BLOCK, :], b * BLOCK)

    def attend(keys, queries, values, count, exact, biases=None):
        scores = [dot_nt(key, queries) for key in keys]
        if biases:
            scores = [a if bias is None else a + bias for a, bias in zip(scores, biases)]
        top = jnp.max(scores[0], axis=0, keepdims=True)
        for part in scores[1:]:
            top = jnp.maximum(top, jnp.max(part, axis=0, keepdims=True))
        top = top * SCALE
        high = below = None
        if not exact:
            high, below = split_top(top)
            top = high + below
        weights = [jnp.exp2(part * SCALE - top).astype(BF16) for part in scores]
        weights = weights[0] if len(weights) == 1 else jnp.concatenate(weights, axis=0)
        results = [
            dot(values[odd], weights[:, odd * count : (odd + 1) * count]) for odd in range(2)
        ]
        return top, high, below, results

    def near_block(b):
        for p in range(2):
            lanes = slice(p * 128, p * 128 + 128)
            keys = [kx[(b + i) * BLOCK : (b + i + 1) * BLOCK, lanes] for i in range(3)]
            values = [vtn[2 * p + odd, :, b * BLOCK : (b + 3) * BLOCK] for odd in range(2)]
            biases = [None, None, None]
            if b == 0:
                biases[0] = jnp.where(s == 0, MASKED, 0.0)
            if b == 3:
                biases[2] = jnp.where(s == last, MASKED, 0.0)
            top, _, _, results = attend(keys, qn[b, p], values, BLOCK, True, biases)
            columns = slice(b * BLOCK, (b + 1) * BLOCK)
            for odd in range(2):
                h = 2 * p + odd
                near[h, :, columns] = results[odd]
                near_top[h : h + 1, columns] = top[:, odd * BLOCK : (odd + 1) * BLOCK]

    def small_rows(count, high, below, total):
        row = iota((16, count), 0)
        total_high = rounded(total)
        rows = jnp.where(row == 2, total_high, total - total_high)
        rows = jnp.where(row == 1, below, rows)
        return jnp.where(row == 0, high, rows)

    def sibling(dst, keys, queries, values, count, column):
        for p in range(2):
            lanes = slice(p * 128, p * 128 + 128)
            _, high, below, results = attend(
                [keys[:, lanes]], queries[p], [values(2 * p), values(2 * p + 1)], count, False
            )
            for odd in range(2):
                h = 2 * p + odd
                own = slice(odd * count, (odd + 1) * count)
                columns = slice(column, column + count)
                dst[h * SLAB : h * SLAB + HD, columns] = results[odd][0:HD].astype(BF16)
                dst[h * SLAB + HD : (h + 1) * SLAB, columns] = small_rows(
                    count, high[:, own], below[:, own], results[odd][HD : HD + 1]
                ).astype(BF16)

    calm = (z < 3) | (z > 3)

    @pl.when((s > 0) & (calm | (y > 0)))
    def _():
        for copy in to_left:
            copy.start()

    @pl.when((s < last) & (calm | (y < 3)))
    def _():
        for copy in to_right:
            copy.start()

    near_block(1)
    near_block(2)
    pooled_q = dot(pooler(1), q_s[...]) * 0.5**0.5
    for b in range(2):
        masked_queries(q1m.at[b], pooled_q[b * BLOCK : (b + 1) * BLOCK, :], BLOCK)
    masked_queries(q2m, dot(pooler(2), q_s[...]) * 0.5, BLOCK)
    masked_queries(q3m, dot(pooler(3), q_s[...]) * 0.5**1.5, 64)
    kp, vp = pool_pair(1, 0.5**0.5)
    k1[...] = kp.astype(BF16)
    v1[...] = vp.astype(BF16)
    for b in range(2):
        turn(vt1, v1[b * BLOCK : (b + 1) * BLOCK, :], b * BLOCK)
    for b in range(2):
        other = 1 - b
        sibling(
            x1, k1[other * BLOCK : (other + 1) * BLOCK, :], q1m.at[b],
            lambda h, other=other: vt1[h, :, other * BLOCK : (other + 1) * BLOCK], BLOCK, b * BLOCK,
        )
    e1[...] = selector(256, ROWS, 1)
    e2[...] = selector(128, ROWS, 2)
    e3[...] = selector(64, ROWS, 3)

    @pl.when(zl <= 1)
    def _():
        pl.semaphore_wait(chain_down, 1)

    @pl.when(zl >= 2)
    def _():
        pl.semaphore_wait(chain_up, 1)

    @pl.when(zl == 1)
    def _():
        signal(chain_down, s - 8, g)

    @pl.when(zl == 2)
    def _():
        signal(chain_up, s + 8, g)

    far_q = remote(r1.at[1], q_far, q_send, q_recv, mirror + y)
    for copy in ring_copies:
        copy.wait_recv()
    far_q.start()

    def forward(f):
        return remote(
            r1.at[0], kv_all.at[z], kv_send.at[f - 1], kv_recv.at[z], column(flipped(f)) + y
        )

    for f in (3, 2, 1):
        forward(f).start()

    @pl.when(ring_start & (z == 3))
    def _():
        for copy in to_left:
            copy.start()

    @pl.when(ring_end & (z == 3))
    def _():
        for copy in to_right:
            copy.start()

    @pl.when(early)
    def _():
        pl.semaphore_wait(late_in, 4)
        for f in range(4, 8):
            forward(f).start()

    l2_copy.wait_recv()
    for j in range(2):
        remote(kv3_s, kv3_r.at[:, pl.ds(j * 64, 64), :], l3_send.at[j], l3_recv.at[j], pair3 + j).wait_recv()
    turn(vt2, kv2_r[1], 0)
    sibling(x2, kv2_r[0], q2m, lambda h: vt2[h], BLOCK, 0)

    turn(vt3, kv3_r[1], 0)
    sibling(x3, kv3_r[0], q3m, lambda h: vt3[h], 64, 0)
    def a2a(block, owner):
        return [
            remote(att_s.at[block], att_r.at[owner], a2a_send.at[block], a2a_recv.at[owner], s, block),
            remote(om_s.at[block], om_r.at[owner], om_send.at[block], om_recv.at[owner], s, block),
        ]

    def combine(blocks):
        for block in blocks:
            columns = slice(block * BLOCK, (block + 1) * BLOCK)
            wide = [
                dot(field[...], select[:, columns])
                for field, select in ((x1, e1), (x2, e2), (x3, e3))
            ]
            mixes, logs = [], []
            for h in range(HEADS_HERE):
                terms = [part[h * SLAB : (h + 1) * SLAB] for part in wide]
                tops = [t[HD : HD + 1] + t[HD + 1 : HD + 2] for t in terms]
                sums = [t[HD + 2 : HD + 3] + t[HD + 3 : HD + 4] for t in terms]
                near_here = near[h, :, columns]
                tops.append(near_top[h : h + 1, columns])
                sums.append(near_here[HD : HD + 1])
                terms.append(near_here)
                top = tops[0]
                for other in tops[1:]:
                    top = jnp.maximum(top, other)
                total = jnp.zeros((1, BLOCK), F32)
                factors = [jnp.exp2(t - top) for t in tops]
                for factor, part in zip(factors, sums):
                    total = total + factor * part
                inverse = 1.0 / total
                mixed = jnp.zeros((HD, BLOCK), F32)
                for factor, part in zip(factors, terms):
                    mixed = mixed + part[0:HD] * (factor * inverse)
                mixes.append(mixed)
                logs.append(top + jnp.log2(total))
            mixed = jnp.concatenate(mixes, axis=0).astype(BF16).T
            row = iota((8, BLOCK), 0)
            rows = jnp.zeros((8, BLOCK), F32)
            for h in range(HEADS_HERE):
                rows = jnp.where(row == h, logs[h], rows)
            att_s[block] = mixed
            om_s[block] = rows
        for block in blocks:

            @pl.when(g == block)
            def _(block=block):
                att_r[g] = att_s[block]
                om_r[g] = om_s[block]

            @pl.when(g != block)
            def _(block=block):
                for copy in a2a(block, g):
                    copy.start()

    combine((1, 2))

    def rest():
        @pl.when(s > 0)
        def _():
            for copy in to_right:
                copy.wait_recv()

        @pl.when(s < last)
        def _():
            for copy in to_left:
                copy.wait_recv()

        turn(vtn, vx[0:BLOCK, :], 0)
        near_block(0)

        turn(vtn, vx[BLOCK + ROWS :, :], BLOCK + ROWS)
        near_block(3)
        combine((0, 3))

    @pl.when(z < 2)
    def _():
        rest()

    far_q.wait_recv()
    def arrive(f):
        other = flipped(f)
        remote(
            kv_all.at[other], kv_all.at[other], kv_send.at[f - 1], kv_recv.at[other], column(other) + y
        ).wait_recv()

    for f in (1, 2, 5, 6, 7):
        arrive(f)
    queries = jnp.concatenate([r1[1], q_far[...]], axis=0)
    ones64 = jnp.ones((HD, 128), BF16)
    top = acc = None
    for f in (0, 1, 2, 7, 6, 5, 3, 4):
        if f == 3:
            for late_block in (3, 4,):
                arrive(late_block)
        block = kv_all[flipped(f)] if f else r1[0]
        scores = dot_nt(block, queries)
        turned = jnp.concatenate([ones64, block.T[HD:]], axis=0)
        here = jnp.max(scores, axis=0, keepdims=True) * SCALE
        high = here if f == 0 else jnp.maximum(top, here)
        weights = jnp.exp2(scores * SCALE - high)
        if f == 0:
            weights = jnp.concatenate([weights[:, 0:128], weights[:, 128:256] * 2.0], axis=1)
        part = dot(turned, weights.astype(BF16))
        acc = part if f == 0 else acc * jnp.exp2(top - high) + part
        top = high
    sums = acc[0:HD]
    logs = top + jnp.log2(sums)
    means = acc[HD:] / sums
    odd_head = lax.rem(y, 2) == 1
    result = jnp.concatenate(
        [jnp.where(odd_head, logs, means), jnp.where(odd_head, means, logs)], axis=0
    )
    ret_s[...] = result.T
    head_here = g * 4 + y

    def give(slot, row, seq, head):
        remote(
            ret_s.at[pl.ds(pl.multiple_of(row, 8), 8), :], top_r.at[slot, head_here],
            ret_send.at[slot], ret_recv.at[slot], seq, head,
        ).start()

    for j in range(4):
        for t in range(4):
            give(1, 128 + j * 32 + t * 8, mirror + j, t)
    for dy in range(4):
        for dg in range(4):
            if dy or dg:
                there, t = lax.rem(y + dy, 4), lax.rem(g + dg, 4)
                give(0, there * 32 + t * 8, ring + there, t)
    top_r[0, head_here] = ret_s[pl.ds(pl.multiple_of(y * 32 + g * 8, 8), 8), :]

    @pl.when(z >= 2)
    def _():
        rest()

    for d in range(1, 4):
        for copy in a2a(0, lax.rem(g + d, 4)):
            copy.wait_recv()
    logs = om_r[...].reshape(32, BLOCK)
    high = rounded(logs)
    middle = rounded(logs - high)
    lowest = rounded(logs - high - middle)
    logs = jnp.concatenate([high, middle, lowest, jnp.zeros((32, BLOCK), F32)], axis=0)
    k, c = iota((128, 1024), 0), iota((128, 1024), 1)
    hit = ((k & 31) == ((c >> 8) * 8 + ((c >> 6) & 3))) & (k < 96)
    spread = jnp.where(hit, 1.0, 0.0).astype(BF16)
    om_x[...] = dot(logs.T.astype(BF16), spread)
    loads[3].wait()

    def arrived(slot, heads):
        remote(
            top_r.at[slot, pl.ds(0, heads)], top_r.at[slot, pl.ds(0, heads)],
            ret_send.at[slot], ret_recv.at[slot], mirror + y,
        ).wait_recv()

    arrived(0, 15)
    arrived(1, 16)
    low8 = iota((8, 128), 1) < HD
    for p in range(8):
        means, logs = [], []
        for slot in range(2):
            even, odd = top_r[slot, 2 * p], top_r[slot, 2 * p + 1]
            means.append(jnp.where(low8, even, odd))
            logs.append(pltpu.roll(jnp.where(low8, odd, even), HD, 1))
        top = jnp.maximum(logs[0], logs[1])
        factors = [jnp.exp2(t - top) for t in logs]
        total = factors[0] + factors[1]
        mean = (means[0] * factors[0] + means[1] * factors[1]) / total
        log = top + jnp.log2(total)
        lanes = slice(p * 128, p * 128 + 128)
        here = slice(p % 2 * 128, p % 2 * 128 + 128)
        for q in range(8):
            rows = slice(q * 16, q * 16 + 16)
            other = att_r[p // 2, rows, here].astype(F32)
            share = 1.0 / (1.0 + jnp.exp2(om_x[rows, lanes] - log[q : q + 1]))
            att_f[rows, lanes] = (other + (mean[q : q + 1] - other) * share).astype(BF16)
    o_ref[0] = dot(att_f[...], w_s[...]).astype(BF16)

    for copy in [*ring_copies, *l3_copies, l2_copy, far_q]:
        copy.wait_send()
    for block in range(4):

        @pl.when(g != block)
        def _(block=block):
            for copy in a2a(block, g):
                copy.wait_send()

    for f in range(1, 4):
        forward(f).wait_send()

    @pl.when(early)
    def _():
        for f in range(4, 8):
            forward(f).wait_send()

    @pl.when(late)
    def _():
        remote(kv_all.at[0:4], kv_all.at[0:4], direct_send, kv_recv.at[z], mirror + y).wait_send()

    for slot, rows in ((0, 120), (1, 128)):
        remote(
            ret_s.at[pl.ds(0, rows)], ret_s.at[pl.ds(0, rows)],
            ret_send.at[slot], ret_recv.at[slot], mirror + y,
        ).wait_send()

    @pl.when(s > 0)
    def _():
        for copy in to_left:
            copy.wait_send()

    @pl.when(s < last)
    def _():
        for copy in to_right:
            copy.wait_send()


def per_device(queries, key_vectors, value_vectors, out_weight):
    def buf(*shape, dtype=BF16):
        return pltpu.VMEM(shape, dtype)

    dma = pltpu.SemaphoreType.DMA
    regular = pltpu.SemaphoreType.REGULAR
    scratch = [
        buf(ROWS, 256), buf(768, 256), buf(768, 256), buf(1024, 1024),
        buf(4, 2, 256, 128), buf(2, 2, 256, 128), buf(2, 256, 128), buf(2, 128, 128),
        buf(256, 256), buf(256, 256), buf(2, 128, 256), buf(2, 128, 256), buf(2, 64, 256), buf(2, 128, 256),
        buf(4, SLAB, 768), buf(4, SLAB, 256), buf(4, SLAB, 128), buf(4, SLAB, 128),
        buf(4, 2, 32, 128), buf(2, 128, 128), buf(8, 128, 128), buf(128, 128),
        buf(256, 128, dtype=F32), buf(2, 16, 8, 128, dtype=F32),
        buf(4 * SLAB, 256), buf(4 * SLAB, 128), buf(4 * SLAB, 64),
        buf(256, ROWS), buf(128, ROWS), buf(64, ROWS),
        buf(4, SLAB, ROWS, dtype=F32), buf(8, ROWS, dtype=F32), buf(4, 128, 256), buf(4, 128, 256),
        buf(4, 8, 128, dtype=F32), buf(4, 8, 128, dtype=F32), buf(128, 1024, dtype=F32), buf(128, 1024),
        dma((4,)), dma((4,)), dma((4,)), dma((3,)), dma((3,)), dma, dma, dma((2,)), dma((2,)),
        dma((7,)), dma, dma((8,)), dma, dma, dma((2,)), dma((2,)), dma((4,)), dma((4,)), dma((4,)), dma((4,)),
        regular, regular, regular,
    ]
    return pl.pallas_call(
        kernel,
        out_shape=pltpu.VMEM((1, BLOCK, 1024), BF16),
        in_specs=[pl.BlockSpec(memory_space=pl.ANY)] * 4,
        out_specs=pl.BlockSpec(memory_space=pltpu.VMEM),
        scratch_shapes=scratch,
        compiler_params=pltpu.CompilerParams(
            collective_id=0, has_side_effects=True, vmem_limit_bytes=58 * 2**20
        ),
    )(queries, key_vectors, value_vectors, out_weight)


def solution(mesh):
    return jax.shard_map(
        per_device,
        mesh=mesh,
        in_specs=(P(None, "seq", "head"), P(None, "seq", "head"), P(None, "seq", "head"), P()),
        out_specs=P(None, ("seq", "head"), None),
        check_vma=False,
    )
```

```python
import math

import jax
import jax.numpy as jnp
from jax import lax
from jax.experimental import pallas as pl
from jax.experimental.pallas import tpu as pltpu
from jax.sharding import PartitionSpec as P

HD = 64
BLOCK = 128
HEADS_HERE = 4
ROWS = 512
FEATURES = HEADS_HERE * HD
SLAB = HD + 16
SCALE = HD**-0.5 * math.log2(math.e)
MASKED = -1e30
BF16, F32 = jnp.bfloat16, jnp.float32
MESH = pl.DeviceIdType.MESH


def iota(shape, axis):
    return lax.broadcasted_iota(jnp.int32, shape, axis)


def dot(a, b):
    return jnp.dot(a, b, preferred_element_type=F32)


def dot_nt(a, b):
    return lax.dot_general(a, b, (((1,), (1,)), ((), ())), preferred_element_type=F32)


def rounded(value):
    return value.astype(BF16).astype(F32)


def split_top(top):
    high = rounded(top)
    return high, rounded(top - high)


def selector(rows, columns, shift, offset=0):
    hit = iota((rows, columns), 0) == offset + (iota((rows, columns), 1) >> shift)
    return jnp.where(hit, 1.0, 0.0).astype(BF16)


def pooler(level):
    rows = ROWS >> level
    hit = iota((rows, ROWS), 0) == (iota((rows, ROWS), 1) >> level)
    return jnp.where(hit, 1.0, 0.0).astype(BF16)


def kernel(
    q_hbm, k_hbm, v_hbm, w_hbm, o_ref,
    q_s, kx, vx, w_s,
    qn, q1m, q2m, q3m,
    k1, v1, kv2_s, kv2_r, kv3_s, kv3_r,
    vtn, vt1, vt2, vt3,
    s1, r1, kv_all, q_far, ret_s, top_r,
    x1, x2, x3, e1, e2, e3,
    near, near_top, att_s, att_r, om_s, om_r, om_x, att_f,
    in_sem, halo_send, halo_recv, s1_send, s1_recv, l2_send, l2_recv, l3_send, l3_recv,
    kv_send, direct_send, kv_recv, q_send, q_recv, ret_send, ret_recv, a2a_send, a2a_recv, om_send, om_recv,
    chain_up, chain_down, late_in,
):
    s, g = lax.axis_index("seq"), lax.axis_index("head")
    last = lax.axis_size("seq") - 1
    z, x, y = lax.div(s, 8), lax.rem(lax.div(s, 4), 2), lax.rem(s, 4)
    ring = s - y
    zl = lax.rem(z, 4)
    bits = [lax.rem(z, 2), lax.rem(lax.div(z, 2), 2), lax.div(z, 4)]
    mirror = z * 8 + (1 - x) * 4
    early, late = z < 4, z >= 4

    def flipped(f):
        low, middle, high = [1 - bit if f >> i & 1 else bit for i, bit in enumerate(bits)]
        return high * 4 + middle * 2 + low

    def column(other):
        return other * 8 + x * 4

    loads = [
        pltpu.make_async_copy(k_hbm.at[0], kx.at[pl.ds(BLOCK, ROWS)], in_sem.at[0]),
        pltpu.make_async_copy(v_hbm.at[0], vx.at[pl.ds(BLOCK, ROWS)], in_sem.at[1]),
        pltpu.make_async_copy(q_hbm.at[0], q_s, in_sem.at[2]),
        pltpu.make_async_copy(w_hbm, w_s, in_sem.at[3]),
    ]
    for load in loads[:3]:
        load.start()

    barrier = pltpu.get_barrier_semaphore()

    def signal(semaphore, seq, head):
        pl.semaphore_signal(semaphore, inc=1, device_id=(seq, head), device_id_type=MESH)

    ring_start, ring_end = (y == 0) & (s > 0), (y == 3) & (s < last)

    @pl.when(early)
    def _():
        for other in range(4, 8):
            for j in range(4):
                signal(barrier, column(other) + j, g)

    @pl.when(ring_start)
    def _():
        signal(barrier, s - 1, g)

    @pl.when(ring_end)
    def _():
        signal(barrier, s + 1, g)

    for d in range(1, 4):
        signal(barrier, ring + lax.rem(y + d, 4), g)
        signal(barrier, s, lax.rem(g + d, 4))
    signal(barrier, mirror + y, g)

    @pl.when(zl < 3)
    def _():
        signal(barrier, s + 8, g)

    @pl.when(zl > 0)
    def _():
        signal(barrier, s - 8, g)

    low32 = iota((32, 128), 1) < HD

    pool4 = pooler(4)
    own_k, own_v = kx.at[pl.ds(BLOCK, ROWS)], vx.at[pl.ds(BLOCK, ROWS)]
    loads[0].wait()
    k4 = rounded(dot(pool4, own_k[...]) * 0.25)
    loads[1].wait()
    v4 = rounded(dot(pool4, own_v[...]) * 0.25)
    loads[2].wait()
    q4 = rounded(dot(pool4, q_s[...]) * 0.25)
    for h in range(HEADS_HERE):
        pair = slice(h // 2 * 128, h // 2 * 128 + 128)
        kp, vp, qp = k4[:, pair], v4[:, pair], q4[:, pair]
        if h % 2 == 0:
            packed = jnp.where(low32, kp, pltpu.roll(vp, HD, 1))
        else:
            packed = jnp.where(low32, pltpu.roll(kp, HD, 1), vp)
            qp = pltpu.roll(qp, HD, 1)
        s1[h, 0] = packed.astype(BF16)
        s1[h, 1] = jnp.where(low32, qp, 0.0).astype(BF16)
    my_rows = pl.ds(pl.multiple_of(y * 32, 32), 32)
    r1[:, my_rows, :] = s1[y]

    pl.semaphore_wait(
        barrier,
        7
        + jnp.where(late, 16, 0)
        + jnp.where(zl > 0, 1, 0)
        + jnp.where(zl < 3, 1, 0)
        + jnp.where(ring_start, 1, 0)
        + jnp.where(ring_end, 1, 0),
    )

    def remote(src, dst, send, recv, seq, head=None):
        return pltpu.make_async_remote_copy(
            src_ref=src, dst_ref=dst, send_sem=send, recv_sem=recv,
            device_id=(seq, g if head is None else head), device_id_type=MESH,
        )

    ring_copies = [
        remote(
            s1.at[lax.rem(y + d, 4)], r1.at[:, my_rows, :],
            s1_send.at[d - 1], s1_recv.at[d - 1], ring + lax.rem(y + d, 4),
        )
        for d in range(1, 4)
    ]
    head_rows, tail_rows = pl.ds(0, BLOCK), pl.ds(ROWS - BLOCK, BLOCK)
    to_left = [
        remote(k_hbm.at[0, head_rows], kx.at[pl.ds(BLOCK + ROWS, BLOCK)], halo_send.at[0], halo_recv.at[0], s - 1),
        remote(v_hbm.at[0, head_rows], vx.at[pl.ds(BLOCK + ROWS, BLOCK)], halo_send.at[1], halo_recv.at[1], s - 1),
    ]
    to_right = [
        remote(k_hbm.at[0, tail_rows], kx.at[pl.ds(0, BLOCK)], halo_send.at[2], halo_recv.at[2], s + 1),
        remote(v_hbm.at[0, tail_rows], vx.at[pl.ds(0, BLOCK)], halo_send.at[3], halo_recv.at[3], s + 1),
    ]
    for copy in ring_copies:
        copy.start()

    @pl.when(zl == 1)
    def _():
        signal(chain_up, s + 8, g)

    @pl.when(zl == 2)
    def _():
        signal(chain_down, s - 8, g)

    @pl.when(late)
    def _():
        for i in range(4):
            h = lax.rem(y + i, 4)
            for other in range(4):
                remote(
                    s1.at[h, 0], kv_all.at[z, my_rows, :], direct_send, kv_recv.at[z],
                    column(other) + h,
                ).start()
        for other in range(4):
            signal(late_in, column(other) + y, g)

    def pool_pair(level, scale):
        pool = pooler(level)
        return dot(pool, own_k[...]) * scale, dot(pool, own_v[...]) * scale

    kp, vp = pool_pair(3, 0.5**1.5)
    kv3_s[0], kv3_s[1] = kp.astype(BF16), vp.astype(BF16)
    kp, vp = pool_pair(2, 0.5)
    kv2_s[0], kv2_s[1] = kp.astype(BF16), vp.astype(BF16)

    slot3 = pl.ds(pl.multiple_of(lax.rem(y, 2) * 64, 64), 64)
    pair3 = ring + (1 - lax.div(y, 2)) * 2
    l3_copies = [
        remote(kv3_s, kv3_r.at[:, slot3, :], l3_send.at[j], l3_recv.at[lax.rem(y, 2)], pair3 + j)
        for j in range(2)
    ]
    l2_copy = remote(kv2_s, kv2_r, l2_send, l2_recv, s + 1 - 2 * lax.rem(y, 2))
    for copy in [*l3_copies, l2_copy]:
        copy.start()

    zeros = jnp.zeros((BLOCK, FEATURES), BF16)

    @pl.when(s == 0)
    def _():
        kx[0:BLOCK] = zeros
        vx[0:BLOCK] = zeros

    @pl.when(s == last)
    def _():
        kx[BLOCK + ROWS :] = zeros
        vx[BLOCK + ROWS :] = zeros

    lane_half = iota((1, 128), 1) < HD
    halves = [jnp.where(lane_half, 1.0, 0.0), jnp.where(lane_half, 0.0, 1.0)]

    def masked_queries(dst, field, count):
        for p in range(2):
            part = field[:, p * 128 : p * 128 + 128]
            for odd in range(2):
                dst[p, odd * count : (odd + 1) * count, :] = (part * halves[odd]).astype(BF16)

    for b in range(4):
        masked_queries(qn.at[b], q_s[b * BLOCK : (b + 1) * BLOCK, :].astype(F32), BLOCK)

    ones16 = jnp.ones((16, BLOCK), BF16)

    def turn(dst, block, column):
        turned = block.T
        for h in range(HEADS_HERE):
            dst[h, 0:HD, column : column + BLOCK] = turned[h * HD : (h + 1) * HD, :]
            dst[h, HD:SLAB, column : column + BLOCK] = ones16

    for b in range(1, 5):
        turn(vtn, vx[b * BLOCK : (b + 1) * BLOCK, :], b * BLOCK)

    def attend(keys, queries, values, count, exact, biases=None):
        scores = [dot_nt(key, queries) for key in keys]
        if biases:
            scores = [a if bias is None else a + bias for a, bias in zip(scores, biases)]
        top = jnp.max(scores[0], axis=0, keepdims=True)
        for part in scores[1:]:
            top = jnp.maximum(top, jnp.max(part, axis=0, keepdims=True))
        top = top * SCALE
        high = below = None
        if not exact:
            high, below = split_top(top)
            top = high + below
        weights = [jnp.exp2(part * SCALE - top).astype(BF16) for part in scores]
        weights = weights[0] if len(weights) == 1 else jnp.concatenate(weights, axis=0)
        results = [
            dot(values[odd], weights[:, odd * count : (odd + 1) * count]) for odd in range(2)
        ]
        return top, high, below, results

    def near_block(b):
        for p in range(2):
            lanes = slice(p * 128, p * 128 + 128)
            keys = [kx[(b + i) * BLOCK : (b + i + 1) * BLOCK, lanes] for i in range(3)]
            values = [vtn[2 * p + odd, :, b * BLOCK : (b + 3) * BLOCK] for odd in range(2)]
            biases = [None, None, None]
            if b == 0:
                biases[0] = jnp.where(s == 0, MASKED, 0.0)
            if b == 3:
                biases[2] = jnp.where(s == last, MASKED, 0.0)
            top, _, _, results = attend(keys, qn[b, p], values, BLOCK, True, biases)
            columns = slice(b * BLOCK, (b + 1) * BLOCK)
            for odd in range(2):
                h = 2 * p + odd
                near[h, :, columns] = results[odd]
                near_top[h : h + 1, columns] = top[:, odd * BLOCK : (odd + 1) * BLOCK]

    def small_rows(count, high, below, total):
        row = iota((16, count), 0)
        total_high = rounded(total)
        rows = jnp.where(row == 2, total_high, total - total_high)
        rows = jnp.where(row == 1, below, rows)
        return jnp.where(row == 0, high, rows)

    def sibling(dst, keys, queries, values, count, column):
        for p in range(2):
            lanes = slice(p * 128, p * 128 + 128)
            _, high, below, results = attend(
                [keys[:, lanes]], queries[p], [values(2 * p), values(2 * p + 1)], count, False
            )
            for odd in range(2):
                h = 2 * p + odd
                own = slice(odd * count, (odd + 1) * count)
                columns = slice(column, column + count)
                dst[h * SLAB : h * SLAB + HD, columns] = results[odd][0:HD].astype(BF16)
                dst[h * SLAB + HD : (h + 1) * SLAB, columns] = small_rows(
                    count, high[:, own], below[:, own], results[odd][HD : HD + 1]
                ).astype(BF16)

    calm = (z < 3) | (z > 3)

    @pl.when((s > 0) & (calm | (y > 0)))
    def _():
        for copy in to_left:
            copy.start()

    @pl.when((s < last) & (calm | (y < 3)))
    def _():
        for copy in to_right:
            copy.start()

    loads[3].start()
    near_block(1)
    near_block(2)
    pooled_q = dot(pooler(1), q_s[...]) * 0.5**0.5
    for b in range(2):
        masked_queries(q1m.at[b], pooled_q[b * BLOCK : (b + 1) * BLOCK, :], BLOCK)
    masked_queries(q2m, dot(pooler(2), q_s[...]) * 0.5, BLOCK)
    masked_queries(q3m, dot(pooler(3), q_s[...]) * 0.5**1.5, 64)
    kp, vp = pool_pair(1, 0.5**0.5)
    k1[...] = kp.astype(BF16)
    v1[...] = vp.astype(BF16)
    for b in range(2):
        turn(vt1, v1[b * BLOCK : (b + 1) * BLOCK, :], b * BLOCK)
    for b in range(2):
        other = 1 - b
        sibling(
            x1, k1[other * BLOCK : (other + 1) * BLOCK, :], q1m.at[b],
            lambda h, other=other: vt1[h, :, other * BLOCK : (other + 1) * BLOCK], BLOCK, b * BLOCK,
        )
    e1[...] = selector(256, ROWS, 1)
    e2[...] = selector(128, ROWS, 2)
    e3[...] = selector(64, ROWS, 3)

    @pl.when(zl <= 1)
    def _():
        pl.semaphore_wait(chain_down, 1)

    @pl.when(zl >= 2)
    def _():
        pl.semaphore_wait(chain_up, 1)

    @pl.when(zl == 1)
    def _():
        signal(chain_down, s - 8, g)

    @pl.when(zl == 2)
    def _():
        signal(chain_up, s + 8, g)

    far_q = remote(r1.at[1], q_far, q_send, q_recv, mirror + y)
    for copy in ring_copies:
        copy.wait_recv()
    far_q.start()

    def forward(f):
        return remote(
            r1.at[0], kv_all.at[z], kv_send.at[f - 1], kv_recv.at[z], column(flipped(f)) + y
        )

    for f in (3, 2, 1):
        forward(f).start()

    @pl.when(ring_start & (z == 3))
    def _():
        for copy in to_left:
            copy.start()

    @pl.when(ring_end & (z == 3))
    def _():
        for copy in to_right:
            copy.start()

    @pl.when(early)
    def _():
        pl.semaphore_wait(late_in, 4)
        for f in range(4, 8):
            forward(f).start()

    l2_copy.wait_recv()
    for j in range(2):
        remote(kv3_s, kv3_r.at[:, pl.ds(j * 64, 64), :], l3_send.at[j], l3_recv.at[j], pair3 + j).wait_recv()
    turn(vt2, kv2_r[1], 0)
    sibling(x2, kv2_r[0], q2m, lambda h: vt2[h], BLOCK, 0)

    turn(vt3, kv3_r[1], 0)
    sibling(x3, kv3_r[0], q3m, lambda h: vt3[h], 64, 0)
    def a2a(block, owner):
        return [
            remote(att_s.at[block], att_r.at[owner], a2a_send.at[block], a2a_recv.at[owner], s, block),
            remote(om_s.at[block], om_r.at[owner], om_send.at[block], om_recv.at[owner], s, block),
        ]

    def combine(blocks):
        for block in blocks:
            columns = slice(block * BLOCK, (block + 1) * BLOCK)
            wide = [
                dot(field[...], select[:, columns])
                for field, select in ((x1, e1), (x2, e2), (x3, e3))
            ]
            mixes, logs = [], []
            for h in range(HEADS_HERE):
                terms = [part[h * SLAB : (h + 1) * SLAB] for part in wide]
                tops = [t[HD : HD + 1] + t[HD + 1 : HD + 2] for t in terms]
                sums = [t[HD + 2 : HD + 3] + t[HD + 3 : HD + 4] for t in terms]
                near_here = near[h, :, columns]
                tops.append(near_top[h : h + 1, columns])
                sums.append(near_here[HD : HD + 1])
                terms.append(near_here)
                top = tops[0]
                for other in tops[1:]:
                    top = jnp.maximum(top, other)
                total = jnp.zeros((1, BLOCK), F32)
                factors = [jnp.exp2(t - top) for t in tops]
                for factor, part in zip(factors, sums):
                    total = total + factor * part
                inverse = 1.0 / total
                mixed = jnp.zeros((HD, BLOCK), F32)
                for factor, part in zip(factors, terms):
                    mixed = mixed + part[0:HD] * (factor * inverse)
                mixes.append(mixed)
                logs.append(top + jnp.log2(total))
            mixed = jnp.concatenate(mixes, axis=0).astype(BF16).T
            row = iota((8, BLOCK), 0)
            rows = jnp.zeros((8, BLOCK), F32)
            for h in range(HEADS_HERE):
                rows = jnp.where(row == h, logs[h], rows)
            att_s[block] = mixed
            om_s[block] = rows
        for block in blocks:

            @pl.when(g == block)
            def _(block=block):
                att_r[g] = att_s[block]
                om_r[g] = om_s[block]

            @pl.when(g != block)
            def _(block=block):
                for copy in a2a(block, g):
                    copy.start()

    combine((1, 2))

    def rest():
        @pl.when(s > 0)
        def _():
            for copy in to_right:
                copy.wait_recv()

        @pl.when(s < last)
        def _():
            for copy in to_left:
                copy.wait_recv()

        turn(vtn, vx[0:BLOCK, :], 0)
        near_block(0)

        turn(vtn, vx[BLOCK + ROWS :, :], BLOCK + ROWS)
        near_block(3)
        combine((0, 3))

    @pl.when(z < 2)
    def _():
        rest()

    far_q.wait_recv()
    def arrive(f):
        other = flipped(f)
        remote(
            kv_all.at[other], kv_all.at[other], kv_send.at[f - 1], kv_recv.at[other], column(other) + y
        ).wait_recv()

    for f in (1, 2, 5, 6, 7):
        arrive(f)
    queries = jnp.concatenate([r1[1], q_far[...]], axis=0)
    ones64 = jnp.ones((HD, 128), BF16)
    top = acc = None
    for f in (0, 1, 2, 7, 6, 5, 3, 4):
        if f == 3:
            for late_block in (3, 4,):
                arrive(late_block)
        block = kv_all[flipped(f)] if f else r1[0]
        scores = dot_nt(block, queries)
        turned = jnp.concatenate([ones64, block.T[HD:]], axis=0)
        here = jnp.max(scores, axis=0, keepdims=True) * SCALE
        high = here if f == 0 else jnp.maximum(top, here)
        weights = jnp.exp2(scores * SCALE - high)
        if f == 0:
            weights = jnp.concatenate([weights[:, 0:128], weights[:, 128:256] * 2.0], axis=1)
        part = dot(turned, weights.astype(BF16))
        acc = part if f == 0 else acc * jnp.exp2(top - high) + part
        top = high
    sums = acc[0:HD]
    logs = top + jnp.log2(sums)
    means = acc[HD:] / sums
    odd_head = lax.rem(y, 2) == 1
    result = jnp.concatenate(
        [jnp.where(odd_head, logs, means), jnp.where(odd_head, means, logs)], axis=0
    )
    ret_s[...] = result.T
    head_here = g * 4 + y

    def give(slot, row, seq, head):
        remote(
            ret_s.at[pl.ds(pl.multiple_of(row, 8), 8), :], top_r.at[slot, head_here],
            ret_send.at[slot], ret_recv.at[slot], seq, head,
        ).start()

    for j in range(4):
        for t in range(4):
            give(1, 128 + j * 32 + t * 8, mirror + j, t)
    for dy in range(4):
        for dg in range(4):
            if dy or dg:
                there, t = lax.rem(y + dy, 4), lax.rem(g + dg, 4)
                give(0, there * 32 + t * 8, ring + there, t)
    top_r[0, head_here] = ret_s[pl.ds(pl.multiple_of(y * 32 + g * 8, 8), 8), :]

    @pl.when(z >= 2)
    def _():
        rest()

    for d in range(1, 4):
        for copy in a2a(0, lax.rem(g + d, 4)):
            copy.wait_recv()
    logs = om_r[...].reshape(32, BLOCK)
    high = rounded(logs)
    middle = rounded(logs - high)
    lowest = rounded(logs - high - middle)
    logs = jnp.concatenate([high, middle, lowest, jnp.zeros((32, BLOCK), F32)], axis=0)
    k, c = iota((128, 1024), 0), iota((128, 1024), 1)
    hit = ((k & 31) == ((c >> 8) * 8 + ((c >> 6) & 3))) & (k < 96)
    spread = jnp.where(hit, 1.0, 0.0).astype(BF16)
    om_x[...] = dot(logs.T.astype(BF16), spread)
    loads[3].wait()

    def arrived(slot, heads):
        remote(
            top_r.at[slot, pl.ds(0, heads)], top_r.at[slot, pl.ds(0, heads)],
            ret_send.at[slot], ret_recv.at[slot], mirror + y,
        ).wait_recv()

    arrived(0, 15)
    arrived(1, 16)
    low8 = iota((8, 128), 1) < HD
    for p in range(8):
        means, logs = [], []
        for slot in range(2):
            even, odd = top_r[slot, 2 * p], top_r[slot, 2 * p + 1]
            means.append(jnp.where(low8, even, odd))
            logs.append(pltpu.roll(jnp.where(low8, odd, even), HD, 1))
        top = jnp.maximum(logs[0], logs[1])
        factors = [jnp.exp2(t - top) for t in logs]
        total = factors[0] + factors[1]
        mean = (means[0] * factors[0] + means[1] * factors[1]) / total
        log = top + jnp.log2(total)
        lanes = slice(p * 128, p * 128 + 128)
        here = slice(p % 2 * 128, p % 2 * 128 + 128)
        for q in range(8):
            rows = slice(q * 16, q * 16 + 16)
            other = att_r[p // 2, rows, here].astype(F32)
            share = 1.0 / (1.0 + jnp.exp2(om_x[rows, lanes] - log[q : q + 1]))
            att_f[rows, lanes] = (other + (mean[q : q + 1] - other) * share).astype(BF16)
    o_ref[0] = dot(att_f[...], w_s[...]).astype(BF16)

    for copy in [*ring_copies, *l3_copies, l2_copy, far_q]:
        copy.wait_send()
    for block in range(4):

        @pl.when(g != block)
        def _(block=block):
            for copy in a2a(block, g):
                copy.wait_send()

    for f in range(1, 4):
        forward(f).wait_send()

    @pl.when(early)
    def _():
        for f in range(4, 8):
            forward(f).wait_send()

    @pl.when(late)
    def _():
        remote(kv_all.at[0:4], kv_all.at[0:4], direct_send, kv_recv.at[z], mirror + y).wait_send()

    for slot, rows in ((0, 120), (1, 128)):
        remote(
            ret_s.at[pl.ds(0, rows)], ret_s.at[pl.ds(0, rows)],
            ret_send.at[slot], ret_recv.at[slot], mirror + y,
        ).wait_send()

    @pl.when(s > 0)
    def _():
        for copy in to_left:
            copy.wait_send()

    @pl.when(s < last)
    def _():
        for copy in to_right:
            copy.wait_send()


def per_device(queries, key_vectors, value_vectors, out_weight):
    def buf(*shape, dtype=BF16):
        return pltpu.VMEM(shape, dtype)

    dma = pltpu.SemaphoreType.DMA
    regular = pltpu.SemaphoreType.REGULAR
    scratch = [
        buf(ROWS, 256), buf(768, 256), buf(768, 256), buf(1024, 1024),
        buf(4, 2, 256, 128), buf(2, 2, 256, 128), buf(2, 256, 128), buf(2, 128, 128),
        buf(256, 256), buf(256, 256), buf(2, 128, 256), buf(2, 128, 256), buf(2, 64, 256), buf(2, 128, 256),
        buf(4, SLAB, 768), buf(4, SLAB, 256), buf(4, SLAB, 128), buf(4, SLAB, 128),
        buf(4, 2, 32, 128), buf(2, 128, 128), buf(8, 128, 128), buf(128, 128),
        buf(256, 128, dtype=F32), buf(2, 16, 8, 128, dtype=F32),
        buf(4 * SLAB, 256), buf(4 * SLAB, 128), buf(4 * SLAB, 64),
        buf(256, ROWS), buf(128, ROWS), buf(64, ROWS),
        buf(4, SLAB, ROWS, dtype=F32), buf(8, ROWS, dtype=F32), buf(4, 128, 256), buf(4, 128, 256),
        buf(4, 8, 128, dtype=F32), buf(4, 8, 128, dtype=F32), buf(128, 1024, dtype=F32), buf(128, 1024),
        dma((4,)), dma((4,)), dma((4,)), dma((3,)), dma((3,)), dma, dma, dma((2,)), dma((2,)),
        dma((7,)), dma, dma((8,)), dma, dma, dma((2,)), dma((2,)), dma((4,)), dma((4,)), dma((4,)), dma((4,)),
        regular, regular, regular,
    ]
    return pl.pallas_call(
        kernel,
        out_shape=pltpu.VMEM((1, BLOCK, 1024), BF16),
        in_specs=[pl.BlockSpec(memory_space=pl.ANY)] * 4,
        out_specs=pl.BlockSpec(memory_space=pltpu.VMEM),
        scratch_shapes=scratch,
        compiler_params=pltpu.CompilerParams(
            collective_id=0, has_side_effects=True, vmem_limit_bytes=58 * 2**20
        ),
    )(queries, key_vectors, value_vectors, out_weight)


def solution(mesh):
    return jax.shard_map(
        per_device,
        mesh=mesh,
        in_specs=(P(None, "seq", "head"), P(None, "seq", "head"), P(None, "seq", "head"), P()),
        out_specs=P(None, ("seq", "head"), None),
        check_vma=False,
    )
```
